32 devices in a mesh: seq: 4 (over x, core), batch: 8 (over z, y).
Axes of the slice: x: 2, y: 2, z: 4, core: 2. Of those that a mesh axis runs over, the one named last changes fastest.
Arguments:
- stream_in: float32 [8, 512, 512], P('batch', 'seq'), may hold values from -6 to 6
- cotangent: float32 [8, 512, 512], P('batch', 'seq'), may hold values from -6 to 6
- lengths: int32 [8], P('batch'), may hold values from 200 to 512, as said below
- norm_gain: float32 [2, 512], replicated, may hold values from 0.5 to 1.5
- decay_rate: float32 [2, 64, 512], replicated, may hold values from 0.0002 to 0.1
- in_map: float32 [2, 64, 512], replicated, may hold values from -0.6 to 0.6
- out_map: float32 [2, 64, 512], replicated, may hold values from -0.75 to 0.75
- skip_gain: float32 [2, 512], replicated, may hold values from -4 to 4
- order_two: float32 [2, 512], replicated, may hold values from -2.5 to 2.5
- step_gain: float32 [2, 512], replicated, may hold values from -4 to 4
- glu_weight: bfloat16 [2, 512, 1024], replicated, may hold values from -0.25 to 0.25
- glu_bias: float32 [2, 1024], replicated, may hold values from -1.8 to 1.8
Outputs:
- outputs: float32 [8, 512, 512], P('batch', 'seq')
- grad_input: float32 [8, 512, 512], P('batch', 'seq')
- grad_norm_gain: float32 [2, 512], replicated
- grad_decay_rate: float32 [2, 64, 512], replicated
- grad_in_map: float32 [2, 64, 512], replicated
- grad_out_map: float32 [2, 64, 512], replicated
- grad_skip_gain: float32 [2, 512], replicated
- grad_order_two: float32 [2, 512], replicated
- grad_step_gain: float32 [2, 512], replicated
- grad_glu_weight: float32 [2, 512, 1024], replicated
- grad_glu_bias: float32 [2, 1024], replicated
- stats: float32 [2, 3], replicated
The draws below stay inside these ranges and needn't reach their ends.
Inputs may be any that keep to these rules, and one draw needn't show every extreme that they name: `lengths`: review 0 has the full length 512 and review 1 the shortest, 200.
All inputs are finite; a program needn't handle non-finite values.
Results may differ from the reference program's by a relative error of at most 0.0073.
Values sent between devices are 32-bit elements; how exact they have to be, the bound alone decides.
A program may use at most 256 MiB of HBM per device.

```python
import math
import jax
import jax.numpy as jnp
from jax import lax

D = 512
NS = 64
LAYERS = 2
MIN_LEN = 200
SEQ_LEN = 512
BATCH = 8


def draw_lengths(key, part):
    length_draw = jax.random.randint(key, (BATCH,), MIN_LEN, SEQ_LEN + 1, dtype=jnp.int32)
    places = jnp.arange(BATCH, dtype=jnp.int32)
    length_draw = jnp.where(places == 0, SEQ_LEN, length_draw)
    length_draw = jnp.where(places == 1, MIN_LEN, length_draw)
    return length_draw.astype(jnp.int32)


def levels(key, shape, pieces, low, top_value):
    level = 1.0
    for axis_at, blocks in pieces:
        draws = jax.random.uniform(jax.random.fold_in(jax.random.fold_in(key, 6), axis_at), (blocks,), jnp.float32, low / len(pieces), top_value / len(pieces))
        level = level * jnp.repeat(jnp.exp(draws), shape[axis_at] // blocks).reshape((-1,) + (1,) * (len(shape) - 1 - axis_at))
    return level


def gaussian(rng, shape, scale, most, split=(), kind=jnp.bfloat16):
    gain = levels(rng, shape, split, -0.22, 0.18) if split else 1.0
    drawn = jax.random.normal(rng, shape, jnp.float32) * scale * gain
    return jnp.minimum(jnp.maximum(drawn, -most), most).astype(kind)


def setup_inputs(seed: int = 0) -> dict:
    key_list = jax.random.split(jax.random.key(seed), 13)
    stream_in = gaussian(key_list[0], (BATCH, SEQ_LEN, D), 1.0, 6.0, ((0, 8), (1, 4)), jnp.float32)
    cotangent = gaussian(key_list[1], (BATCH, SEQ_LEN, D), 1.0, 6.0, ((0, 8), (1, 4)), jnp.float32)
    lengths = draw_lengths(jax.random.fold_in(key_list[12], 71), 0)
    norm_gain = jnp.clip(1.0 + 0.1 * jax.random.normal(key_list[3], (LAYERS, D), jnp.float32), 0.5, 1.5)
    decay_rate = jnp.clip(jnp.exp(jax.random.uniform(key_list[4], (LAYERS, NS, D), jnp.float32, math.log(0.0002), math.log(0.1))), 0.0002, 0.1)
    in_map = gaussian(key_list[5], (LAYERS, NS, D), 0.1, 0.6, (), jnp.float32)
    out_map = gaussian(key_list[6], (LAYERS, NS, D), NS ** -0.5, 0.75, (), jnp.float32)
    skip_gain = gaussian(key_list[7], (LAYERS, D), 1.0, 4.0, (), jnp.float32)
    order_two = gaussian(key_list[8], (LAYERS, D), 0.5, 2.5, (), jnp.float32)
    step_gain = gaussian(key_list[9], (LAYERS, D), 1.0, 4.0, (), jnp.float32)
    glu_weight = gaussian(key_list[10], (LAYERS, D, 2 * D), D ** -0.5, 0.25)
    glu_bias = gaussian(key_list[11], (LAYERS, 2 * D), 0.3, 1.8, (), jnp.float32)
    return {"stream_in": stream_in, "cotangent": cotangent, "lengths": lengths, "norm_gain": norm_gain, "decay_rate": decay_rate, "in_map": in_map, "out_map": out_map, "skip_gain": skip_gain, "order_two": order_two, "step_gain": step_gain, "glu_weight": glu_weight, "glu_bias": glu_bias}


epsilon = 1e-05
highest = lax.Precision.HIGHEST

@jax.custom_vjp
def low(v):
    return lax.optimization_barrier(v.astype(jnp.bfloat16)).astype(jnp.float32)

@jax.custom_vjp
def low_back(v):
    return v

def low_keep(v):
    return (low(v), None)

def low_pass(kept, grad):
    return (grad,)

def back_keep(v):
    return (v, None)

def back_low(kept, grad):
    return (low(grad),)
low.defvjp(low_keep, low_pass)
low_back.defvjp(back_keep, back_low)

def layer_norm(stream, gain_row):
    center = stream - lax.optimization_barrier(jnp.mean(stream, axis=-1, keepdims=True))
    spread = lax.optimization_barrier(jnp.mean(center * center, axis=-1, keepdims=True))
    return center * lax.rsqrt(spread + epsilon) * gain_row

def recurrence(rates_in, driven, decay_rate, in_map, out_map):
    length_all = rates_in.shape[0]
    block_len = math.gcd(length_all, 64)
    count_blocks = length_all // block_len

    def one_step(state_now, inputs):
        rate_now, drive_now = inputs
        state_now = jnp.exp(-decay_rate * rate_now[None, :]) * state_now + in_map * drive_now[None, :]
        return (state_now, lax.optimization_barrier(jnp.sum(out_map * state_now, axis=0)))

    @jax.checkpoint
    def one_block(state_now, inputs):
        return lax.scan(one_step, state_now, inputs)
    start_state = jnp.zeros(decay_rate.shape, jnp.float32)
    unused, outputs = lax.scan(one_block, start_state, (rates_in.reshape(count_blocks, block_len, -1), driven.reshape(count_blocks, block_len, -1)))
    return outputs.reshape(length_all, -1)

def one_layer(stream, valid_mask, gain_row, decay_rate, in_map, out_map, skip_gain, order_two, step_gain, weight, glu_bias):
    normed = layer_norm(stream, gain_row)
    previous = jnp.concatenate([jnp.zeros((1, D), jnp.float32), normed[:-1]], axis=0)
    driven = normed + order_two * normed * previous
    rates_in = jax.nn.softplus(step_gain * normed)
    mixed_out = recurrence(rates_in, driven, decay_rate, in_map, out_map) + skip_gain * driven
    activated = jax.nn.gelu(mixed_out)
    projected = low_back(jnp.dot(low(activated), weight, precision=highest, preferred_element_type=jnp.float32)) + glu_bias
    branch = projected[:, :D] * jax.nn.sigmoid(projected[:, D:]) * valid_mask
    return (stream + branch, activated, branch)

def run_layers(stream, param_tuple, valid_mask):
    norm_gain, decay_rate, in_map, out_map, skip_gain, order_two, step_gain, glu_weight, glu_bias = param_tuple
    squares_all = []
    for layer_index in range(LAYERS):
        stream, activated, branch = one_layer(stream, valid_mask, norm_gain[layer_index], decay_rate[layer_index], in_map[layer_index], out_map[layer_index], skip_gain[layer_index], order_two[layer_index], step_gain[layer_index], glu_weight[layer_index], glu_bias[layer_index])
        squares_all.append(jnp.stack([jnp.sum(valid_mask * activated * activated), jnp.sum(branch * branch), jnp.sum(valid_mask * stream * stream)]))
    return (stream, jnp.stack(squares_all))

def reference(stream_in, cotangent, lengths, norm_gain, decay_rate, in_map, out_map, skip_gain, order_two, step_gain, glu_weight, glu_bias):
    params = (norm_gain, decay_rate, in_map, out_map, skip_gain, order_two, step_gain, glu_weight.astype(jnp.float32), glu_bias)
    positions = jnp.arange(SEQ_LEN, dtype=jnp.int32)

    def per_review(totals, inputs):
        review_in, review_grad, review_len = inputs
        valid_mask = (positions < review_len).astype(jnp.float32)[:, None]

        def forward(review_stream, param_tuple):
            return run_layers(review_stream, param_tuple, valid_mask)
        result, pullback, squares = jax.vjp(forward, review_in, params, has_aux=True)
        grad_in, grad_params = pullback(review_grad)
        summed = jax.tree.map(jnp.add, totals[0], grad_params)
        return ((summed, totals[1] + squares, totals[2] + jnp.sum(valid_mask)), (result, grad_in))
    start = (jax.tree.map(jnp.zeros_like, params), jnp.zeros((LAYERS, 3), jnp.float32), jnp.zeros((), jnp.float32))
    finals, stacked = lax.scan(per_review, start, (stream_in, cotangent, lengths))
    grad_params, squares, valid_count = finals
    outputs, grad_input = stacked
    stats = jnp.sqrt(squares / (valid_count * D))
    return (outputs, grad_input, grad_params[0], grad_params[1], grad_params[2], grad_params[3], grad_params[4], grad_params[5], grad_params[6], grad_params[7], grad_params[8], stats)
```

```python
import functools
import math

import jax
import jax.numpy as jnp
from jax import lax
from jax.experimental import pallas as pl
from jax.experimental.pallas import tpu as pltpu
from jax.sharding import PartitionSpec as P

MESH = pl.DeviceIdType.MESH
EPSILON = 1e-05
LOG2E = 1.4426950408889634
LN2 = 0.6931471805599453
GELU_K = math.sqrt(2.0 / math.pi)
F32 = jnp.float32
BF16 = jnp.bfloat16
LANES = 128
CHUNK = 32
EXTRA = 16


def rows8(v):
    return v.reshape(v.shape[0] // 8, 8, v.shape[1]).sum(0)


def sigmoid(v):
    return 1.0 / (1.0 + jnp.exp(-v))


def gelu_parts(m):
    th = jnp.tanh(GELU_K * (m + 0.044715 * m * m * m))
    return th


def bits_of(n):
    return [i for i in range(n.bit_length() - 1)]


def orders(seq, batch):
    s = [("seq", b) for b in bits_of(seq)]
    b = [("batch", b) for b in bits_of(batch)]
    first = s[:1]
    s, b = s[1:], b
    one, two = [], []
    for i in range(max(len(s), len(b))):
        one += s[i : i + 1] + b[i : i + 1]
        two += b[i : i + 1] + s[i : i + 1]
    return [first + one, first + two]


def kernel(cfg, *refs):
    S, B, TL, D, NS, L, UN = cfg
    CG = D // LANES
    NSP = S // CG
    NL = NS // NSP
    E2 = 2 * D
    CB = E2 // LANES
    GROWS = D * CB
    SB_ROWS = 2 * NL + 24
    plans = orders(S, B)
    HALF = GROWS // 2
    (
        x_ref, ct_ref, len_ref, gain_ref, dec_hbm, in_hbm, out_hbm, skip_ref, o2_ref, step_ref, w_hbm, bias_ref,
        y_out, gx_out, ggain_out, gdec_out, gin_out, gout_out, gskip_out, go2_out, gstep_out, gw_hbm, gbias_out, stats_out,
        W, DEC, INM, OUTM, NA, WT,
        XS, XR, RSTD, R, Y, YR, GS, GMR, GXR,
        SIG, P1, P2, LA, PJ, LG, GA, STR, GRD, ST,
        FB, RB, FG, SBW, SBR, SBG, VEC,
        load_sem, send_sem, recv_sem, ar_ssem, ar_rsem, sb_ssem, sb_rsem, sg_ssem, sg_rsem, out_sem,
    ) = refs
    U, GX = P2, Y
    me = lax.axis_index("seq")
    bi = lax.axis_index("batch")
    cg = me // NSP
    nh = lax.rem(me, NSP)
    n0 = nh * NL
    first_part = (nh == 0).astype(F32)
    clane = pl.ds(pl.multiple_of(cg * LANES, LANES), LANES)

    loads = [
        pltpu.make_async_copy(w_hbm, W, load_sem.at[0]),
        pltpu.make_async_copy(dec_hbm, DEC, load_sem.at[1]),
        pltpu.make_async_copy(in_hbm, INM, load_sem.at[2]),
        pltpu.make_async_copy(out_hbm, OUTM, load_sem.at[3]),
    ]
    for c in loads:
        c.start()

    barrier = pltpu.get_barrier_semaphore()
    partners = [(me ^ d, bi) for d in range(1, S)] + [(me, bi ^ (1 << b)) for b in bits_of(B)]
    for p in partners:
        pl.semaphore_signal(barrier, inc=1, device_id=p, device_id_type=MESH)

    pending = []

    def seq_copy(l, ph, j, src, dst):
        return pltpu.make_async_remote_copy(
            src_ref=src,
            dst_ref=dst,
            send_sem=send_sem.at[l * 4 + ph, j],
            recv_sem=recv_sem.at[l * 4 + ph, me],
            device_id=(j, bi),
            device_id_type=MESH,
        )

    def seq_wait(l, ph, k, src, dst):
        pltpu.make_async_remote_copy(
            src_ref=src,
            dst_ref=dst,
            send_sem=send_sem.at[l * 4 + ph, k],
            recv_sem=recv_sem.at[l * 4 + ph, k],
            device_id=(k, bi),
            device_id_type=MESH,
        ).wait_recv()

    def tblock(k):
        return pl.ds(pl.multiple_of(k * TL, TL), TL)

    def swap(axis, bit):
        return (me ^ (1 << bit), bi) if axis == "seq" else (me, bi ^ (1 << bit))

    def my_bit(axis, bit):
        return lax.rem((me if axis == "seq" else bi) // (1 << bit), 2)

    class Reduce:
        def __init__(self, l):
            self.l = l
            self.chains = []
            for c, plan in enumerate(plans):
                off, size, roff, stages = HALF * c, HALF, 0, []
                for i, (axis, bit) in enumerate(plan):
                    half = size // 2
                    mine = my_bit(axis, bit)
                    keep = pl.multiple_of(off + mine * half, 8)
                    give = pl.multiple_of(off + (1 - mine) * half, 8)
                    stages.append((i, axis, bit, half, keep, give, roff))
                    off, size, roff = keep, half, roff + half
                self.chains.append(stages)
            n = len(plans[0])
            self.n = n
            self.todo = [functools.partial(self.begin, 0)]
            for i in range(n):
                self.todo.append(functools.partial(self.reduce_step, i))
            for i in range(n - 1, -1, -1):
                self.todo.append(functools.partial(self.gather_step, i))

        def rs(self, c, stage):
            i, axis, bit, half, keep, give, roff = stage
            return pltpu.make_async_remote_copy(
                src_ref=FB.at[self.l, pl.ds(give, half)],
                dst_ref=RB.at[self.l, c, pl.ds(roff, half)],
                send_sem=ar_ssem.at[(self.l * 2 + c) * 2, i],
                recv_sem=ar_rsem.at[(self.l * 2 + c) * 2, i],
                device_id=swap(axis, bit),
                device_id_type=MESH,
            )

        def ag(self, c, stage):
            i, axis, bit, half, keep, give, roff = stage
            return pltpu.make_async_remote_copy(
                src_ref=FG.at[self.l, pl.ds(keep, half)],
                dst_ref=FG.at[self.l, pl.ds(keep, half)],
                send_sem=ar_ssem.at[(self.l * 2 + c) * 2 + 1, i],
                recv_sem=ar_rsem.at[(self.l * 2 + c) * 2 + 1, i],
                device_id=swap(axis, bit),
                device_id_type=MESH,
            )

        def begin(self, i):
            for c, stages in enumerate(self.chains):
                self.rs(c, stages[i]).start()

        def reduce_step(self, i):
            for c, stages in enumerate(self.chains):
                _, _, _, half, keep, _, roff = stages[i]
                self.rs(c, stages[i]).wait()
                step = min(half, 64)
                total = FB if i + 1 < self.n else FG

                def add(j, _, keep=keep, roff=roff, step=step, total=total):
                    at = pl.ds(pl.multiple_of(keep + j * step, 8), step)
                    total[self.l, at, :] = FB[self.l, at, :] + RB[self.l, c, pl.ds(pl.multiple_of(roff + j * step, 8), step), :]
                    return 0

                lax.fori_loop(0, half // step, add, 0)
                if i + 1 < self.n:
                    self.rs(c, stages[i + 1]).start()
                else:
                    self.ag(c, stages[i]).start()

        def gather_step(self, i):
            for c, stages in enumerate(self.chains):
                self.ag(c, stages[i]).wait()
                if i > 0:
                    self.ag(c, stages[i - 1]).start()
                else:
                    for q in range(CB // 2):
                        cb = c * (CB // 2) + q
                        copy = pltpu.make_async_copy(
                            FG.at[self.l, pl.ds(cb * D, D)],
                            gw_hbm.at[self.l, :, pl.ds(cb * LANES, LANES)],
                            out_sem.at[self.l, cb],
                        )
                        copy.start()
                        pending.append(copy.wait)

        def tick(self):
            if self.todo:
                self.todo.pop(0)()

    def norm_forward(l, src):
        def step(i, _):
            rows = pl.ds(pl.multiple_of(i * CHUNK, CHUNK), CHUNK)
            x = src[rows, :]
            center = x - jnp.mean(x, axis=-1, keepdims=True)
            spread = jnp.mean(center * center, axis=-1, keepdims=True)
            inv = lax.rsqrt(spread + EPSILON)
            xhat = center * inv
            RSTD[l, rows, :] = jnp.broadcast_to(inv, (CHUNK, LANES))
            for g in range(CG):
                XS[l, g, rows, :] = xhat[:, g * LANES : (g + 1) * LANES]
            return 0

        lax.fori_loop(0, TL // CHUNK, step, 0)

    def send_normed(l):
        for d in range(1, S):
            j = me ^ d
            copy = seq_copy(l, 0, j, XS.at[l, j // NSP], XR.at[l, tblock(me)])
            copy.start()
            pending.append(copy.wait_send)
        XR[l, tblock(me), :] = XS[l, cg]

    def scan_forward(l):
        gain = gain_ref[l : l + 1, clane]
        o2 = o2_ref[l : l + 1, clane]
        stp = step_ref[l : l + 1, clane]
        skip = skip_ref[l : l + 1, clane] * first_part
        first_row = lax.broadcasted_iota(jnp.int32, (TL, LANES), 0) == 0
        SIG[l, 0] = jnp.zeros((NL, LANES), F32)

        def block(k, carry):
            sig, last = carry

            @pl.when(k != me)
            def _():
                seq_wait(l, 0, k, XS.at[l, 0], XR.at[l, tblock(k)])

            normed = XR[l, tblock(k), :] * gain
            prev = jnp.where(first_row, last, pltpu.roll(normed, 1, 0))
            U[tblock(k), :] = normed + o2 * normed * prev
            z = stp * normed
            R[l, tblock(k), :] = jnp.maximum(z, 0.0) + jnp.log1p(jnp.exp(-jnp.abs(z)))
            na, wt = NA[l], WT[l]

            def inner(i, sig):
                for s in range(UN):
                    t = i * UN + s
                    at = pl.ds(k * TL + t, 1)
                    sig = jnp.exp2(na * R[l, at, :]) * sig + U[at, :]
                    SIG[l, k * TL + t + 1] = sig
                    P1[pl.ds(pl.multiple_of(t * 8, 8), 8), :] = rows8(wt * sig)
                return sig

            sig = lax.fori_loop(0, TL // UN, inner, sig)

            def finish(j, _):
                total = P1[pl.ds(j * 64, 8, stride=8), :]
                for s in range(1, 8):
                    total = total + P1[pl.ds(j * 64 + s, 8, stride=8), :]
                at = pl.ds(pl.multiple_of(k * TL + j * 8, 8), 8)
                Y[at, :] = total + skip * U[at, :]
                return 0

            lax.fori_loop(0, TL // 8, finish, 0)

            @pl.when(k == me)
            def _():
                YR[l, me] = Y[tblock(k), :]

            @pl.when(k != me)
            def _():
                seq_copy(l, 1, k, Y.at[tblock(k)], YR.at[l, me]).start()

            return sig, normed[TL - 1 : TL, :]

        lax.fori_loop(0, S, block, (jnp.zeros((NL, LANES), F32), jnp.zeros((1, LANES), F32)))
        return [seq_copy(l, 1, me ^ d, Y.at[tblock(me ^ d)], YR.at[l, me]).wait_send for d in range(1, S)]

    def mixed_of(l, g, rows):
        m = YR[l, g * NSP, rows, :]
        for h in range(1, NSP):
            m = m + YR[l, g * NSP + h, rows, :]
        return m

    def valid_of(i):
        pos = me * TL + i * CHUNK + lax.broadcasted_iota(jnp.int32, (CHUNK, 1), 0)
        return (pos < len_ref[0]).astype(F32)

    def glu_forward(l, src, dst):
        for d in range(1, S):
            j = me ^ d
            seq_wait(l, 1, j, Y.at[pl.ds(0, TL)], YR.at[l, j])

        def act(i, sq):
            rows = pl.ds(pl.multiple_of(i * CHUNK, CHUNK), CHUNK)
            valid = valid_of(i)
            for g in range(CG):
                m = mixed_of(l, g, rows)
                a = 0.5 * m * (1.0 + gelu_parts(m))
                LA[l, rows, g * LANES : (g + 1) * LANES] = a.astype(BF16)
                sq = sq + rows8(a * a * valid)
            return sq

        zero = jnp.zeros((8, LANES), F32)
        sq_act = lax.fori_loop(0, TL // CHUNK, act, zero)
        PJ[l] = jnp.dot(LA[l], W[l], preferred_element_type=F32) + bias_ref[l : l + 1, :]

        def gate(i, sq):
            sq_b, sq_s, cnt = sq
            rows = pl.ds(pl.multiple_of(i * CHUNK, CHUNK), CHUNK)
            valid = valid_of(i)
            for g in range(CG):
                cols = slice(g * LANES, (g + 1) * LANES)
                gcols = slice(D + g * LANES, D + (g + 1) * LANES)
                branch = PJ[l, rows, cols] * sigmoid(PJ[l, rows, gcols]) * valid
                out = src[rows, cols] + branch
                dst[rows, cols] = out
                sq_b = sq_b + rows8(branch * branch)
                sq_s = sq_s + rows8(out * out * valid)
            cnt = cnt + rows8(jnp.broadcast_to(valid, (CHUNK, LANES)))
            return sq_b, sq_s, cnt

        sq_b, sq_s, cnt = lax.fori_loop(0, TL // CHUNK, gate, (zero, zero, zero))
        for k, v in enumerate((sq_act, sq_b, sq_s, cnt)):
            ST[l, k] = v

    def glu_backward(l, gsrc):
        def gate(i, acc):
            rows = pl.ds(pl.multiple_of(i * CHUNK, CHUNK), CHUNK)
            valid = valid_of(i)
            out = []
            for g in range(CG):
                cols = slice(g * LANES, (g + 1) * LANES)
                gcols = slice(D + g * LANES, D + (g + 1) * LANES)
                gb = gsrc[rows, cols] * valid
                s = sigmoid(PJ[l, rows, gcols])
                one = gb * s
                two = one * PJ[l, rows, cols] * (1.0 - s)
                LG[rows, cols] = one.astype(BF16)
                LG[rows, gcols] = two.astype(BF16)
                out.append((rows8(one), rows8(two)))
            return tuple(a + b for a, b in zip(acc, [o[0] for o in out] + [o[1] for o in out]))

        zero = jnp.zeros((8, LANES), F32)
        bias = lax.fori_loop(0, TL // CHUNK, gate, (zero,) * CB)
        GA[...] = lax.dot_general(LG[...], W[l], (((1,), (1,)), ((), ())), preferred_element_type=F32)

        def act(i, _):
            rows = pl.ds(pl.multiple_of(i * CHUNK, CHUNK), CHUNK)
            for g in range(CG):
                m = mixed_of(l, g, rows)
                th = gelu_parts(m)
                slope = 0.5 * (1.0 + th) + 0.5 * m * (1.0 - th * th) * GELU_K * (1.0 + 3 * 0.044715 * m * m)
                GS[l, g, rows, :] = GA[rows, g * LANES : (g + 1) * LANES] * slope
            return 0

        lax.fori_loop(0, TL // CHUNK, act, 0)
        extra = [jnp.sum(b, axis=0, keepdims=True) for b in bias]
        extra += [jnp.sum(ST[l, k], axis=0, keepdims=True) for k in range(4)]
        extra += [jnp.zeros((EXTRA - len(extra), LANES), F32)]
        extra = jnp.concatenate(extra, axis=0)
        for g in range(CG):
            GS[l, g, TL : TL + EXTRA, :] = extra
        for d in range(1, S):
            j = me ^ d
            copy = seq_copy(l, 2, j, GS.at[l, j // NSP], GMR.at[l, me])
            copy.start()
            pending.append(copy.wait_send)
        GMR[l, me] = GS[l, cg]

    def weight_grad(l):
        for c in range(2):
            half = lax.dot_general(
                LA[l], LG[:, c * D : (c + 1) * D], (((0,), (0,)), ((), ())), preferred_element_type=F32
            )
            for q in range(CB // 2):
                FB[l, pl.ds((c * (CB // 2) + q) * D, D), :] = half[:, q * LANES : (q + 1) * LANES]

    def scan_backward(l, ticks):
        gain = gain_ref[l : l + 1, clane]
        o2 = o2_ref[l : l + 1, clane]
        stp = step_ref[l : l + 1, clane]
        skip = skip_ref[l : l + 1, clane]
        row_id = lax.broadcasted_iota(jnp.int32, (TL, LANES), 0)
        zero8 = jnp.zeros((8, LANES), F32)
        zeros = jnp.zeros((NL, LANES), F32)
        for v in range(4):
            VEC[v] = zero8

        def block(kk, carry):
            nu, acc, gdc, after = carry
            k = S - 1 - kk

            @pl.when(k != me)
            def _():
                seq_wait(l, 2, k, GS.at[l, 0], GMR.at[l, k])

            na, wt = NA[l], WT[l]

            def inner(ii, c):
                nu, acc, gdc = c
                i = TL // UN - 1 - ii
                for s in range(UN - 1, -1, -1):
                    t = i * UN + s
                    rate = R[l, pl.ds(k * TL + t, 1), :]
                    gm = GMR[l, k, pl.ds(t, 1), :]
                    mu = wt * gm + nu
                    acc = acc + gm * SIG[l, k * TL + t + 1]
                    at = pl.ds(pl.multiple_of(t * 8, 8), 8)
                    P1[at, :] = rows8(mu)
                    nu = jnp.exp2(na * rate) * mu
                    q = nu * SIG[l, k * TL + t]
                    gdc = gdc + q * rate
                    P2[at, :] = rows8(na * q)
                return nu, acc, gdc

            nu, acc, gdc = lax.fori_loop(0, TL // UN, inner, (nu, acc, gdc))

            def finish(j, _):
                one = P1[pl.ds(j * 64, 8, stride=8), :]
                two = P2[pl.ds(j * 64, 8, stride=8), :]
                for s in range(1, 8):
                    one = one + P1[pl.ds(j * 64 + s, 8, stride=8), :]
                    two = two + P2[pl.ds(j * 64 + s, 8, stride=8), :]
                at = pl.ds(pl.multiple_of(j * 8, 8), 8)
                GX[pl.ds(pl.multiple_of(k * TL + j * 8, 8), 8), :] = one
                GA[at, 0:LANES] = two
                return 0

            lax.fori_loop(0, TL // 8, finish, 0)
            xhat = XR[l, tblock(k), :]
            normed = xhat * gain
            before = XR[l, pl.ds(jnp.maximum(k * TL - 1, 0), 1), :] * gain
            before = jnp.where(k == 0, 0.0, before)
            prev = jnp.where(row_id == 0, before, pltpu.roll(normed, 1, 0))
            gm = GMR[l, k, 0:TL, :] * first_part
            gdrv = GX[tblock(k), :] + skip * gm
            grate = GA[0:TL, 0:LANES] * LN2
            both = gdrv * normed
            h = o2 * both
            later = jnp.where(row_id == TL - 1, after, pltpu.roll(h, TL - 1, 0))
            slope = sigmoid(stp * normed) * grate
            gnormed = gdrv * (1.0 + o2 * prev) + later + slope * stp
            GX[tblock(k), :] = gnormed * gain
            VEC[0] = VEC[0] + rows8(gm * (normed + o2 * normed * prev))
            VEC[1] = VEC[1] + rows8(both * prev)
            VEC[2] = VEC[2] + rows8(slope * normed)
            VEC[3] = VEC[3] + rows8(gnormed * xhat)

            @pl.when(k == me)
            def _():
                GXR[l, me] = GX[tblock(k), :]

            @pl.when(k != me)
            def _():
                seq_copy(l, 3, k, GX.at[tblock(k)], GXR.at[l, me]).start()

            for at, tick in ticks.items():

                @pl.when(kk == at)
                def _(tick=tick):
                    tick()

            return nu, acc, gdc, h[0:1, :]

        carry = (zeros, zeros, zeros, jnp.zeros((1, LANES), F32))
        _, acc, gdc, _ = lax.fori_loop(0, S, block, carry)
        sent = [seq_copy(l, 3, me ^ d, GX.at[tblock(me ^ d)], GXR.at[l, me]).wait_send for d in range(1, S)]
        SBW[l, 0, 0:NL, :] = acc
        SBW[l, 0, NL : 2 * NL, :] = gdc
        vec = [jnp.sum(VEC[v], axis=0, keepdims=True) for v in range(4)]
        vec += [jnp.zeros((4, LANES), F32)]
        SBW[l, 0, 2 * NL : 2 * NL + 8, :] = jnp.concatenate(vec, axis=0)
        extra = GMR[l, 0, TL : TL + EXTRA, :]
        for k in range(1, S):
            extra = extra + GMR[l, k, TL : TL + EXTRA, :]
        SBW[l, 0, 2 * NL + 8 : 2 * NL + 8 + EXTRA, :] = extra
        return sent

    class Small:
        def __init__(self, l):
            self.l = l
            nb = len(bits_of(B))
            self.todo = [functools.partial(self.start, 0)]
            self.todo += [functools.partial(self.join, i) for i in range(nb)]
            self.todo += [self.gathered]
            self.nb = nb

        def copy(self, i):
            return pltpu.make_async_remote_copy(
                src_ref=SBW.at[self.l, i],
                dst_ref=SBR.at[self.l, i],
                send_sem=sb_ssem.at[self.l, i],
                recv_sem=sb_rsem.at[self.l, i],
                device_id=(me, bi ^ (1 << i)),
                device_id_type=MESH,
            )

        def seq(self, j, slot, rslot):
            return pltpu.make_async_remote_copy(
                src_ref=SBW.at[self.l, self.nb],
                dst_ref=SBG.at[self.l, slot],
                send_sem=sg_ssem.at[self.l, j],
                recv_sem=sg_rsem.at[self.l, rslot],
                device_id=(j, bi),
                device_id_type=MESH,
            )

        def start(self, i):
            self.copy(i).start()

        def join(self, i):
            self.copy(i).wait()
            SBW[self.l, i + 1] = SBW[self.l, i] + SBR[self.l, i]
            if i + 1 < self.nb:
                self.start(i + 1)
            else:
                for d in range(1, S):
                    self.seq(me ^ d, me, me).start()
                SBG[self.l, me] = SBW[self.l, self.nb]

        def gathered(self):
            for d in range(1, S):
                self.seq(me ^ d, me ^ d, me ^ d).wait()
            l = self.l
            for g in range(CG):
                cols = slice(g * LANES, (g + 1) * LANES)
                vec = None
                for h in range(NSP):
                    slot = g * NSP + h
                    rows = slice(h * NL, (h + 1) * NL)
                    acc = SBG[l, slot, 0:NL, :]
                    gin_out[l, rows, cols] = OUTM[l, rows, cols] * acc
                    gout_out[l, rows, cols] = INM[l, rows, cols] * acc
                    gdec_out[l, rows, cols] = -SBG[l, slot, NL : 2 * NL, :]
                    part = SBG[l, slot, 2 * NL : 2 * NL + 8, :]
                    vec = part if vec is None else vec + part
                gskip_out[l : l + 1, cols] = vec[0:1]
                go2_out[l : l + 1, cols] = vec[1:2]
                gstep_out[l : l + 1, cols] = vec[2:3]
                ggain_out[l : l + 1, cols] = vec[3:4]
            base = 2 * NL + 8
            for q in range(CB):
                gbias_out[l : l + 1, q * LANES : (q + 1) * LANES] = SBG[l, 0, base + q : base + q + 1, :]
            sq = jnp.sum(SBG[l, 0, base + CB : base + CB + 8, :], axis=1, keepdims=True)
            count = sq[3:4] * (1.0 / LANES)
            root = jnp.sqrt(sq[0:3] / (count * D))
            col = lax.broadcasted_iota(jnp.int32, (1, 3), 1)
            stats_out[l : l + 1, :] = jnp.where(col == 0, root[0:1], jnp.where(col == 1, root[1:2], root[2:3]))

        def tick(self):
            if self.todo:
                self.todo.pop(0)()

    def norm_backward(l, gsrc, gdst):
        for d in range(1, S):
            j = me ^ d
            seq_wait(l, 3, j, GX.at[pl.ds(0, TL)], GXR.at[l, j])

        def step(i, _):
            rows = pl.ds(pl.multiple_of(i * CHUNK, CHUNK), CHUNK)
            inv = RSTD[l, rows, :]
            gx, xh = [], []
            s1 = s2 = None
            for g in range(CG):
                v = GXR[l, g * NSP, rows, :]
                for h in range(1, NSP):
                    v = v + GXR[l, g * NSP + h, rows, :]
                x = XS[l, g, rows, :]
                gx.append(v)
                xh.append(x)
                s1 = v if s1 is None else s1 + v
                s2 = v * x if s2 is None else s2 + v * x
            m1 = jnp.sum(s1, axis=-1, keepdims=True) * (1.0 / D)
            m2 = jnp.sum(s2, axis=-1, keepdims=True) * (1.0 / D)
            for g in range(CG):
                cols = slice(g * LANES, (g + 1) * LANES)
                gdst[rows, cols] = gsrc[rows, cols] + inv * (gx[g] - m1 - xh[g] * m2)
            return 0

        lax.fori_loop(0, TL // CHUNK, step, 0)

    norm_forward(0, x_ref)
    pl.semaphore_wait(barrier, len(partners))
    send_normed(0)
    for c in loads:
        c.wait()
    nrows = pl.ds(pl.multiple_of(n0, 8), NL)
    for l in range(L):
        NA[l] = DEC[l, nrows, clane] * (-LOG2E)
        WT[l] = INM[l, nrows, clane] * OUTM[l, nrows, clane]
    streams = [x_ref] + [STR.at[l] for l in range(L - 1)] + [y_out]
    for l in range(L):
        if l:
            norm_forward(l, streams[l])
            send_normed(l)
        sent = scan_forward(l)
        glu_forward(l, streams[l], streams[l + 1])
        for done in sent:
            done()

    grads = [gx_out] + [GRD.at[l] for l in range(L - 1)] + [ct_ref]
    reduces = []
    smalls = []
    for l in range(L - 1, -1, -1):
        glu_backward(l, grads[l + 1])
        weight_grad(l)
        mine = Reduce(l)
        mine.tick()
        reduces.append(mine)

        def some():
            for r in reduces + smalls:
                r.tick()

        ticks = {}
        if S >= 4:
            ticks = {S // 4 - 1: some, S // 2 - 1: some, 3 * S // 4 - 1: some}
        sent = scan_backward(l, ticks)
        small = Small(l)
        small.tick()
        smalls.append(small)
        some()
        norm_backward(l, grads[l + 1], grads[l])
        for done in sent:
            done()
    while any(r.todo for r in reduces + smalls):
        for r in reduces + smalls:
            r.tick()
    for done in pending:
        done()


def per_device(
    stream_in, cotangent, lengths, norm_gain, decay_rate, in_map, out_map, skip_gain, order_two, step_gain, glu_weight, glu_bias
):
    S, B = lax.axis_size("seq"), lax.axis_size("batch")
    _, TL, D = stream_in.shape
    L, NS = decay_rate.shape[:2]
    UN = math.gcd(TL, 16)
    CG, E2 = D // LANES, 2 * D
    NL = NS // (S // CG)
    TA = S * TL
    CB = E2 // LANES
    GROWS = D * CB
    SBR = 2 * NL + 8 + EXTRA
    NB, NST = len(bits_of(B)), len(bits_of(B)) + len(bits_of(S))
    shape = jax.ShapeDtypeStruct
    vmem = pl.BlockSpec(memory_space=pltpu.VMEM)
    smem = pl.BlockSpec(memory_space=pltpu.SMEM)
    hbm = pl.BlockSpec(memory_space=pl.ANY)
    buf = pltpu.VMEM
    dma = pltpu.SemaphoreType.DMA
    outs = pl.pallas_call(
        functools.partial(kernel, (S, B, TL, D, NS, L, UN)),
        out_shape=[
            shape((TL, D), F32), shape((TL, D), F32), shape((L, D), F32),
            shape((L, NS, D), F32), shape((L, NS, D), F32), shape((L, NS, D), F32),
            shape((L, D), F32), shape((L, D), F32), shape((L, D), F32),
            shape((L, D, E2), F32), shape((L, E2), F32), shape((L, 3), F32),
        ],
        in_specs=[vmem, vmem, smem, vmem, hbm, hbm, hbm, vmem, vmem, vmem, hbm, vmem],
        out_specs=[vmem] * 9 + [hbm, vmem, vmem],
        scratch_shapes=[
            buf((L, D, E2), BF16), buf((L, NS, D), F32), buf((L, NS, D), F32), buf((L, NS, D), F32),
            buf((L, NL, LANES), F32), buf((L, NL, LANES), F32),
            buf((L, CG, TL, LANES), F32), buf((L, TA, LANES), F32), buf((L, TL, LANES), F32),
            buf((L, TA, LANES), F32), buf((TA, LANES), F32),
            buf((L, S, TL, LANES), F32), buf((L, CG, TL + EXTRA, LANES), F32), buf((L, S, TL + EXTRA, LANES), F32),
            buf((L, S, TL, LANES), F32),
            buf((L, TA + 1, NL, LANES), F32), buf((TL * 8, LANES), F32), buf((max(TL * 8, TA), LANES), F32),
            buf((L, TL, D), BF16), buf((L, TL, E2), F32), buf((TL, E2), BF16), buf((TL, D), F32),
            buf((L - 1, TL, D), F32), buf((L - 1, TL, D), F32), buf((L, 4, 8, LANES), F32),
            buf((L, GROWS, LANES), F32), buf((L, 2, GROWS // 2, LANES), F32), buf((L, GROWS, LANES), F32),
            buf((L, NB + 1, SBR, LANES), F32), buf((L, NB, SBR, LANES), F32), buf((L, S, SBR, LANES), F32),
            buf((4, 8, LANES), F32),
            dma((4,)), dma((L * 4, S)), dma((L * 4, S)), dma((L * 4, NST)), dma((L * 4, NST)),
            dma((L, NB)), dma((L, NB)), dma((L, S)), dma((L, S)), dma((L, CB)),
        ],
        compiler_params=pltpu.CompilerParams(
            collective_id=0, has_side_effects=True, vmem_limit_bytes=61 * 2**20
        ),
        name="liquid_layers",
    )(
        stream_in[0], cotangent[0], lengths, norm_gain, decay_rate, in_map, out_map,
        skip_gain, order_two, step_gain, glu_weight, glu_bias,
    )
    return (outs[0][None], outs[1][None], *outs[2:])


def solution(mesh):
    split = P("batch", "seq", None)
    in_specs = (split, split, P("batch")) + (P(),) * 9
    out_specs = (split, split) + (P(),) * 10
    return jax.shard_map(per_device, mesh=mesh, in_specs=in_specs, out_specs=out_specs, check_vma=False)
```

```python
import functools
import math

import jax
import jax.numpy as jnp
from jax import lax
from jax.experimental import pallas as pl
from jax.experimental.pallas import tpu as pltpu
from jax.sharding import PartitionSpec as P

MESH = pl.DeviceIdType.MESH
EPSILON = 1e-05
LOG2E = 1.4426950408889634
LN2 = 0.6931471805599453
GELU_K = math.sqrt(2.0 / math.pi)
F32 = jnp.float32
BF16 = jnp.bfloat16
LANES = 128
CHUNK = 32
EXTRA = 16


def rows8(v):
    return v.reshape(v.shape[0] // 8, 8, v.shape[1]).sum(0)


def sigmoid(v):
    return 1.0 / (1.0 + jnp.exp(-v))


def gelu_parts(m):
    th = jnp.tanh(GELU_K * (m + 0.044715 * m * m * m))
    return th


def bits_of(n):
    return [i for i in range(n.bit_length() - 1)]


def orders(seq, batch):
    s = [("seq", b) for b in bits_of(seq)]
    b = [("batch", b) for b in bits_of(batch)]
    first = s[:1]
    s, b = s[1:], b
    one, two = [], []
    for i in range(max(len(s), len(b))):
        one += s[i : i + 1] + b[i : i + 1]
        two += b[i : i + 1] + s[i : i + 1]
    return [first + one, first + two]


def kernel(cfg, *refs):
    S, B, TL, D, NS, L, UN = cfg
    CG = D // LANES
    NSP = S // CG
    NL = NS // NSP
    E2 = 2 * D
    CB = E2 // LANES
    GROWS = D * CB
    SB_ROWS = 2 * NL + 24
    plans = orders(S, B)
    HALF = GROWS // 2
    (
        x_ref, ct_ref, len_ref, gain_ref, dec_hbm, in_hbm, out_hbm, skip_ref, o2_ref, step_ref, w_hbm, bias_ref,
        y_out, gx_out, ggain_out, gdec_out, gin_out, gout_out, gskip_out, go2_out, gstep_out, gw_hbm, gbias_out, stats_out,
        W, DEC, INM, OUTM, NA, WT,
        XS, XR, RSTD, R, Y, YR, GS, GMR, GXR,
        SIG, P1, P2, LA, PJ, LG, GA, STR, GRD, ST,
        FB, RB, FG, SBW, SBR, SBG, VEC,
        load_sem, send_sem, recv_sem, ar_ssem, ar_rsem, sb_ssem, sb_rsem, sg_ssem, sg_rsem, out_sem,
    ) = refs
    U, GX = P2, Y
    me = lax.axis_index("seq")
    bi = lax.axis_index("batch")
    cg = me // NSP
    nh = lax.rem(me, NSP)
    n0 = nh * NL
    first_part = (nh == 0).astype(F32)
    clane = pl.ds(pl.multiple_of(cg * LANES, LANES), LANES)

    loads = [
        pltpu.make_async_copy(w_hbm, W, load_sem.at[0]),
        pltpu.make_async_copy(dec_hbm, DEC, load_sem.at[1]),
        pltpu.make_async_copy(in_hbm, INM, load_sem.at[2]),
        pltpu.make_async_copy(out_hbm, OUTM, load_sem.at[3]),
    ]
    for c in loads:
        c.start()

    barrier = pltpu.get_barrier_semaphore()
    partners = [(me ^ d, bi) for d in range(1, S)] + [(me, bi ^ (1 << b)) for b in bits_of(B)]
    for p in partners:
        pl.semaphore_signal(barrier, inc=1, device_id=p, device_id_type=MESH)

    pending = []

    def seq_copy(l, ph, j, src, dst):
        return pltpu.make_async_remote_copy(
            src_ref=src,
            dst_ref=dst,
            send_sem=send_sem.at[l * 4 + ph, j],
            recv_sem=recv_sem.at[l * 4 + ph, me],
            device_id=(j, bi),
            device_id_type=MESH,
        )

    def seq_wait(l, ph, k, src, dst):
        pltpu.make_async_remote_copy(
            src_ref=src,
            dst_ref=dst,
            send_sem=send_sem.at[l * 4 + ph, k],
            recv_sem=recv_sem.at[l * 4 + ph, k],
            device_id=(k, bi),
            device_id_type=MESH,
        ).wait_recv()

    def tblock(k):
        return pl.ds(pl.multiple_of(k * TL, TL), TL)

    def swap(axis, bit):
        return (me ^ (1 << bit), bi) if axis == "seq" else (me, bi ^ (1 << bit))

    def my_bit(axis, bit):
        return lax.rem((me if axis == "seq" else bi) // (1 << bit), 2)

    class Reduce:
        def __init__(self, l):
            self.l = l
            self.chains = []
            for c, plan in enumerate(plans):
                off, size, roff, stages = HALF * c, HALF, 0, []
                for i, (axis, bit) in enumerate(plan):
                    half = size // 2
                    mine = my_bit(axis, bit)
                    keep = pl.multiple_of(off + mine * half, 8)
                    give = pl.multiple_of(off + (1 - mine) * half, 8)
                    stages.append((i, axis, bit, half, keep, give, roff))
                    off, size, roff = keep, half, roff + half
                self.chains.append(stages)
            n = len(plans[0])
            self.n = n
            self.todo = [functools.partial(self.begin, 0)]
            for i in range(n):
                self.todo.append(functools.partial(self.reduce_step, i))
            for i in range(n - 1, -1, -1):
                self.todo.append(functools.partial(self.gather_step, i))

        def rs(self, c, stage):
            i, axis, bit, half, keep, give, roff = stage
            return pltpu.make_async_remote_copy(
                src_ref=FB.at[self.l, pl.ds(give, half)],
                dst_ref=RB.at[self.l, c, pl.ds(roff, half)],
                send_sem=ar_ssem.at[(self.l * 2 + c) * 2, i],
                recv_sem=ar_rsem.at[(self.l * 2 + c) * 2, i],
                device_id=swap(axis, bit),
                device_id_type=MESH,
            )

        def ag(self, c, stage):
            i, axis, bit, half, keep, give, roff = stage
            return pltpu.make_async_remote_copy(
                src_ref=FG.at[self.l, pl.ds(keep, half)],
                dst_ref=FG.at[self.l, pl.ds(keep, half)],
                send_sem=ar_ssem.at[(self.l * 2 + c) * 2 + 1, i],
                recv_sem=ar_rsem.at[(self.l * 2 + c) * 2 + 1, i],
                device_id=swap(axis, bit),
                device_id_type=MESH,
            )

        def begin(self, i):
            for c, stages in enumerate(self.chains):
                self.rs(c, stages[i]).start()

        def reduce_step(self, i):
            for c, stages in enumerate(self.chains):
                _, _, _, half, keep, _, roff = stages[i]
                self.rs(c, stages[i]).wait()
                step = min(half, 64)
                total = FB if i + 1 < self.n else FG

                def add(j, _, keep=keep, roff=roff, step=step, total=total):
                    at = pl.ds(pl.multiple_of(keep + j * step, 8), step)
                    total[self.l, at, :] = FB[self.l, at, :] + RB[self.l, c, pl.ds(pl.multiple_of(roff + j * step, 8), step), :]
                    return 0

                lax.fori_loop(0, half // step, add, 0)
                if i + 1 < self.n:
                    self.rs(c, stages[i + 1]).start()
                else:
                    self.ag(c, stages[i]).start()

        def gather_step(self, i):
            for c, stages in enumerate(self.chains):
                self.ag(c, stages[i]).wait()
                if i > 0:
                    self.ag(c, stages[i - 1]).start()
                else:
                    for q in range(CB // 2):
                        cb = c * (CB // 2) + q
                        copy = pltpu.make_async_copy(
                            FG.at[self.l, pl.ds(cb * D, D)],
                            gw_hbm.at[self.l, :, pl.ds(cb * LANES, LANES)],
                            out_sem.at[self.l, cb],
                        )
                        copy.start()
                        pending.append(copy.wait)

        def tick(self):
            if self.todo:
                self.todo.pop(0)()

    def norm_forward(l, src):
        def step(i, _):
            rows = pl.ds(pl.multiple_of(i * CHUNK, CHUNK), CHUNK)
            x = src[rows, :]
            center = x - jnp.mean(x, axis=-1, keepdims=True)
            spread = jnp.mean(center * center, axis=-1, keepdims=True)
            inv = lax.rsqrt(spread + EPSILON)
            xhat = center * inv
            RSTD[l, rows, :] = jnp.broadcast_to(inv, (CHUNK, LANES))
            for g in range(CG):
                XS[l, g, rows, :] = xhat[:, g * LANES : (g + 1) * LANES]
            return 0

        lax.fori_loop(0, TL // CHUNK, step, 0)

    def send_normed(l):
        for d in range(1, S):
            j = me ^ d
            copy = seq_copy(l, 0, j, XS.at[l, j // NSP], XR.at[l, tblock(me)])
            copy.start()
            pending.append(copy.wait_send)
        XR[l, tblock(me), :] = XS[l, cg]

    def scan_forward(l):
        gain = gain_ref[l : l + 1, clane]
        o2 = o2_ref[l : l + 1, clane]
        stp = step_ref[l : l + 1, clane]
        skip = skip_ref[l : l + 1, clane] * first_part
        first_row = lax.broadcasted_iota(jnp.int32, (TL, LANES), 0) == 0
        SIG[l, 0] = jnp.zeros((NL, LANES), F32)

        def block(k, carry):
            sig, last = carry

            @pl.when(k != me)
            def _():
                seq_wait(l, 0, k, XS.at[l, 0], XR.at[l, tblock(k)])

            normed = XR[l, tblock(k), :] * gain
            prev = jnp.where(first_row, last, pltpu.roll(normed, 1, 0))
            U[tblock(k), :] = normed + o2 * normed * prev
            z = stp * normed
            R[l, tblock(k), :] = jnp.maximum(z, 0.0) + jnp.log1p(jnp.exp(-jnp.abs(z)))
            na, wt = NA[l], WT[l]

            def inner(i, sig):
                for s in range(UN):
                    t = i * UN + s
                    at = pl.ds(k * TL + t, 1)
                    sig = jnp.exp2(na * R[l, at, :]) * sig + U[at, :]
                    SIG[l, k * TL + t + 1] = sig
                    P1[pl.ds(pl.multiple_of(t * 8, 8), 8), :] = rows8(wt * sig)
                return sig

            sig = lax.fori_loop(0, TL // UN, inner, sig)

            def finish(j, _):
                total = P1[pl.ds(j * 64, 8, stride=8), :]
                for s in range(1, 8):
                    total = total + P1[pl.ds(j * 64 + s, 8, stride=8), :]
                at = pl.ds(pl.multiple_of(k * TL + j * 8, 8), 8)
                Y[at, :] = total + skip * U[at, :]
                return 0

            lax.fori_loop(0, TL // 8, finish, 0)

            @pl.when(k == me)
            def _():
                YR[l, me] = Y[tblock(k), :]

            @pl.when(k != me)
            def _():
                seq_copy(l, 1, k, Y.at[tblock(k)], YR.at[l, me]).start()

            return sig, normed[TL - 1 : TL, :]

        lax.fori_loop(0, S, block, (jnp.zeros((NL, LANES), F32), jnp.zeros((1, LANES), F32)))
        return [seq_copy(l, 1, me ^ d, Y.at[tblock(me ^ d)], YR.at[l, me]).wait_send for d in range(1, S)]

    def mixed_of(l, g, rows):
        m = YR[l, g * NSP, rows, :]
        for h in range(1, NSP):
            m = m + YR[l, g * NSP + h, rows, :]
        return m

    def valid_of(i):
        pos = me * TL + i * CHUNK + lax.broadcasted_iota(jnp.int32, (CHUNK, 1), 0)
        return (pos < len_ref[0]).astype(F32)

    def glu_forward(l, src, dst):
        for d in range(1, S):
            j = me ^ d
            seq_wait(l, 1, j, Y.at[pl.ds(0, TL)], YR.at[l, j])

        def act(i, sq):
            rows = pl.ds(pl.multiple_of(i * CHUNK, CHUNK), CHUNK)
            valid = valid_of(i)
            for g in range(CG):
                m = mixed_of(l, g, rows)
                a = 0.5 * m * (1.0 + gelu_parts(m))
                LA[l, rows, g * LANES : (g + 1) * LANES] = a.astype(BF16)
                sq = sq + rows8(a * a * valid)
            return sq

        zero = jnp.zeros((8, LANES), F32)
        sq_act = lax.fori_loop(0, TL // CHUNK, act, zero)
        PJ[l] = jnp.dot(LA[l], W[l], preferred_element_type=F32) + bias_ref[l : l + 1, :]

        def gate(i, sq):
            sq_b, sq_s, cnt = sq
            rows = pl.ds(pl.multiple_of(i * CHUNK, CHUNK), CHUNK)
            valid = valid_of(i)
            for g in range(CG):
                cols = slice(g * LANES, (g + 1) * LANES)
                gcols = slice(D + g * LANES, D + (g + 1) * LANES)
                branch = PJ[l, rows, cols] * sigmoid(PJ[l, rows, gcols]) * valid
                out = src[rows, cols] + branch
                dst[rows, cols] = out
                sq_b = sq_b + rows8(branch * branch)
                sq_s = sq_s + rows8(out * out * valid)
            cnt = cnt + rows8(jnp.broadcast_to(valid, (CHUNK, LANES)))
            return sq_b, sq_s, cnt

        sq_b, sq_s, cnt = lax.fori_loop(0, TL // CHUNK, gate, (zero, zero, zero))
        for k, v in enumerate((sq_act, sq_b, sq_s, cnt)):
            ST[l, k] = v

    def glu_backward(l, gsrc):
        def gate(i, acc):
            rows = pl.ds(pl.multiple_of(i * CHUNK, CHUNK), CHUNK)
            valid = valid_of(i)
            out = []
            for g in range(CG):
                cols = slice(g * LANES, (g + 1) * LANES)
                gcols = slice(D + g * LANES, D + (g + 1) * LANES)
                gb = gsrc[rows, cols] * valid
                s = sigmoid(PJ[l, rows, gcols])
                one = gb * s
                two = one * PJ[l, rows, cols] * (1.0 - s)
                LG[rows, cols] = one.astype(BF16)
                LG[rows, gcols] = two.astype(BF16)
                out.append((rows8(one), rows8(two)))
            return tuple(a + b for a, b in zip(acc, [o[0] for o in out] + [o[1] for o in out]))

        zero = jnp.zeros((8, LANES), F32)
        bias = lax.fori_loop(0, TL // CHUNK, gate, (zero,) * CB)
        GA[...] = lax.dot_general(LG[...], W[l], (((1,), (1,)), ((), ())), preferred_element_type=F32)

        def act(i, _):
            rows = pl.ds(pl.multiple_of(i * CHUNK, CHUNK), CHUNK)
            for g in range(CG):
                m = mixed_of(l, g, rows)
                th = gelu_parts(m)
                slope = 0.5 * (1.0 + th) + 0.5 * m * (1.0 - th * th) * GELU_K * (1.0 + 3 * 0.044715 * m * m)
                GS[l, g, rows, :] = GA[rows, g * LANES : (g + 1) * LANES] * slope
            return 0

        lax.fori_loop(0, TL // CHUNK, act, 0)
        extra = [jnp.sum(b, axis=0, keepdims=True) for b in bias]
        extra += [jnp.sum(ST[l, k], axis=0, keepdims=True) for k in range(4)]
        extra += [jnp.zeros((EXTRA - len(extra), LANES), F32)]
        extra = jnp.concatenate(extra, axis=0)
        for g in range(CG):
            GS[l, g, TL : TL + EXTRA, :] = extra
        for d in range(1, S):
            j = me ^ d
            copy = seq_copy(l, 2, j, GS.at[l, j // NSP], GMR.at[l, me])
            copy.start()
            pending.append(copy.wait_send)
        GMR[l, me] = GS[l, cg]

    def weight_grad(l):
        for c in range(2):
            half = lax.dot_general(
                LA[l], LG[:, c * D : (c + 1) * D], (((0,), (0,)), ((), ())), preferred_element_type=F32
            )
            for q in range(CB // 2):
                FB[l, pl.ds((c * (CB // 2) + q) * D, D), :] = half[:, q * LANES : (q + 1) * LANES]

    def scan_backward(l, ticks):
        gain = gain_ref[l : l + 1, clane]
        o2 = o2_ref[l : l + 1, clane]
        stp = step_ref[l : l + 1, clane]
        skip = skip_ref[l : l + 1, clane]
        row_id = lax.broadcasted_iota(jnp.int32, (TL, LANES), 0)
        zero8 = jnp.zeros((8, LANES), F32)
        zeros = jnp.zeros((NL, LANES), F32)
        for v in range(4):
            VEC[v] = zero8

        def block(kk, carry):
            nu, acc, gdc, after = carry
            k = S - 1 - kk

            @pl.when(k != me)
            def _():
                seq_wait(l, 2, k, GS.at[l, 0], GMR.at[l, k])

            na, wt = NA[l], WT[l]

            def inner(ii, c):
                nu, acc, gdc = c
                i = TL // UN - 1 - ii
                for s in range(UN - 1, -1, -1):
                    t = i * UN + s
                    rate = R[l, pl.ds(k * TL + t, 1), :]
                    gm = GMR[l, k, pl.ds(t, 1), :]
                    mu = wt * gm + nu
                    acc = acc + gm * SIG[l, k * TL + t + 1]
                    at = pl.ds(pl.multiple_of(t * 8, 8), 8)
                    P1[at, :] = rows8(mu)
                    nu = jnp.exp2(na * rate) * mu
                    q = nu * SIG[l, k * TL + t]
                    gdc = gdc + q * rate
                    P2[at, :] = rows8(na * q)
                return nu, acc, gdc

            nu, acc, gdc = lax.fori_loop(0, TL // UN, inner, (nu, acc, gdc))

            def finish(j, _):
                one = P1[pl.ds(j * 64, 8, stride=8), :]
                two = P2[pl.ds(j * 64, 8, stride=8), :]
                for s in range(1, 8):
                    one = one + P1[pl.ds(j * 64 + s, 8, stride=8), :]
                    two = two + P2[pl.ds(j * 64 + s, 8, stride=8), :]
                at = pl.ds(pl.multiple_of(j * 8, 8), 8)
                GX[pl.ds(pl.multiple_of(k * TL + j * 8, 8), 8), :] = one
                GA[at, 0:LANES] = two
                return 0

            lax.fori_loop(0, TL // 8, finish, 0)
            xhat = XR[l, tblock(k), :]
            normed = xhat * gain
            before = XR[l, pl.ds(jnp.maximum(k * TL - 1, 0), 1), :] * gain
            before = jnp.where(k == 0, 0.0, before)
            prev = jnp.where(row_id == 0, before, pltpu.roll(normed, 1, 0))
            gm = GMR[l, k, 0:TL, :] * first_part
            gdrv = GX[tblock(k), :] + skip * gm
            grate = GA[0:TL, 0:LANES] * LN2
            both = gdrv * normed
            h = o2 * both
            later = jnp.where(row_id == TL - 1, after, pltpu.roll(h, TL - 1, 0))
            slope = sigmoid(stp * normed) * grate
            gnormed = gdrv * (1.0 + o2 * prev) + later + slope * stp
            GX[tblock(k), :] = gnormed * gain
            VEC[0] = VEC[0] + rows8(gm * (normed + o2 * normed * prev))
            VEC[1] = VEC[1] + rows8(both * prev)
            VEC[2] = VEC[2] + rows8(slope * normed)
            VEC[3] = VEC[3] + rows8(gnormed * xhat)

            @pl.when(k == me)
            def _():
                GXR[l, me] = GX[tblock(k), :]

            @pl.when(k != me)
            def _():
                seq_copy(l, 3, k, GX.at[tblock(k)], GXR.at[l, me]).start()

            for at, tick in ticks.items():

                @pl.when(kk == at)
                def _(tick=tick):
                    tick()

            return nu, acc, gdc, h[0:1, :]

        carry = (zeros, zeros, zeros, jnp.zeros((1, LANES), F32))
        _, acc, gdc, _ = lax.fori_loop(0, S, block, carry)
        sent = [seq_copy(l, 3, me ^ d, GX.at[tblock(me ^ d)], GXR.at[l, me]).wait_send for d in range(1, S)]
        SBW[l, 0, 0:NL, :] = acc
        SBW[l, 0, NL : 2 * NL, :] = gdc
        vec = [jnp.sum(VEC[v], axis=0, keepdims=True) for v in range(4)]
        vec += [jnp.zeros((4, LANES), F32)]
        SBW[l, 0, 2 * NL : 2 * NL + 8, :] = jnp.concatenate(vec, axis=0)
        extra = GMR[l, 0, TL : TL + EXTRA, :]
        for k in range(1, S):
            extra = extra + GMR[l, k, TL : TL + EXTRA, :]
        SBW[l, 0, 2 * NL + 8 : 2 * NL + 8 + EXTRA, :] = extra
        return sent

    class Small:
        def __init__(self, l):
            self.l = l
            nb = len(bits_of(B))
            self.todo = [functools.partial(self.start, 0)]
            self.todo += [functools.partial(self.join, i) for i in range(nb)]
            self.todo += [self.gathered]
            self.nb = nb

        def copy(self, i):
            return pltpu.make_async_remote_copy(
                src_ref=SBW.at[self.l, i],
                dst_ref=SBR.at[self.l, i],
                send_sem=sb_ssem.at[self.l, i],
                recv_sem=sb_rsem.at[self.l, i],
                device_id=(me, bi ^ (1 << i)),
                device_id_type=MESH,
            )

        def seq(self, j, slot, rslot):
            return pltpu.make_async_remote_copy(
                src_ref=SBW.at[self.l, self.nb],
                dst_ref=SBG.at[self.l, slot],
                send_sem=sg_ssem.at[self.l, j],
                recv_sem=sg_rsem.at[self.l, rslot],
                device_id=(j, bi),
                device_id_type=MESH,
            )

        def start(self, i):
            self.copy(i).start()

        def join(self, i):
            self.copy(i).wait()
            SBW[self.l, i + 1] = SBW[self.l, i] + SBR[self.l, i]
            if i + 1 < self.nb:
                self.start(i + 1)
            else:
                for d in range(1, S):
                    self.seq(me ^ d, me, me).start()
                SBG[self.l, me] = SBW[self.l, self.nb]

        def gathered(self):
            for d in range(1, S):
                self.seq(me ^ d, me ^ d, me ^ d).wait()
            l = self.l
            for g in range(CG):
                cols = slice(g * LANES, (g + 1) * LANES)
                vec = None
                for h in range(NSP):
                    slot = g * NSP + h
                    rows = slice(h * NL, (h + 1) * NL)
                    acc = SBG[l, slot, 0:NL, :]
                    gin_out[l, rows, cols] = OUTM[l, rows, cols] * acc
                    gout_out[l, rows, cols] = INM[l, rows, cols] * acc
                    gdec_out[l, rows, cols] = -SBG[l, slot, NL : 2 * NL, :]
                    part = SBG[l, slot, 2 * NL : 2 * NL + 8, :]
                    vec = part if vec is None else vec + part
                gskip_out[l : l + 1, cols] = vec[0:1]
                go2_out[l : l + 1, cols] = vec[1:2]
                gstep_out[l : l + 1, cols] = vec[2:3]
                ggain_out[l : l + 1, cols] = vec[3:4]
            base = 2 * NL + 8
            for q in range(CB):
                gbias_out[l : l + 1, q * LANES : (q + 1) * LANES] = SBG[l, 0, base + q : base + q + 1, :]
            sq = jnp.sum(SBG[l, 0, base + CB : base + CB + 8, :], axis=1, keepdims=True)
            count = sq[3:4] * (1.0 / LANES)
            root = jnp.sqrt(sq[0:3] / (count * D))
            col = lax.broadcasted_iota(jnp.int32, (1, 3), 1)
            stats_out[l : l + 1, :] = jnp.where(col == 0, root[0:1], jnp.where(col == 1, root[1:2], root[2:3]))

        def tick(self):
            if self.todo:
                self.todo.pop(0)()

    def norm_backward(l, gsrc, gdst):
        for d in range(1, S):
            j = me ^ d
            seq_wait(l, 3, j, GX.at[pl.ds(0, TL)], GXR.at[l, j])

        def step(i, _):
            rows = pl.ds(pl.multiple_of(i * CHUNK, CHUNK), CHUNK)
            inv = RSTD[l, rows, :]
            gx, xh = [], []
            s1 = s2 = None
            for g in range(CG):
                v = GXR[l, g * NSP, rows, :]
                for h in range(1, NSP):
                    v = v + GXR[l, g * NSP + h, rows, :]
                x = XS[l, g, rows, :]
                gx.append(v)
                xh.append(x)
                s1 = v if s1 is None else s1 + v
                s2 = v * x if s2 is None else s2 + v * x
            m1 = jnp.sum(s1, axis=-1, keepdims=True) * (1.0 / D)
            m2 = jnp.sum(s2, axis=-1, keepdims=True) * (1.0 / D)
            for g in range(CG):
                cols = slice(g * LANES, (g + 1) * LANES)
                gdst[rows, cols] = gsrc[rows, cols] + inv * (gx[g] - m1 - xh[g] * m2)
            return 0

        lax.fori_loop(0, TL // CHUNK, step, 0)

    norm_forward(0, x_ref)
    pl.semaphore_wait(barrier, len(partners))
    send_normed(0)
    for c in loads:
        c.wait()
    nrows = pl.ds(pl.multiple_of(n0, 8), NL)
    for l in range(L):
        NA[l] = DEC[l, nrows, clane] * (-LOG2E)
        WT[l] = INM[l, nrows, clane] * OUTM[l, nrows, clane]
    streams = [x_ref] + [STR.at[l] for l in range(L - 1)] + [y_out]
    for l in range(L):
        if l:
            norm_forward(l, streams[l])
            send_normed(l)
        sent = scan_forward(l)
        glu_forward(l, streams[l], streams[l + 1])
        for done in sent:
            done()

    grads = [gx_out] + [GRD.at[l] for l in range(L - 1)] + [ct_ref]
    reduces = []
    smalls = []
    for l in range(L - 1, -1, -1):
        glu_backward(l, grads[l + 1])
        weight_grad(l)
        mine = Reduce(l)
        mine.tick()
        reduces.append(mine)

        def some():
            for r in reduces + smalls:
                r.tick()

        ticks = {}
        if S >= 4:
            ticks = {S // 4 - 1: some, S // 2 - 1: some, 3 * S // 4 - 1: some}
        sent = scan_backward(l, ticks)
        small = Small(l)
        small.tick()
        smalls.append(small)
        some()
        norm_backward(l, grads[l + 1], grads[l])
        for done in sent:
            done()
    while any(r.todo for r in reduces + smalls):
        for r in reduces + smalls:
            r.tick()
    for done in pending:
        done()


def hand_on(n, *refs):
    ins, outs, held, sem_in, sem_out = refs[:n], refs[n : 2 * n], refs[2 * n : 3 * n], refs[-2], refs[-1]
    parts = []
    for a, o, h in zip(ins, outs, held):
        if len(a.shape) == 3:
            parts += [(a.at[l], h.at[l], o.at[l]) for l in range(a.shape[0])]
        else:
            parts.append((a, h, o))
    parts.sort(key=lambda p: math.prod(p[0].shape))
    for i, (a, h, _) in enumerate(parts):
        pltpu.make_async_copy(a, h, sem_in.at[i]).start()
    for i, (a, h, o) in enumerate(parts):
        pltpu.make_async_copy(a, h, sem_in.at[i]).wait()
        pltpu.make_async_copy(h, o, sem_out.at[i]).start()
    for i, (_, h, o) in enumerate(parts):
        pltpu.make_async_copy(h, o, sem_out.at[i]).wait()


def per_device(
    stream_in, cotangent, lengths, norm_gain, decay_rate, in_map, out_map, skip_gain, order_two, step_gain, glu_weight, glu_bias
):
    S, B = lax.axis_size("seq"), lax.axis_size("batch")
    _, TL, D = stream_in.shape
    L, NS = decay_rate.shape[:2]
    UN = math.gcd(TL, 16)
    CG, E2 = D // LANES, 2 * D
    NL = NS // (S // CG)
    TA = S * TL
    CB = E2 // LANES
    GROWS = D * CB
    SBR = 2 * NL + 8 + EXTRA
    NB, NST = len(bits_of(B)), len(bits_of(B)) + len(bits_of(S))
    shape = jax.ShapeDtypeStruct
    vmem = pl.BlockSpec(memory_space=pltpu.VMEM)
    smem = pl.BlockSpec(memory_space=pltpu.SMEM)
    hbm = pl.BlockSpec(memory_space=pl.ANY)
    buf = pltpu.VMEM
    dma = pltpu.SemaphoreType.DMA
    outs = pl.pallas_call(
        functools.partial(kernel, (S, B, TL, D, NS, L, UN)),
        out_shape=[
            shape((TL, D), F32), shape((TL, D), F32), shape((L, D), F32),
            shape((L, NS, D), F32), shape((L, NS, D), F32), shape((L, NS, D), F32),
            shape((L, D), F32), shape((L, D), F32), shape((L, D), F32),
            shape((L, D, E2), F32), shape((L, E2), F32), shape((L, 3), F32),
        ],
        in_specs=[vmem, vmem, smem, vmem, hbm, hbm, hbm, vmem, vmem, vmem, hbm, vmem],
        out_specs=[vmem] * 9 + [hbm, vmem, vmem],
        scratch_shapes=[
            buf((L, D, E2), BF16), buf((L, NS, D), F32), buf((L, NS, D), F32), buf((L, NS, D), F32),
            buf((L, NL, LANES), F32), buf((L, NL, LANES), F32),
            buf((L, CG, TL, LANES), F32), buf((L, TA, LANES), F32), buf((L, TL, LANES), F32),
            buf((L, TA, LANES), F32), buf((TA, LANES), F32),
            buf((L, S, TL, LANES), F32), buf((L, CG, TL + EXTRA, LANES), F32), buf((L, S, TL + EXTRA, LANES), F32),
            buf((L, S, TL, LANES), F32),
            buf((L, TA + 1, NL, LANES), F32), buf((TL * 8, LANES), F32), buf((max(TL * 8, TA), LANES), F32),
            buf((L, TL, D), BF16), buf((L, TL, E2), F32), buf((TL, E2), BF16), buf((TL, D), F32),
            buf((L - 1, TL, D), F32), buf((L - 1, TL, D), F32), buf((L, 4, 8, LANES), F32),
            buf((L, GROWS, LANES), F32), buf((L, 2, GROWS // 2, LANES), F32), buf((L, GROWS, LANES), F32),
            buf((L, NB + 1, SBR, LANES), F32), buf((L, NB, SBR, LANES), F32), buf((L, S, SBR, LANES), F32),
            buf((4, 8, LANES), F32),
            dma((4,)), dma((L * 4, S)), dma((L * 4, S)), dma((L * 4, NST)), dma((L * 4, NST)),
            dma((L, NB)), dma((L, NB)), dma((L, S)), dma((L, S)), dma((L, CB)),
        ],
        compiler_params=pltpu.CompilerParams(
            collective_id=0, has_side_effects=True, vmem_limit_bytes=61 * 2**20
        ),
        name="liquid_layers",
    )(
        stream_in[0], cotangent[0], lengths, norm_gain, decay_rate, in_map, out_map,
        skip_gain, order_two, step_gain, glu_weight, glu_bias,
    )
    outs = pl.pallas_call(
        functools.partial(hand_on, len(outs)),
        out_shape=[shape(o.shape, o.dtype) for o in outs],
        in_specs=[hbm] * len(outs),
        out_specs=[hbm] * len(outs),
        scratch_shapes=[buf(o.shape, o.dtype) for o in outs] + [dma((2 * len(outs),)), dma((2 * len(outs),))],
        compiler_params=pltpu.CompilerParams(vmem_limit_bytes=61 * 2**20),
        name="results",
    )(*outs)
    return (outs[0][None], outs[1][None], *outs[2:])


def solution(mesh):
    split = P("batch", "seq", None)
    in_specs = (split, split, P("batch")) + (P(),) * 9
    out_specs = (split, split) + (P(),) * 10
    return jax.shard_map(per_device, mesh=mesh, in_specs=in_specs, out_specs=out_specs, check_vma=False)
```

```python
import functools
import math

import jax
import jax.numpy as jnp
from jax import lax
from jax.experimental import pallas as pl
from jax.experimental.pallas import tpu as pltpu
from jax.sharding import PartitionSpec as P

MESH = pl.DeviceIdType.MESH
EPSILON = 1e-05
LOG2E = 1.4426950408889634
LN2 = 0.6931471805599453
GELU_K = math.sqrt(2.0 / math.pi)
F32 = jnp.float32
BF16 = jnp.bfloat16
LANES = 128
CHUNK = 32
CHAINS = 6
UROWS = 256
EXTRA = 16


def rows8(v):
    return v.reshape(v.shape[0] // 8, 8, v.shape[1]).sum(0)


def sigmoid(v):
    return 1.0 / (1.0 + jnp.exp(-v))


def gelu_parts(m):
    th = jnp.tanh(GELU_K * (m + 0.044715 * m * m * m))
    return th


def bits_of(n):
    return [i for i in range(n.bit_length() - 1)]


def orders(seq, batch, chains):
    s = [("seq", b) for b in bits_of(seq)]
    b = [("batch", b) for b in bits_of(batch)]
    near = s[1:2] + b[:2]
    rest = b[2:] + s[2:]
    plans = []
    for c in range(chains):
        turn = c % len(near)
        plans.append(s[:1] + near[turn:] + near[:turn] + rest)
    return plans


def chain_rows(rows, devices, most):
    unit = 8 * devices
    units = rows // unit
    chains = min(most, units)
    cut = [units // chains + (1 if c < units % chains else 0) for c in range(chains)]
    return [(sum(cut[:c]) * unit, cut[c] * unit) for c in range(chains)]


def kernel(cfg, *refs):
    S, B, TL, D, NS, L, UN = cfg
    CG = D // LANES
    NSP = S // CG
    NL = NS // NSP
    E2 = 2 * D
    CB = E2 // LANES
    GROWS = D * CB
    SB_ROWS = 2 * NL + 24
    spans = chain_rows(GROWS, S * B, CHAINS)
    plans = orders(S, B, len(spans))
    (
        x_ref, ct_ref, len_ref, gain_ref, dec_hbm, in_hbm, out_hbm, skip_ref, o2_ref, step_ref, w_hbm, bias_ref,
        y_out, gx_out, ggain_out, gdec_out, gin_out, gout_out, gskip_out, go2_out, gstep_out, gw_hbm, gbias_out, stats_out,
        W, DEC, INM, OUTM, NA, WT,
        XS, XR, RSTD, R, Y, YR, GS, GMR, GXR,
        SIG, P1, P2, LA, PJ, LG, GA, STR, GRD, ST,
        FB, RB, FG, SBW, SBR, SBG, VEC,
        load_sem, send_sem, recv_sem, ar_ssem, ar_rsem, sb_ssem, sb_rsem, sg_ssem, sg_rsem, out_sem,
    ) = refs
    U, GX = P2, Y
    me = lax.axis_index("seq")
    bi = lax.axis_index("batch")
    cg = me // NSP
    nh = lax.rem(me, NSP)
    n0 = nh * NL
    first_part = (nh == 0).astype(F32)
    clane = pl.ds(pl.multiple_of(cg * LANES, LANES), LANES)

    loads = [
        pltpu.make_async_copy(w_hbm, W, load_sem.at[0]),
        pltpu.make_async_copy(dec_hbm, DEC, load_sem.at[1]),
        pltpu.make_async_copy(in_hbm, INM, load_sem.at[2]),
        pltpu.make_async_copy(out_hbm, OUTM, load_sem.at[3]),
    ]
    for c in loads:
        c.start()

    barrier = pltpu.get_barrier_semaphore()
    partners = [(me ^ d, bi) for d in range(1, S)] + [(me, bi ^ (1 << b)) for b in bits_of(B)]
    for p in partners:
        pl.semaphore_signal(barrier, inc=1, device_id=p, device_id_type=MESH)

    pending = []

    def seq_copy(l, ph, j, src, dst):
        return pltpu.make_async_remote_copy(
            src_ref=src,
            dst_ref=dst,
            send_sem=send_sem.at[l * 4 + ph, j],
            recv_sem=recv_sem.at[l * 4 + ph, me],
            device_id=(j, bi),
            device_id_type=MESH,
        )

    def seq_wait(l, ph, k, src, dst):
        pltpu.make_async_remote_copy(
            src_ref=src,
            dst_ref=dst,
            send_sem=send_sem.at[l * 4 + ph, k],
            recv_sem=recv_sem.at[l * 4 + ph, k],
            device_id=(k, bi),
            device_id_type=MESH,
        ).wait_recv()

    def tblock(k):
        return pl.ds(pl.multiple_of(k * TL, TL), TL)

    def swap(axis, bit):
        return (me ^ (1 << bit), bi) if axis == "seq" else (me, bi ^ (1 << bit))

    def my_bit(axis, bit):
        return lax.rem((me if axis == "seq" else bi) // (1 << bit), 2)

    class Reduce:
        def __init__(self, l):
            self.l = l
            self.chains = []
            for (base, rows), plan in zip(spans, plans):
                off, size, roff, stages = base, rows, base, []
                for i, (axis, bit) in enumerate(plan):
                    half = size // 2
                    mine = my_bit(axis, bit)
                    keep = pl.multiple_of(off + mine * half, 8)
                    give = pl.multiple_of(off + (1 - mine) * half, 8)
                    stages.append((i, axis, bit, half, keep, give, roff))
                    off, size, roff = keep, half, roff + half
                self.chains.append(stages)
            self.n = n = len(plans[0])
            self.todo = [self.begin]
            self.todo += [functools.partial(self.reduce_step, i) for i in range(n)]
            self.todo += [functools.partial(self.gather_step, i) for i in range(n - 1, -1, -1)]

        def rs(self, c, stage):
            i, axis, bit, half, keep, give, roff = stage
            return pltpu.make_async_remote_copy(
                src_ref=FB.at[self.l, pl.ds(give, half)],
                dst_ref=RB.at[self.l, pl.ds(roff, half)],
                send_sem=ar_ssem.at[self.l, c, i],
                recv_sem=ar_rsem.at[self.l, c, i],
                device_id=swap(axis, bit),
                device_id_type=MESH,
            )

        def ag(self, c, stage):
            i, axis, bit, half, keep, give, roff = stage
            return pltpu.make_async_remote_copy(
                src_ref=FG.at[self.l, pl.ds(keep, half)],
                dst_ref=FG.at[self.l, pl.ds(keep, half)],
                send_sem=ar_ssem.at[self.l, c, self.n + i],
                recv_sem=ar_rsem.at[self.l, c, self.n + i],
                device_id=swap(axis, bit),
                device_id_type=MESH,
            )

        def begin(self):
            for c, stages in enumerate(self.chains):
                self.rs(c, stages[0]).start()

        def reduce_step(self, i):
            for c, stages in enumerate(self.chains):
                _, _, _, half, keep, _, roff = stages[i]
                self.rs(c, stages[i]).wait()
                step = math.gcd(half, 64)
                total = FB if i + 1 < self.n else FG

                def add(j, _, keep=keep, roff=roff, step=step, total=total):
                    at = pl.ds(pl.multiple_of(keep + j * step, 8), step)
                    total[self.l, at, :] = FB[self.l, at, :] + RB[self.l, pl.ds(pl.multiple_of(roff + j * step, 8), step), :]
                    return 0

                lax.fori_loop(0, half // step, add, 0)
                if i + 1 < self.n:
                    self.rs(c, stages[i + 1]).start()
                else:
                    self.ag(c, stages[i]).start()

        def gather_step(self, i):
            for c, stages in enumerate(self.chains):
                self.ag(c, stages[i]).wait()
                if i > 0:
                    self.ag(c, stages[i - 1]).start()
                else:
                    base, rows = spans[c]
                    for u in range(base // UROWS, (base + rows) // UROWS):
                        cb, r = divmod(u * UROWS, D)
                        copy = pltpu.make_async_copy(
                            FG.at[self.l, pl.ds(u * UROWS, UROWS)],
                            gw_hbm.at[self.l, pl.ds(r, UROWS), pl.ds(cb * LANES, LANES)],
                            out_sem.at[self.l, u],
                        )
                        copy.start()
                        pending.append(copy.wait)

        def tick(self):
            if self.todo:
                self.todo.pop(0)()

    def norm_forward(l, src):
        def step(i, _):
            rows = pl.ds(pl.multiple_of(i * CHUNK, CHUNK), CHUNK)
            x = src[rows, :]
            center = x - jnp.mean(x, axis=-1, keepdims=True)
            spread = jnp.mean(center * center, axis=-1, keepdims=True)
            inv = lax.rsqrt(spread + EPSILON)
            xhat = center * inv
            RSTD[l, rows, :] = jnp.broadcast_to(inv, (CHUNK, LANES))
            for g in range(CG):
                XS[l, g, rows, :] = xhat[:, g * LANES : (g + 1) * LANES]
            return 0

        lax.fori_loop(0, TL // CHUNK, step, 0)

    def send_normed(l):
        for d in range(1, S):
            j = me ^ d
            copy = seq_copy(l, 0, j, XS.at[l, j // NSP], XR.at[l, tblock(me)])
            copy.start()
            pending.append(copy.wait_send)
        XR[l, tblock(me), :] = XS[l, cg]

    def scan_forward(l):
        gain = gain_ref[l : l + 1, clane]
        o2 = o2_ref[l : l + 1, clane]
        stp = step_ref[l : l + 1, clane]
        skip = skip_ref[l : l + 1, clane] * first_part
        first_row = lax.broadcasted_iota(jnp.int32, (TL, LANES), 0) == 0
        SIG[l, 0] = jnp.zeros((NL, LANES), F32)

        def block(k, carry):
            sig, last = carry

            @pl.when(k != me)
            def _():
                seq_wait(l, 0, k, XS.at[l, 0], XR.at[l, tblock(k)])

            normed = XR[l, tblock(k), :] * gain
            prev = jnp.where(first_row, last, pltpu.roll(normed, 1, 0))
            U[tblock(k), :] = normed + o2 * normed * prev
            z = stp * normed
            R[l, tblock(k), :] = jnp.maximum(z, 0.0) + jnp.log1p(jnp.exp(-jnp.abs(z)))
            na, wt = NA[l], WT[l]

            def inner(i, sig):
                for s in range(UN):
                    t = i * UN + s
                    at = pl.ds(k * TL + t, 1)
                    sig = jnp.exp2(na * R[l, at, :]) * sig + U[at, :]
                    SIG[l, k * TL + t + 1] = sig
                    P1[pl.ds(pl.multiple_of(t * 8, 8), 8), :] = rows8(wt * sig)
                return sig

            sig = lax.fori_loop(0, TL // UN, inner, sig)

            def finish(j, _):
                total = P1[pl.ds(j * 64, 8, stride=8), :]
                for s in range(1, 8):
                    total = total + P1[pl.ds(j * 64 + s, 8, stride=8), :]
                at = pl.ds(pl.multiple_of(k * TL + j * 8, 8), 8)
                Y[at, :] = total + skip * U[at, :]
                return 0

            lax.fori_loop(0, TL // 8, finish, 0)

            @pl.when(k == me)
            def _():
                YR[l, me] = Y[tblock(k), :]

            @pl.when(k != me)
            def _():
                seq_copy(l, 1, k, Y.at[tblock(k)], YR.at[l, me]).start()

            return sig, normed[TL - 1 : TL, :]

        lax.fori_loop(0, S, block, (jnp.zeros((NL, LANES), F32), jnp.zeros((1, LANES), F32)))
        return [seq_copy(l, 1, me ^ d, Y.at[tblock(me ^ d)], YR.at[l, me]).wait_send for d in range(1, S)]

    def mixed_of(l, g, rows):
        m = YR[l, g * NSP, rows, :]
        for h in range(1, NSP):
            m = m + YR[l, g * NSP + h, rows, :]
        return m

    def valid_of(i):
        pos = me * TL + i * CHUNK + lax.broadcasted_iota(jnp.int32, (CHUNK, 1), 0)
        return (pos < len_ref[0]).astype(F32)

    def glu_forward(l, src, dst):
        for d in range(1, S):
            j = me ^ d
            seq_wait(l, 1, j, Y.at[pl.ds(0, TL)], YR.at[l, j])

        def act(i, sq):
            rows = pl.ds(pl.multiple_of(i * CHUNK, CHUNK), CHUNK)
            valid = valid_of(i)
            for g in range(CG):
                m = mixed_of(l, g, rows)
                a = 0.5 * m * (1.0 + gelu_parts(m))
                LA[l, rows, g * LANES : (g + 1) * LANES] = a.astype(BF16)
                sq = sq + rows8(a * a * valid)
            return sq

        zero = jnp.zeros((8, LANES), F32)
        sq_act = lax.fori_loop(0, TL // CHUNK, act, zero)
        PJ[l] = jnp.dot(LA[l], W[l], preferred_element_type=F32) + bias_ref[l : l + 1, :]

        def gate(i, sq):
            sq_b, sq_s, cnt = sq
            rows = pl.ds(pl.multiple_of(i * CHUNK, CHUNK), CHUNK)
            valid = valid_of(i)
            for g in range(CG):
                cols = slice(g * LANES, (g + 1) * LANES)
                gcols = slice(D + g * LANES, D + (g + 1) * LANES)
                branch = PJ[l, rows, cols] * sigmoid(PJ[l, rows, gcols]) * valid
                out = src[rows, cols] + branch
                dst[rows, cols] = out
                sq_b = sq_b + rows8(branch * branch)
                sq_s = sq_s + rows8(out * out * valid)
            cnt = cnt + rows8(jnp.broadcast_to(valid, (CHUNK, LANES)))
            return sq_b, sq_s, cnt

        sq_b, sq_s, cnt = lax.fori_loop(0, TL // CHUNK, gate, (zero, zero, zero))
        for k, v in enumerate((sq_act, sq_b, sq_s, cnt)):
            ST[l, k] = v

    def glu_backward(l, gsrc):
        def gate(i, acc):
            rows = pl.ds(pl.multiple_of(i * CHUNK, CHUNK), CHUNK)
            valid = valid_of(i)
            out = []
            for g in range(CG):
                cols = slice(g * LANES, (g + 1) * LANES)
                gcols = slice(D + g * LANES, D + (g + 1) * LANES)
                gb = gsrc[rows, cols] * valid
                s = sigmoid(PJ[l, rows, gcols])
                one = gb * s
                two = one * PJ[l, rows, cols] * (1.0 - s)
                LG[rows, cols] = one.astype(BF16)
                LG[rows, gcols] = two.astype(BF16)
                out.append((rows8(one), rows8(two)))
            return tuple(a + b for a, b in zip(acc, [o[0] for o in out] + [o[1] for o in out]))

        zero = jnp.zeros((8, LANES), F32)
        bias = lax.fori_loop(0, TL // CHUNK, gate, (zero,) * CB)
        GA[...] = lax.dot_general(LG[...], W[l], (((1,), (1,)), ((), ())), preferred_element_type=F32)

        def act(i, _):
            rows = pl.ds(pl.multiple_of(i * CHUNK, CHUNK), CHUNK)
            for g in range(CG):
                m = mixed_of(l, g, rows)
                th = gelu_parts(m)
                slope = 0.5 * (1.0 + th) + 0.5 * m * (1.0 - th * th) * GELU_K * (1.0 + 3 * 0.044715 * m * m)
                GS[l, g, rows, :] = GA[rows, g * LANES : (g + 1) * LANES] * slope
            return 0

        lax.fori_loop(0, TL // CHUNK, act, 0)
        extra = [jnp.sum(b, axis=0, keepdims=True) for b in bias]
        extra += [jnp.sum(ST[l, k], axis=0, keepdims=True) for k in range(4)]
        extra += [jnp.zeros((EXTRA - len(extra), LANES), F32)]
        extra = jnp.concatenate(extra, axis=0)
        for g in range(CG):
            GS[l, g, TL : TL + EXTRA, :] = extra
        for d in range(1, S):
            j = me ^ d
            copy = seq_copy(l, 2, j, GS.at[l, j // NSP], GMR.at[l, me])
            copy.start()
            pending.append(copy.wait_send)
        GMR[l, me] = GS[l, cg]

    def weight_grad(l):
        for c in range(2):
            half = lax.dot_general(
                LA[l], LG[:, c * D : (c + 1) * D], (((0,), (0,)), ((), ())), preferred_element_type=F32
            )
            for q in range(CB // 2):
                FB[l, pl.ds((c * (CB // 2) + q) * D, D), :] = half[:, q * LANES : (q + 1) * LANES]

    def scan_backward(l, ticks):
        gain = gain_ref[l : l + 1, clane]
        o2 = o2_ref[l : l + 1, clane]
        stp = step_ref[l : l + 1, clane]
        skip = skip_ref[l : l + 1, clane]
        row_id = lax.broadcasted_iota(jnp.int32, (TL, LANES), 0)
        zero8 = jnp.zeros((8, LANES), F32)
        zeros = jnp.zeros((NL, LANES), F32)
        for v in range(4):
            VEC[v] = zero8

        def block(kk, carry):
            nu, acc, gdc, after = carry
            k = S - 1 - kk

            @pl.when(k != me)
            def _():
                seq_wait(l, 2, k, GS.at[l, 0], GMR.at[l, k])

            na, wt = NA[l], WT[l]

            def inner(ii, c):
                nu, acc, gdc = c
                i = TL // UN - 1 - ii
                for s in range(UN - 1, -1, -1):
                    t = i * UN + s
                    rate = R[l, pl.ds(k * TL + t, 1), :]
                    gm = GMR[l, k, pl.ds(t, 1), :]
                    mu = wt * gm + nu
                    acc = acc + gm * SIG[l, k * TL + t + 1]
                    at = pl.ds(pl.multiple_of(t * 8, 8), 8)
                    P1[at, :] = rows8(mu)
                    nu = jnp.exp2(na * rate) * mu
                    q = nu * SIG[l, k * TL + t]
                    gdc = gdc + q * rate
                    P2[at, :] = rows8(na * q)
                return nu, acc, gdc

            nu, acc, gdc = lax.fori_loop(0, TL // UN, inner, (nu, acc, gdc))

            def finish(j, _):
                one = P1[pl.ds(j * 64, 8, stride=8), :]
                two = P2[pl.ds(j * 64, 8, stride=8), :]
                for s in range(1, 8):
                    one = one + P1[pl.ds(j * 64 + s, 8, stride=8), :]
                    two = two + P2[pl.ds(j * 64 + s, 8, stride=8), :]
                at = pl.ds(pl.multiple_of(j * 8, 8), 8)
                GX[pl.ds(pl.multiple_of(k * TL + j * 8, 8), 8), :] = one
                GA[at, 0:LANES] = two
                return 0

            lax.fori_loop(0, TL // 8, finish, 0)
            xhat = XR[l, tblock(k), :]
            normed = xhat * gain
            before = XR[l, pl.ds(jnp.maximum(k * TL - 1, 0), 1), :] * gain
            before = jnp.where(k == 0, 0.0, before)
            prev = jnp.where(row_id == 0, before, pltpu.roll(normed, 1, 0))
            gm = GMR[l, k, 0:TL, :] * first_part
            gdrv = GX[tblock(k), :] + skip * gm
            grate = GA[0:TL, 0:LANES] * LN2
            both = gdrv * normed
            h = o2 * both
            later = jnp.where(row_id == TL - 1, after, pltpu.roll(h, TL - 1, 0))
            slope = sigmoid(stp * normed) * grate
            gnormed = gdrv * (1.0 + o2 * prev) + later + slope * stp
            GX[tblock(k), :] = gnormed * gain
            VEC[0] = VEC[0] + rows8(gm * (normed + o2 * normed * prev))
            VEC[1] = VEC[1] + rows8(both * prev)
            VEC[2] = VEC[2] + rows8(slope * normed)
            VEC[3] = VEC[3] + rows8(gnormed * xhat)

            @pl.when(k == me)
            def _():
                GXR[l, me] = GX[tblock(k), :]

            @pl.when(k != me)
            def _():
                seq_copy(l, 3, k, GX.at[tblock(k)], GXR.at[l, me]).start()

            for at, todo in ticks.items():

                @pl.when(kk == at)
                def _(todo=todo):
                    for t in todo:
                        t.tick()

            return nu, acc, gdc, h[0:1, :]

        carry = (zeros, zeros, zeros, jnp.zeros((1, LANES), F32))
        _, acc, gdc, _ = lax.fori_loop(0, S, block, carry)
        sent = [seq_copy(l, 3, me ^ d, GX.at[tblock(me ^ d)], GXR.at[l, me]).wait_send for d in range(1, S)]
        SBW[l, 0, 0:NL, :] = acc
        SBW[l, 0, NL : 2 * NL, :] = gdc
        vec = [jnp.sum(VEC[v], axis=0, keepdims=True) for v in range(4)]
        vec += [jnp.zeros((4, LANES), F32)]
        SBW[l, 0, 2 * NL : 2 * NL + 8, :] = jnp.concatenate(vec, axis=0)
        extra = GMR[l, 0, TL : TL + EXTRA, :]
        for k in range(1, S):
            extra = extra + GMR[l, k, TL : TL + EXTRA, :]
        SBW[l, 0, 2 * NL + 8 : 2 * NL + 8 + EXTRA, :] = extra
        return sent

    class Small:
        def __init__(self, l):
            self.l = l
            nb = len(bits_of(B))
            self.todo = [functools.partial(self.start, 0)]
            self.todo += [functools.partial(self.join, i) for i in range(nb)]
            self.todo += [self.gathered]
            self.nb = nb

        def copy(self, i):
            return pltpu.make_async_remote_copy(
                src_ref=SBW.at[self.l, i],
                dst_ref=SBR.at[self.l, i],
                send_sem=sb_ssem.at[self.l, i],
                recv_sem=sb_rsem.at[self.l, i],
                device_id=(me, bi ^ (1 << i)),
                device_id_type=MESH,
            )

        def seq(self, j, slot, rslot):
            return pltpu.make_async_remote_copy(
                src_ref=SBW.at[self.l, self.nb],
                dst_ref=SBG.at[self.l, slot],
                send_sem=sg_ssem.at[self.l, j],
                recv_sem=sg_rsem.at[self.l, rslot],
                device_id=(j, bi),
                device_id_type=MESH,
            )

        def start(self, i):
            self.copy(i).start()

        def join(self, i):
            self.copy(i).wait()
            SBW[self.l, i + 1] = SBW[self.l, i] + SBR[self.l, i]
            if i + 1 < self.nb:
                self.start(i + 1)
            else:
                for d in range(1, S):
                    self.seq(me ^ d, me, me).start()
                SBG[self.l, me] = SBW[self.l, self.nb]

        def gathered(self):
            for d in range(1, S):
                self.seq(me ^ d, me ^ d, me ^ d).wait()
            l = self.l
            for g in range(CG):
                cols = slice(g * LANES, (g + 1) * LANES)
                vec = None
                for h in range(NSP):
                    slot = g * NSP + h
                    rows = slice(h * NL, (h + 1) * NL)
                    acc = SBG[l, slot, 0:NL, :]
                    gin_out[l, rows, cols] = OUTM[l, rows, cols] * acc
                    gout_out[l, rows, cols] = INM[l, rows, cols] * acc
                    gdec_out[l, rows, cols] = -SBG[l, slot, NL : 2 * NL, :]
                    part = SBG[l, slot, 2 * NL : 2 * NL + 8, :]
                    vec = part if vec is None else vec + part
                gskip_out[l : l + 1, cols] = vec[0:1]
                go2_out[l : l + 1, cols] = vec[1:2]
                gstep_out[l : l + 1, cols] = vec[2:3]
                ggain_out[l : l + 1, cols] = vec[3:4]
            base = 2 * NL + 8
            for q in range(CB):
                gbias_out[l : l + 1, q * LANES : (q + 1) * LANES] = SBG[l, 0, base + q : base + q + 1, :]
            sq = jnp.sum(SBG[l, 0, base + CB : base + CB + 8, :], axis=1, keepdims=True)
            count = sq[3:4] * (1.0 / LANES)
            root = jnp.sqrt(sq[0:3] / (count * D))
            col = lax.broadcasted_iota(jnp.int32, (1, 3), 1)
            stats_out[l : l + 1, :] = jnp.where(col == 0, root[0:1], jnp.where(col == 1, root[1:2], root[2:3]))

        def tick(self):
            if self.todo:
                self.todo.pop(0)()

    def norm_backward(l, gsrc, gdst):
        for d in range(1, S):
            j = me ^ d
            seq_wait(l, 3, j, GX.at[pl.ds(0, TL)], GXR.at[l, j])

        def step(i, _):
            rows = pl.ds(pl.multiple_of(i * CHUNK, CHUNK), CHUNK)
            inv = RSTD[l, rows, :]
            gx, xh = [], []
            s1 = s2 = None
            for g in range(CG):
                v = GXR[l, g * NSP, rows, :]
                for h in range(1, NSP):
                    v = v + GXR[l, g * NSP + h, rows, :]
                x = XS[l, g, rows, :]
                gx.append(v)
                xh.append(x)
                s1 = v if s1 is None else s1 + v
                s2 = v * x if s2 is None else s2 + v * x
            m1 = jnp.sum(s1, axis=-1, keepdims=True) * (1.0 / D)
            m2 = jnp.sum(s2, axis=-1, keepdims=True) * (1.0 / D)
            for g in range(CG):
                cols = slice(g * LANES, (g + 1) * LANES)
                gdst[rows, cols] = gsrc[rows, cols] + inv * (gx[g] - m1 - xh[g] * m2)
            return 0

        lax.fori_loop(0, TL // CHUNK, step, 0)

    norm_forward(0, x_ref)
    pl.semaphore_wait(barrier, len(partners))
    send_normed(0)
    for c in loads:
        c.wait()
    nrows = pl.ds(pl.multiple_of(n0, 8), NL)
    for l in range(L):
        NA[l] = DEC[l, nrows, clane] * (-LOG2E)
        WT[l] = INM[l, nrows, clane] * OUTM[l, nrows, clane]
    streams = [x_ref] + [STR.at[l] for l in range(L - 1)] + [y_out]
    for l in range(L):
        if l:
            norm_forward(l, streams[l])
            send_normed(l)
        sent = scan_forward(l)
        glu_forward(l, streams[l], streams[l + 1])
        for done in sent:
            done()

    grads = [gx_out] + [GRD.at[l] for l in range(L - 1)] + [ct_ref]
    def at_blocks(plan):
        return {(q + 1) * S // 4 - 1: todo for q, todo in enumerate(plan) if todo}

    older = []
    for l in range(L - 1, -1, -1):
        run = lambda things: [t.tick() for t in things]
        glu_backward(l, grads[l + 1])
        run(older)
        weight_grad(l)
        big, small = Reduce(l), Small(l)
        big.tick()
        sent = scan_backward(l, at_blocks([older, [big] + older[1:], older, [big] + older[1:]]))
        small.tick()
        norm_backward(l, grads[l + 1], grads[l])
        for done in sent:
            done()
        run([small, big] + older)
        older = [big, small] + older
    while any(t.todo for t in older):
        for t in older:
            t.tick()
    for done in pending:
        done()


def hand_on(n, *refs):
    ins, outs, held, sem_in, sem_out = refs[:n], refs[n : 2 * n], refs[2 * n : 3 * n], refs[-2], refs[-1]
    parts = []
    for a, o, h in zip(ins, outs, held):
        if len(a.shape) == 3:
            parts += [(a.at[l], h.at[l], o.at[l]) for l in range(a.shape[0])]
        else:
            parts.append((a, h, o))
    parts.sort(key=lambda p: math.prod(p[0].shape))
    for i, (a, h, _) in enumerate(parts):
        pltpu.make_async_copy(a, h, sem_in.at[i]).start()
    for i, (a, h, o) in enumerate(parts):
        pltpu.make_async_copy(a, h, sem_in.at[i]).wait()
        pltpu.make_async_copy(h, o, sem_out.at[i]).start()
    for i, (_, h, o) in enumerate(parts):
        pltpu.make_async_copy(h, o, sem_out.at[i]).wait()


def per_device(
    stream_in, cotangent, lengths, norm_gain, decay_rate, in_map, out_map, skip_gain, order_two, step_gain, glu_weight, glu_bias
):
    S, B = lax.axis_size("seq"), lax.axis_size("batch")
    _, TL, D = stream_in.shape
    L, NS = decay_rate.shape[:2]
    UN = math.gcd(TL, 16)
    CG, E2 = D // LANES, 2 * D
    NL = NS // (S // CG)
    TA = S * TL
    CB = E2 // LANES
    GROWS = D * CB
    SBR = 2 * NL + 8 + EXTRA
    NB, NST = len(bits_of(B)), len(bits_of(B)) + len(bits_of(S))
    shape = jax.ShapeDtypeStruct
    vmem = pl.BlockSpec(memory_space=pltpu.VMEM)
    smem = pl.BlockSpec(memory_space=pltpu.SMEM)
    hbm = pl.BlockSpec(memory_space=pl.ANY)
    buf = pltpu.VMEM
    dma = pltpu.SemaphoreType.DMA
    outs = pl.pallas_call(
        functools.partial(kernel, (S, B, TL, D, NS, L, UN)),
        out_shape=[
            shape((TL, D), F32), shape((TL, D), F32), shape((L, D), F32),
            shape((L, NS, D), F32), shape((L, NS, D), F32), shape((L, NS, D), F32),
            shape((L, D), F32), shape((L, D), F32), shape((L, D), F32),
            shape((L, D, E2), F32), shape((L, E2), F32), shape((L, 3), F32),
        ],
        in_specs=[vmem, vmem, smem, vmem, hbm, hbm, hbm, vmem, vmem, vmem, hbm, vmem],
        out_specs=[vmem] * 9 + [hbm, vmem, vmem],
        scratch_shapes=[
            buf((L, D, E2), BF16), buf((L, NS, D), F32), buf((L, NS, D), F32), buf((L, NS, D), F32),
            buf((L, NL, LANES), F32), buf((L, NL, LANES), F32),
            buf((L, CG, TL, LANES), F32), buf((L, TA, LANES), F32), buf((L, TL, LANES), F32),
            buf((L, TA, LANES), F32), buf((TA, LANES), F32),
            buf((L, S, TL, LANES), F32), buf((L, CG, TL + EXTRA, LANES), F32), buf((L, S, TL + EXTRA, LANES), F32),
            buf((L, S, TL, LANES), F32),
            buf((L, TA + 1, NL, LANES), F32), buf((TL * 8, LANES), F32), buf((max(TL * 8, TA), LANES), F32),
            buf((L, TL, D), BF16), buf((L, TL, E2), F32), buf((TL, E2), BF16), buf((TL, D), F32),
            buf((L - 1, TL, D), F32), buf((L - 1, TL, D), F32), buf((L, 4, 8, LANES), F32),
            buf((L, GROWS, LANES), F32), buf((L, GROWS, LANES), F32), buf((L, GROWS, LANES), F32),
            buf((L, NB + 1, SBR, LANES), F32), buf((L, NB, SBR, LANES), F32), buf((L, S, SBR, LANES), F32),
            buf((4, 8, LANES), F32),
            dma((4,)), dma((L * 4, S)), dma((L * 4, S)), dma((L, CHAINS, 2 * NST)), dma((L, CHAINS, 2 * NST)),
            dma((L, NB)), dma((L, NB)), dma((L, S)), dma((L, S)), dma((L, GROWS // UROWS)),
        ],
        compiler_params=pltpu.CompilerParams(
            collective_id=0, has_side_effects=True, vmem_limit_bytes=61 * 2**20
        ),
        name="liquid_layers",
    )(
        stream_in[0], cotangent[0], lengths, norm_gain, decay_rate, in_map, out_map,
        skip_gain, order_two, step_gain, glu_weight, glu_bias,
    )
    outs = pl.pallas_call(
        functools.partial(hand_on, len(outs)),
        out_shape=[shape(o.shape, o.dtype) for o in outs],
        in_specs=[hbm] * len(outs),
        out_specs=[hbm] * len(outs),
        scratch_shapes=[buf(o.shape, o.dtype) for o in outs] + [dma((2 * len(outs),)), dma((2 * len(outs),))],
        compiler_params=pltpu.CompilerParams(vmem_limit_bytes=61 * 2**20),
        name="results",
    )(*outs)
    return (outs[0][None], outs[1][None], *outs[2:])


def solution(mesh):
    split = P("batch", "seq", None)
    in_specs = (split, split, P("batch")) + (P(),) * 9
    out_specs = (split, split) + (P(),) * 10
    return jax.shard_map(per_device, mesh=mesh, in_specs=in_specs, out_specs=out_specs, check_vma=False)
```

```python
import functools
import math

import jax
import jax.numpy as jnp
from jax import lax
from jax.experimental import pallas as pl
from jax.experimental.pallas import tpu as pltpu
from jax.sharding import PartitionSpec as P

MESH = pl.DeviceIdType.MESH
EPSILON = 1e-05
LOG2E = 1.4426950408889634
LN2 = 0.6931471805599453
GELU_K = math.sqrt(2.0 / math.pi)
F32 = jnp.float32
BF16 = jnp.bfloat16
LANES = 128
CHUNK = 32
CHAINS = 6
UROWS = 256
EXTRA = 16


def rows8(v):
    return v.reshape(v.shape[0] // 8, 8, v.shape[1]).sum(0)


def sigmoid(v):
    return 1.0 / (1.0 + jnp.exp(-v))


def gelu_parts(m):
    th = jnp.tanh(GELU_K * (m + 0.044715 * m * m * m))
    return th


def bits_of(n):
    return [i for i in range(n.bit_length() - 1)]


def orders(seq, batch, chains):
    s = [("seq", b) for b in bits_of(seq)]
    b = [("batch", b) for b in bits_of(batch)]
    near = s[1:2] + b[:2]
    rest = b[2:] + s[2:]
    plans = []
    for c in range(chains):
        turn = c % len(near)
        plans.append(s[:1] + near[turn:] + near[:turn] + rest)
    return plans


def chain_rows(rows, devices, most):
    unit = 8 * devices
    units = rows // unit
    chains = min(most, units)
    cut = [units // chains + (1 if c < units % chains else 0) for c in range(chains)]
    return [(sum(cut[:c]) * unit, cut[c] * unit) for c in range(chains)]


def small_rows(states, batch):
    unit = 8 * batch
    return -(-(2 * states + 8 + EXTRA) // unit) * unit


def kernel(cfg, *refs):
    S, B, TL, D, NS, L, UN = cfg
    CG = D // LANES
    NSP = S // CG
    NL = NS // NSP
    E2 = 2 * D
    CB = E2 // LANES
    GROWS = D * CB
    SB_ROWS = small_rows(NL, B)
    spans = chain_rows(GROWS, S * B, CHAINS)
    plans = orders(S, B, len(spans))
    (
        x_ref, ct_ref, len_ref, gain_ref, dec_hbm, in_hbm, out_hbm, skip_ref, o2_ref, step_ref, w_hbm, bias_ref,
        y_out, gx_out, ggain_out, gdec_out, gin_out, gout_out, gskip_out, go2_out, gstep_out, FG, gbias_out, stats_out,
        W, DEC, INM, OUTM, NA, WT,
        XS, XR, RSTD, R, Y, YR, GS, GMR, GXR,
        SIG, P1, P2, LA, PJ, LG, GA, STR, GRD, ST,
        FB, RB, SBW, SBR, SBG, VEC,
        load_sem, send_sem, recv_sem, ar_ssem, ar_rsem, sb_ssem, sb_rsem, sg_ssem, sg_rsem,
    ) = refs
    U, GX = P2, Y
    me = lax.axis_index("seq")
    bi = lax.axis_index("batch")
    cg = me // NSP
    nh = lax.rem(me, NSP)
    n0 = nh * NL
    first_part = (nh == 0).astype(F32)
    clane = pl.ds(pl.multiple_of(cg * LANES, LANES), LANES)

    loads = [
        pltpu.make_async_copy(w_hbm, W, load_sem.at[0]),
        pltpu.make_async_copy(dec_hbm, DEC, load_sem.at[1]),
        pltpu.make_async_copy(in_hbm, INM, load_sem.at[2]),
        pltpu.make_async_copy(out_hbm, OUTM, load_sem.at[3]),
    ]
    for c in loads:
        c.start()

    barrier = pltpu.get_barrier_semaphore()
    partners = [(me ^ d, bi) for d in range(1, S)] + [(me, bi ^ (1 << b)) for b in bits_of(B)]
    for p in partners:
        pl.semaphore_signal(barrier, inc=1, device_id=p, device_id_type=MESH)

    pending = []

    def seq_copy(l, ph, j, src, dst):
        return pltpu.make_async_remote_copy(
            src_ref=src,
            dst_ref=dst,
            send_sem=send_sem.at[l * 4 + ph, j],
            recv_sem=recv_sem.at[l * 4 + ph, me],
            device_id=(j, bi),
            device_id_type=MESH,
        )

    def seq_wait(l, ph, k, src, dst):
        pltpu.make_async_remote_copy(
            src_ref=src,
            dst_ref=dst,
            send_sem=send_sem.at[l * 4 + ph, k],
            recv_sem=recv_sem.at[l * 4 + ph, k],
            device_id=(k, bi),
            device_id_type=MESH,
        ).wait_recv()

    def tblock(k):
        return pl.ds(pl.multiple_of(k * TL, TL), TL)

    def swap(axis, bit):
        return (me ^ (1 << bit), bi) if axis == "seq" else (me, bi ^ (1 << bit))

    def my_bit(axis, bit):
        return lax.rem((me if axis == "seq" else bi) // (1 << bit), 2)

    class Reduce:
        def __init__(self, l):
            self.l = l
            self.chains = []
            for (base, rows), plan in zip(spans, plans):
                off, size, roff, stages = base, rows, base, []
                for i, (axis, bit) in enumerate(plan):
                    half = size // 2
                    mine = my_bit(axis, bit)
                    keep = pl.multiple_of(off + mine * half, 8)
                    give = pl.multiple_of(off + (1 - mine) * half, 8)
                    stages.append((i, axis, bit, half, keep, give, roff))
                    off, size, roff = keep, half, roff + half
                self.chains.append(stages)
            self.n = n = len(plans[0])
            self.todo = [self.begin]
            self.todo += [functools.partial(self.reduce_step, i) for i in range(n)]
            self.todo += [functools.partial(self.gather_step, i) for i in range(n - 1, -1, -1)]

        def rs(self, c, stage):
            i, axis, bit, half, keep, give, roff = stage
            return pltpu.make_async_remote_copy(
                src_ref=FB.at[self.l, pl.ds(give, half)],
                dst_ref=RB.at[self.l, pl.ds(roff, half)],
                send_sem=ar_ssem.at[self.l, c, i],
                recv_sem=ar_rsem.at[self.l, c, i],
                device_id=swap(axis, bit),
                device_id_type=MESH,
            )

        def ag(self, c, stage):
            i, axis, bit, half, keep, give, roff = stage
            return pltpu.make_async_remote_copy(
                src_ref=FG.at[self.l, pl.ds(keep, half)],
                dst_ref=FG.at[self.l, pl.ds(keep, half)],
                send_sem=ar_ssem.at[self.l, c, self.n + i],
                recv_sem=ar_rsem.at[self.l, c, self.n + i],
                device_id=swap(axis, bit),
                device_id_type=MESH,
            )

        def begin(self):
            for c, stages in enumerate(self.chains):
                self.rs(c, stages[0]).start()

        def reduce_step(self, i):
            for c, stages in enumerate(self.chains):
                _, _, _, half, keep, _, roff = stages[i]
                self.rs(c, stages[i]).wait()
                step = math.gcd(half, 64)
                total = FB if i + 1 < self.n else FG

                def add(j, _, keep=keep, roff=roff, step=step, total=total):
                    at = pl.ds(pl.multiple_of(keep + j * step, 8), step)
                    total[self.l, at, :] = FB[self.l, at, :] + RB[self.l, pl.ds(pl.multiple_of(roff + j * step, 8), step), :]
                    return 0

                lax.fori_loop(0, half // step, add, 0)
                if i + 1 < self.n:
                    self.rs(c, stages[i + 1]).start()
                else:
                    self.ag(c, stages[i]).start()

        def gather_step(self, i):
            for c, stages in enumerate(self.chains):
                self.ag(c, stages[i]).wait()
                if i > 0:
                    self.ag(c, stages[i - 1]).start()

        def tick(self):
            if self.todo:
                self.todo.pop(0)()

    def norm_forward(l, src):
        def step(i, _):
            rows = pl.ds(pl.multiple_of(i * CHUNK, CHUNK), CHUNK)
            x = src[rows, :]
            center = x - jnp.mean(x, axis=-1, keepdims=True)
            spread = jnp.mean(center * center, axis=-1, keepdims=True)
            inv = lax.rsqrt(spread + EPSILON)
            xhat = center * inv
            RSTD[l, rows, :] = jnp.broadcast_to(inv, (CHUNK, LANES))
            for g in range(CG):
                XS[l, g, rows, :] = xhat[:, g * LANES : (g + 1) * LANES]
            return 0

        lax.fori_loop(0, TL // CHUNK, step, 0)

    def send_normed(l):
        for d in range(1, S):
            j = me ^ d
            copy = seq_copy(l, 0, j, XS.at[l, j // NSP], XR.at[l, tblock(me)])
            copy.start()
            pending.append(copy.wait_send)
        XR[l, tblock(me), :] = XS[l, cg]

    def scan_forward(l):
        gain = gain_ref[l : l + 1, clane]
        o2 = o2_ref[l : l + 1, clane]
        stp = step_ref[l : l + 1, clane]
        skip = skip_ref[l : l + 1, clane] * first_part
        first_row = lax.broadcasted_iota(jnp.int32, (TL, LANES), 0) == 0
        SIG[l, 0] = jnp.zeros((NL, LANES), F32)

        def block(k, carry):
            sig, last = carry

            @pl.when(k != me)
            def _():
                seq_wait(l, 0, k, XS.at[l, 0], XR.at[l, tblock(k)])

            normed = XR[l, tblock(k), :] * gain
            prev = jnp.where(first_row, last, pltpu.roll(normed, 1, 0))
            U[tblock(k), :] = normed + o2 * normed * prev
            z = stp * normed
            R[l, tblock(k), :] = jnp.maximum(z, 0.0) + jnp.log1p(jnp.exp(-jnp.abs(z)))
            na, wt = NA[l], WT[l]

            def inner(i, sig):
                for s in range(UN):
                    t = i * UN + s
                    at = pl.ds(k * TL + t, 1)
                    sig = jnp.exp2(na * R[l, at, :]) * sig + U[at, :]
                    SIG[l, k * TL + t + 1] = sig
                    P1[pl.ds(pl.multiple_of(t * 8, 8), 8), :] = rows8(wt * sig)
                return sig

            sig = lax.fori_loop(0, TL // UN, inner, sig)

            def finish(j, _):
                total = P1[pl.ds(j * 64, 8, stride=8), :]
                for s in range(1, 8):
                    total = total + P1[pl.ds(j * 64 + s, 8, stride=8), :]
                at = pl.ds(pl.multiple_of(k * TL + j * 8, 8), 8)
                Y[at, :] = total + skip * U[at, :]
                return 0

            lax.fori_loop(0, TL // 8, finish, 0)

            @pl.when(k == me)
            def _():
                YR[l, me] = Y[tblock(k), :]

            @pl.when(k != me)
            def _():
                seq_copy(l, 1, k, Y.at[tblock(k)], YR.at[l, me]).start()

            return sig, normed[TL - 1 : TL, :]

        lax.fori_loop(0, S, block, (jnp.zeros((NL, LANES), F32), jnp.zeros((1, LANES), F32)))
        return [seq_copy(l, 1, me ^ d, Y.at[tblock(me ^ d)], YR.at[l, me]).wait_send for d in range(1, S)]

    def mixed_of(l, g, rows):
        m = YR[l, g * NSP, rows, :]
        for h in range(1, NSP):
            m = m + YR[l, g * NSP + h, rows, :]
        return m

    def valid_of(i):
        pos = me * TL + i * CHUNK + lax.broadcasted_iota(jnp.int32, (CHUNK, 1), 0)
        return (pos < len_ref[0]).astype(F32)

    def glu_forward(l, src, dst):
        for d in range(1, S):
            j = me ^ d
            seq_wait(l, 1, j, Y.at[pl.ds(0, TL)], YR.at[l, j])

        def act(i, sq):
            rows = pl.ds(pl.multiple_of(i * CHUNK, CHUNK), CHUNK)
            valid = valid_of(i)
            for g in range(CG):
                m = mixed_of(l, g, rows)
                a = 0.5 * m * (1.0 + gelu_parts(m))
                LA[l, rows, g * LANES : (g + 1) * LANES] = a.astype(BF16)
                sq = sq + rows8(a * a * valid)
            return sq

        zero = jnp.zeros((8, LANES), F32)
        sq_act = lax.fori_loop(0, TL // CHUNK, act, zero)
        PJ[l] = jnp.dot(LA[l], W[l], preferred_element_type=F32) + bias_ref[l : l + 1, :]

        def gate(i, sq):
            sq_b, sq_s, cnt = sq
            rows = pl.ds(pl.multiple_of(i * CHUNK, CHUNK), CHUNK)
            valid = valid_of(i)
            for g in range(CG):
                cols = slice(g * LANES, (g + 1) * LANES)
                gcols = slice(D + g * LANES, D + (g + 1) * LANES)
                branch = PJ[l, rows, cols] * sigmoid(PJ[l, rows, gcols]) * valid
                out = src[rows, cols] + branch
                dst[rows, cols] = out
                sq_b = sq_b + rows8(branch * branch)
                sq_s = sq_s + rows8(out * out * valid)
            cnt = cnt + rows8(jnp.broadcast_to(valid, (CHUNK, LANES)))
            return sq_b, sq_s, cnt

        sq_b, sq_s, cnt = lax.fori_loop(0, TL // CHUNK, gate, (zero, zero, zero))
        for k, v in enumerate((sq_act, sq_b, sq_s, cnt)):
            ST[l, k] = v

    def gate_backward(l, gsrc):
        def gate(i, acc):
            rows = pl.ds(pl.multiple_of(i * CHUNK, CHUNK), CHUNK)
            valid = valid_of(i)
            out = []
            for g in range(CG):
                cols = slice(g * LANES, (g + 1) * LANES)
                gcols = slice(D + g * LANES, D + (g + 1) * LANES)
                gb = gsrc[rows, cols] * valid
                s = sigmoid(PJ[l, rows, gcols])
                one = gb * s
                two = one * PJ[l, rows, cols] * (1.0 - s)
                LG[rows, cols] = one.astype(BF16)
                LG[rows, gcols] = two.astype(BF16)
                out.append((rows8(one), rows8(two)))
            return tuple(a + b for a, b in zip(acc, [o[0] for o in out] + [o[1] for o in out]))

        zero = jnp.zeros((8, LANES), F32)
        return lax.fori_loop(0, TL // CHUNK, gate, (zero,) * CB)

    def act_backward(l, bias):
        GA[...] = lax.dot_general(LG[...], W[l], (((1,), (1,)), ((), ())), preferred_element_type=F32)

        def act(i, _):
            rows = pl.ds(pl.multiple_of(i * CHUNK, CHUNK), CHUNK)
            for g in range(CG):
                m = mixed_of(l, g, rows)
                th = gelu_parts(m)
                slope = 0.5 * (1.0 + th) + 0.5 * m * (1.0 - th * th) * GELU_K * (1.0 + 3 * 0.044715 * m * m)
                GS[l, g, rows, :] = GA[rows, g * LANES : (g + 1) * LANES] * slope
            return 0

        lax.fori_loop(0, TL // CHUNK, act, 0)
        extra = [jnp.sum(b, axis=0, keepdims=True) for b in bias]
        extra += [jnp.sum(ST[l, k], axis=0, keepdims=True) for k in range(4)]
        extra += [jnp.zeros((EXTRA - len(extra), LANES), F32)]
        extra = jnp.concatenate(extra, axis=0)
        for g in range(CG):
            GS[l, g, TL : TL + EXTRA, :] = extra
        for d in range(1, S):
            j = me ^ d
            copy = seq_copy(l, 2, j, GS.at[l, j // NSP], GMR.at[l, me])
            copy.start()
            pending.append(copy.wait_send)
        GMR[l, me] = GS[l, cg]

    def weight_grad(l):
        for c in range(2):
            half = lax.dot_general(
                LA[l], LG[:, c * D : (c + 1) * D], (((0,), (0,)), ((), ())), preferred_element_type=F32
            )
            for q in range(CB // 2):
                FB[l, pl.ds((c * (CB // 2) + q) * D, D), :] = half[:, q * LANES : (q + 1) * LANES]

    def scan_backward(l, ticks):
        gain = gain_ref[l : l + 1, clane]
        o2 = o2_ref[l : l + 1, clane]
        stp = step_ref[l : l + 1, clane]
        skip = skip_ref[l : l + 1, clane]
        row_id = lax.broadcasted_iota(jnp.int32, (TL, LANES), 0)
        zero8 = jnp.zeros((8, LANES), F32)
        zeros = jnp.zeros((NL, LANES), F32)
        for v in range(4):
            VEC[v] = zero8

        def block(kk, carry):
            nu, acc, gdc, after = carry
            k = S - 1 - kk

            @pl.when(k != me)
            def _():
                seq_wait(l, 2, k, GS.at[l, 0], GMR.at[l, k])

            na, wt = NA[l], WT[l]

            def inner(ii, c):
                nu, acc, gdc = c
                i = TL // UN - 1 - ii
                for s in range(UN - 1, -1, -1):
                    t = i * UN + s
                    rate = R[l, pl.ds(k * TL + t, 1), :]
                    gm = GMR[l, k, pl.ds(t, 1), :]
                    mu = wt * gm + nu
                    acc = acc + gm * SIG[l, k * TL + t + 1]
                    at = pl.ds(pl.multiple_of(t * 8, 8), 8)
                    P1[at, :] = rows8(mu)
                    nu = jnp.exp2(na * rate) * mu
                    q = nu * SIG[l, k * TL + t]
                    gdc = gdc + q * rate
                    P2[at, :] = rows8(na * q)
                return nu, acc, gdc

            nu, acc, gdc = lax.fori_loop(0, TL // UN, inner, (nu, acc, gdc))

            def finish(j, _):
                one = P1[pl.ds(j * 64, 8, stride=8), :]
                two = P2[pl.ds(j * 64, 8, stride=8), :]
                for s in range(1, 8):
                    one = one + P1[pl.ds(j * 64 + s, 8, stride=8), :]
                    two = two + P2[pl.ds(j * 64 + s, 8, stride=8), :]
                at = pl.ds(pl.multiple_of(j * 8, 8), 8)
                GX[pl.ds(pl.multiple_of(k * TL + j * 8, 8), 8), :] = one
                GA[at, 0:LANES] = two
                return 0

            lax.fori_loop(0, TL // 8, finish, 0)
            xhat = XR[l, tblock(k), :]
            normed = xhat * gain
            before = XR[l, pl.ds(jnp.maximum(k * TL - 1, 0), 1), :] * gain
            before = jnp.where(k == 0, 0.0, before)
            prev = jnp.where(row_id == 0, before, pltpu.roll(normed, 1, 0))
            gm = GMR[l, k, 0:TL, :] * first_part
            gdrv = GX[tblock(k), :] + skip * gm
            grate = GA[0:TL, 0:LANES] * LN2
            both = gdrv * normed
            h = o2 * both
            later = jnp.where(row_id == TL - 1, after, pltpu.roll(h, TL - 1, 0))
            slope = sigmoid(stp * normed) * grate
            gnormed = gdrv * (1.0 + o2 * prev) + later + slope * stp
            GX[tblock(k), :] = gnormed * gain
            VEC[0] = VEC[0] + rows8(gm * (normed + o2 * normed * prev))
            VEC[1] = VEC[1] + rows8(both * prev)
            VEC[2] = VEC[2] + rows8(slope * normed)
            VEC[3] = VEC[3] + rows8(gnormed * xhat)

            @pl.when(k == me)
            def _():
                GXR[l, me] = GX[tblock(k), :]

            @pl.when(k != me)
            def _():
                seq_copy(l, 3, k, GX.at[tblock(k)], GXR.at[l, me]).start()

            for at, todo in ticks.items():

                @pl.when(kk == at)
                def _(todo=todo):
                    for t in todo:
                        t.tick()

            return nu, acc, gdc, h[0:1, :]

        carry = (zeros, zeros, zeros, jnp.zeros((1, LANES), F32))
        _, acc, gdc, _ = lax.fori_loop(0, S, block, carry)
        sent = [seq_copy(l, 3, me ^ d, GX.at[tblock(me ^ d)], GXR.at[l, me]).wait_send for d in range(1, S)]
        SBW[l, 0:NL, :] = acc
        SBW[l, NL : 2 * NL, :] = gdc
        vec = [jnp.sum(VEC[v], axis=0, keepdims=True) for v in range(4)]
        vec += [jnp.zeros((4, LANES), F32)]
        SBW[l, 2 * NL : 2 * NL + 8, :] = jnp.concatenate(vec, axis=0)
        extra = GMR[l, 0, TL : TL + EXTRA, :]
        for k in range(1, S):
            extra = extra + GMR[l, k, TL : TL + EXTRA, :]
        SBW[l, 2 * NL + 8 : 2 * NL + 8 + EXTRA, :] = extra
        if SB_ROWS > 2 * NL + 8 + EXTRA:
            SBW[l, 2 * NL + 8 + EXTRA :, :] = jnp.zeros((SB_ROWS - 2 * NL - 8 - EXTRA, LANES), F32)
        return sent

    class Small:
        def __init__(self, l):
            self.l = l
            self.n = nb = len(bits_of(B))
            off, size, roff, self.stages = 0, SB_ROWS, 0, []
            for i in range(nb):
                half = size // 2
                mine = my_bit("batch", i)
                keep = pl.multiple_of(off + mine * half, 8)
                give = pl.multiple_of(off + (1 - mine) * half, 8)
                self.stages.append((i, half, keep, give, roff))
                off, size, roff = keep, half, roff + half
            self.todo = [lambda: self.rs(0).start()]
            self.todo += [functools.partial(self.reduce_step, i) for i in range(nb)]
            self.todo += [functools.partial(self.gather_step, i) for i in range(nb - 1, -1, -1)]
            self.todo += [self.gathered]

        def rs(self, i):
            _, half, keep, give, roff = self.stages[i]
            return pltpu.make_async_remote_copy(
                src_ref=SBW.at[self.l, pl.ds(give, half)],
                dst_ref=SBR.at[self.l, pl.ds(roff, half)],
                send_sem=sb_ssem.at[self.l, i],
                recv_sem=sb_rsem.at[self.l, i],
                device_id=(me, bi ^ (1 << i)),
                device_id_type=MESH,
            )

        def ag(self, i):
            _, half, keep, give, roff = self.stages[i]
            return pltpu.make_async_remote_copy(
                src_ref=SBG.at[self.l, me, pl.ds(keep, half)],
                dst_ref=SBG.at[self.l, me, pl.ds(keep, half)],
                send_sem=sb_ssem.at[self.l, self.n + i],
                recv_sem=sb_rsem.at[self.l, self.n + i],
                device_id=(me, bi ^ (1 << i)),
                device_id_type=MESH,
            )

        def seq(self, j, slot, rslot):
            return pltpu.make_async_remote_copy(
                src_ref=SBG.at[self.l, me],
                dst_ref=SBG.at[self.l, slot],
                send_sem=sg_ssem.at[self.l, j],
                recv_sem=sg_rsem.at[self.l, rslot],
                device_id=(j, bi),
                device_id_type=MESH,
            )

        def reduce_step(self, i):
            _, half, keep, _, roff = self.stages[i]
            self.rs(i).wait()
            total = SBW[self.l, pl.ds(keep, half), :] + SBR[self.l, pl.ds(roff, half), :]
            if i + 1 < self.n:
                SBW[self.l, pl.ds(keep, half), :] = total
                self.rs(i + 1).start()
            else:
                SBG[self.l, me, pl.ds(keep, half), :] = total
                self.ag(i).start()

        def gather_step(self, i):
            self.ag(i).wait()
            if i > 0:
                self.ag(i - 1).start()
            else:
                for d in range(1, S):
                    self.seq(me ^ d, me, me).start()

        def gathered(self):
            for d in range(1, S):
                self.seq(me ^ d, me ^ d, me ^ d).wait()
            l = self.l
            for g in range(CG):
                cols = slice(g * LANES, (g + 1) * LANES)
                vec = None
                for h in range(NSP):
                    slot = g * NSP + h
                    rows = slice(h * NL, (h + 1) * NL)
                    acc = SBG[l, slot, 0:NL, :]
                    gin_out[l, rows, cols] = OUTM[l, rows, cols] * acc
                    gout_out[l, rows, cols] = INM[l, rows, cols] * acc
                    gdec_out[l, rows, cols] = -SBG[l, slot, NL : 2 * NL, :]
                    part = SBG[l, slot, 2 * NL : 2 * NL + 8, :]
                    vec = part if vec is None else vec + part
                gskip_out[l : l + 1, cols] = vec[0:1]
                go2_out[l : l + 1, cols] = vec[1:2]
                gstep_out[l : l + 1, cols] = vec[2:3]
                ggain_out[l : l + 1, cols] = vec[3:4]
            base = 2 * NL + 8
            for q in range(CB):
                gbias_out[l : l + 1, q * LANES : (q + 1) * LANES] = SBG[l, 0, base + q : base + q + 1, :]
            sq = jnp.sum(SBG[l, 0, base + CB : base + CB + 8, :], axis=1, keepdims=True)
            count = sq[3:4] * (1.0 / LANES)
            root = jnp.sqrt(sq[0:3] / (count * D))
            col = lax.broadcasted_iota(jnp.int32, (1, 3), 1)
            stats_out[l : l + 1, :] = jnp.where(col == 0, root[0:1], jnp.where(col == 1, root[1:2], root[2:3]))

        def tick(self):
            if self.todo:
                self.todo.pop(0)()

    def norm_backward(l, gsrc, gdst):
        for d in range(1, S):
            j = me ^ d
            seq_wait(l, 3, j, GX.at[pl.ds(0, TL)], GXR.at[l, j])

        def step(i, _):
            rows = pl.ds(pl.multiple_of(i * CHUNK, CHUNK), CHUNK)
            inv = RSTD[l, rows, :]
            gx, xh = [], []
            s1 = s2 = None
            for g in range(CG):
                v = GXR[l, g * NSP, rows, :]
                for h in range(1, NSP):
                    v = v + GXR[l, g * NSP + h, rows, :]
                x = XS[l, g, rows, :]
                gx.append(v)
                xh.append(x)
                s1 = v if s1 is None else s1 + v
                s2 = v * x if s2 is None else s2 + v * x
            m1 = jnp.sum(s1, axis=-1, keepdims=True) * (1.0 / D)
            m2 = jnp.sum(s2, axis=-1, keepdims=True) * (1.0 / D)
            for g in range(CG):
                cols = slice(g * LANES, (g + 1) * LANES)
                gdst[rows, cols] = gsrc[rows, cols] + inv * (gx[g] - m1 - xh[g] * m2)
            return 0

        lax.fori_loop(0, TL // CHUNK, step, 0)

    norm_forward(0, x_ref)
    pl.semaphore_wait(barrier, len(partners))
    send_normed(0)
    for c in loads:
        c.wait()
    nrows = pl.ds(pl.multiple_of(n0, 8), NL)
    for l in range(L):
        NA[l] = DEC[l, nrows, clane] * (-LOG2E)
        WT[l] = INM[l, nrows, clane] * OUTM[l, nrows, clane]
    streams = [x_ref] + [STR.at[l] for l in range(L - 1)] + [y_out]
    for l in range(L):
        if l:
            norm_forward(l, streams[l])
            send_normed(l)
        sent = scan_forward(l)
        glu_forward(l, streams[l], streams[l + 1])
        for done in sent:
            done()

    grads = [gx_out] + [GRD.at[l] for l in range(L - 1)] + [ct_ref]
    def at_blocks(plan):
        return {(q + 1) * S // 4 - 1: todo for q, todo in enumerate(plan) if todo}

    run = lambda *things: [t.tick() for t in things]
    above = ()
    for l in range(L - 1, -1, -1):
        big, small = Reduce(l), Small(l)
        bias = gate_backward(l, grads[l + 1])
        weight_grad(l)
        run(big)
        run(*above)
        act_backward(l, bias)
        plan = [above, (big,), above, (big,)] if above else [(), (big,), (), ()]
        sent = scan_backward(l, at_blocks(plan))
        run(small)
        norm_backward(l, grads[l + 1], grads[l])
        for done in sent:
            done()
        run(big, *above, small)
        above = (big, small) + above
    while any(t.todo for t in above):
        run(*above)
    for done in pending:
        done()


def hand_on(*refs):
    n = (len(refs) - 2) // 2
    sem, block_sem = refs[-2], refs[-1]
    copies = []
    for i, (a, o) in enumerate(zip(refs[:n], refs[n : 2 * n])):
        if a.shape == o.shape:
            copies.append(pltpu.make_async_copy(a, o, sem.at[i]))
            continue
        layers, rows, columns = o.shape
        for l in range(layers):
            for c in range(columns // LANES):
                block = o.at[l, :, pl.ds(c * LANES, LANES)]
                copies.append(pltpu.make_async_copy(a.at[l, pl.ds(c * rows, rows)], block, block_sem.at[l, c]))
    for c in copies:
        c.start()
    for c in copies:
        c.wait()


def per_device(
    stream_in, cotangent, lengths, norm_gain, decay_rate, in_map, out_map, skip_gain, order_two, step_gain, glu_weight, glu_bias
):
    S, B = lax.axis_size("seq"), lax.axis_size("batch")
    _, TL, D = stream_in.shape
    L, NS = decay_rate.shape[:2]
    UN = math.gcd(TL, 16)
    CG, E2 = D // LANES, 2 * D
    NL = NS // (S // CG)
    TA = S * TL
    CB = E2 // LANES
    GROWS = D * CB
    SBR = small_rows(NL, B)
    NB, NST = len(bits_of(B)), len(bits_of(B)) + len(bits_of(S))
    shape = jax.ShapeDtypeStruct
    vmem = pl.BlockSpec(memory_space=pltpu.VMEM)
    smem = pl.BlockSpec(memory_space=pltpu.SMEM)
    hbm = pl.BlockSpec(memory_space=pl.ANY)
    buf = pltpu.VMEM
    dma = pltpu.SemaphoreType.DMA
    outs = pl.pallas_call(
        functools.partial(kernel, (S, B, TL, D, NS, L, UN)),
        out_shape=[
            buf((TL, D), F32), buf((TL, D), F32), buf((L, D), F32),
            buf((L, NS, D), F32), buf((L, NS, D), F32), buf((L, NS, D), F32),
            buf((L, D), F32), buf((L, D), F32), buf((L, D), F32),
            buf((L, GROWS, LANES), F32), buf((L, E2), F32), buf((L, 3), F32),
        ],
        in_specs=[vmem, vmem, smem, vmem, hbm, hbm, hbm, vmem, vmem, vmem, hbm, vmem],
        out_specs=[vmem] * 12,
        scratch_shapes=[
            buf((L, D, E2), BF16), buf((L, NS, D), F32), buf((L, NS, D), F32), buf((L, NS, D), F32),
            buf((L, NL, LANES), F32), buf((L, NL, LANES), F32),
            buf((L, CG, TL, LANES), F32), buf((L, TA, LANES), F32), buf((L, TL, LANES), F32),
            buf((L, TA, LANES), F32), buf((TA, LANES), F32),
            buf((L, S, TL, LANES), F32), buf((L, CG, TL + EXTRA, LANES), F32), buf((L, S, TL + EXTRA, LANES), F32),
            buf((L, S, TL, LANES), F32),
            buf((L, TA + 1, NL, LANES), F32), buf((TL * 8, LANES), F32), buf((max(TL * 8, TA), LANES), F32),
            buf((L, TL, D), BF16), buf((L, TL, E2), F32), buf((TL, E2), BF16), buf((TL, D), F32),
            buf((L - 1, TL, D), F32), buf((L - 1, TL, D), F32), buf((L, 4, 8, LANES), F32),
            buf((L, GROWS, LANES), F32), buf((L, GROWS, LANES), F32),
            buf((L, SBR, LANES), F32), buf((L, SBR, LANES), F32), buf((L, S, SBR, LANES), F32),
            buf((4, 8, LANES), F32),
            dma((4,)), dma((L * 4, S)), dma((L * 4, S)), dma((L, CHAINS, 2 * NST)), dma((L, CHAINS, 2 * NST)),
            dma((L, 2 * NB)), dma((L, 2 * NB)), dma((L, S)), dma((L, S)),
        ],
        compiler_params=pltpu.CompilerParams(
            collective_id=0, has_side_effects=True, vmem_limit_bytes=57 * 2**20
        ),
        name="liquid_layers",
    )(
        stream_in[0], cotangent[0], lengths, norm_gain, decay_rate, in_map, out_map,
        skip_gain, order_two, step_gain, glu_weight, glu_bias,
    )
    outs = pl.pallas_call(
        hand_on,
        out_shape=[shape((L, D, E2), F32) if o.ndim == 3 and o.shape[1] == GROWS else shape(o.shape, F32) for o in outs],
        in_specs=[vmem] * len(outs),
        out_specs=[hbm] * len(outs),
        scratch_shapes=[dma((len(outs),)), dma((L, CB))],
        compiler_params=pltpu.CompilerParams(vmem_limit_bytes=2**20),
        name="results",
    )(*outs)
    return (outs[0][None], outs[1][None], *outs[2:])


def solution(mesh):
    split = P("batch", "seq", None)
    in_specs = (split, split, P("batch")) + (P(),) * 9
    out_specs = (split, split) + (P(),) * 10
    return jax.shard_map(per_device, mesh=mesh, in_specs=in_specs, out_specs=out_specs, check_vma=False)
```

```python
import functools
import math

import jax
import jax.numpy as jnp
from jax import lax
from jax.experimental import pallas as pl
from jax.experimental.pallas import tpu as pltpu
from jax.sharding import PartitionSpec as P

MESH = pl.DeviceIdType.MESH
EPSILON = 1e-05
LOG2E = 1.4426950408889634
LN2 = 0.6931471805599453
GELU_K = math.sqrt(2.0 / math.pi)
F32 = jnp.float32
BF16 = jnp.bfloat16
LANES = 128
CHUNK = 32
CHAINS = 6
UROWS = 256
PIECES = 4
EXTRA = 16


def rows8(v):
    return v.reshape(v.shape[0] // 8, 8, v.shape[1]).sum(0)


def sigmoid(v):
    return 1.0 / (1.0 + jnp.exp(-v))


def gelu_parts(m):
    th = jnp.tanh(GELU_K * (m + 0.044715 * m * m * m))
    return th


def bits_of(n):
    return [i for i in range(n.bit_length() - 1)]


def orders(seq, batch, chains, spare):
    s = [("seq", b) for b in bits_of(seq)]
    b = [("batch", b) for b in bits_of(batch)]
    near = b[:2] if spare else s[1:2] + b[:2]
    rest = s[1:2] + b[2:] + s[2:] if spare else b[2:] + s[2:]
    plans = []
    for c in range(chains):
        turn = c % len(near)
        plans.append(near[turn:] + near[:turn] + rest)
    return plans


def chain_rows(rows, devices, most):
    unit = 8 * devices
    units = rows // unit
    chains = min(most, units)
    cut = [units // chains + (1 if c < units % chains else 0) for c in range(chains)]
    return [(sum(cut[:c]) * unit, cut[c] * unit) for c in range(chains)]


def small_rows(layers, states, batch):
    unit = 8 * batch
    return -(-layers * (2 * states + EXTRA) // unit) * unit


def kernel(cfg, *refs):
    S, B, TL, D, NS, L, UN = cfg
    CG = D // LANES
    NSP = S // CG
    NL = NS // NSP
    E2 = 2 * D
    CB = E2 // LANES
    GROWS = D * CB
    NQ = PIECES
    TB = TL // NQ
    SB_LAYER = 2 * NL + EXTRA
    SB_ROWS = small_rows(L, NL, B)
    SP = SB_ROWS // B
    spans = chain_rows(GROWS // 2, S * B // 2, CHAINS)
    (
        x_hbm, ct_hbm, len_hbm, gain_hbm, dec_hbm, in_hbm, out_hbm, skip_hbm, o2_hbm, step_hbm, w_hbm, bias_hbm,
        y_out, gx_out, ggain_out, gdec_out, gin_out, gout_out, gskip_out, go2_out, gstep_out, FG, gbias_out, stats_out,
        x_ref, ct_ref, len_ref, gain_ref, DEC, INM, OUTM, skip_ref, o2_ref, step_ref, W, bias_ref, NA, WT,
        XS, XR, RSTD, R, Y, YR, GS, GMR, GXR,
        SIG, P1, P2, LA, PJ, LG, GA, STR, GRD, ST,
        FB, RB, AF, AR, GF, GFR, LA2, LG2, SBW, SBR, SBG, VEC,
        load_sem, send_sem, recv_sem, ar_ssem, ar_rsem, sb_ssem, sb_rsem, sg_ssem, sg_rsem, pair_ssem, pair_rsem,
    ) = refs
    U, GX = P2, Y
    me = lax.axis_index("seq")
    bi = lax.axis_index("batch")
    cg = me // NSP
    nh = lax.rem(me, NSP)
    n0 = nh * NL
    first_part = (nh == 0).astype(F32)
    clane = pl.ds(pl.multiple_of(cg * LANES, LANES), LANES)

    sources = (x_hbm, len_hbm, gain_hbm, o2_hbm, step_hbm, dec_hbm, in_hbm, out_hbm, skip_hbm, w_hbm, bias_hbm, ct_hbm)
    targets = (x_ref, len_ref, gain_ref, o2_ref, step_ref, DEC, INM, OUTM, skip_ref, W, bias_ref, ct_ref)
    loads = [pltpu.make_async_copy(h, v, load_sem.at[i]) for i, (h, v) in enumerate(zip(sources, targets))]
    for c in loads:
        c.start()

    barrier = pltpu.get_barrier_semaphore()
    partners = [(me ^ d, bi) for d in range(1, S)]
    partners += [(me ^ 1, bi ^ (1 << b)) for b in bits_of(B)]
    for p in partners:
        pl.semaphore_signal(barrier, inc=1, device_id=p, device_id_type=MESH)

    sends = []

    def sent():
        while sends:
            sends.pop(0)()

    def seq_copy(ph, j, q, src, dst):
        return pltpu.make_async_remote_copy(
            src_ref=src,
            dst_ref=dst,
            send_sem=send_sem.at[j, q],
            recv_sem=recv_sem.at[ph % 2, me, q],
            device_id=(j, bi),
            device_id_type=MESH,
        )

    def seq_wait(ph, k, q, ref):
        pltpu.make_async_remote_copy(
            src_ref=ref,
            dst_ref=ref,
            send_sem=send_sem.at[k, q],
            recv_sem=recv_sem.at[ph % 2, k, q],
            device_id=(k, bi),
            device_id_type=MESH,
        ).wait_recv()

    def rows_of(q, extra=0):
        return pl.ds(q * TB if isinstance(q, int) else pl.multiple_of(q * TB, TB), TB + extra)

    def span(k, q):
        return pl.ds(pl.multiple_of((k * NQ + q) * TB, TB), TB)

    peers = list(range(S - 1, 0, -1))

    def tblock(k):
        return pl.ds(pl.multiple_of(k * TL, TL), TL)

    def bit_of(v, bit):
        return lax.rem(v // (1 << bit), 2)

    def swap(axis, bit):
        if axis == "batch":
            return (me ^ 1, bi ^ (1 << bit))
        return (me ^ (1 << bit) ^ 1, bi)

    def my_bit(axis, bit):
        return bit_of(me if axis == "seq" else bi, bit)

    side = lax.rem(sum(bit_of(me, i) for i in bits_of(S)) + sum(bit_of(bi, i) for i in bits_of(B)), 2)

    def pair_copy(which, l, src, dst):
        return pltpu.make_async_remote_copy(
            src_ref=src,
            dst_ref=dst,
            send_sem=pair_ssem.at[which],
            recv_sem=pair_rsem.at[which, l],
            device_id=(me ^ 1, bi),
            device_id_type=MESH,
        )

    def act_copy(l):
        return pair_copy(0, l, AF, AR.at[l])

    def grad_copy(l):
        return pair_copy(1, l, GF.at[1 - side], GFR.at[l])

    class Reduce:
        after = ()

        def __init__(self, l):
            self.l = l
            self.chains = []
            plans = orders(S, B, len(spans), False)
            for (base, rows), plan in zip(spans, plans):
                off, size, roff, stages = base, rows, base, []
                for i, (axis, bit) in enumerate(plan):
                    half = size // 2
                    mine = my_bit(axis, bit)
                    keep = pl.multiple_of(off + mine * half, 8)
                    give = pl.multiple_of(off + (1 - mine) * half, 8)
                    stages.append((i, axis, bit, half, keep, give, roff))
                    off, size, roff = keep, half, roff + half
                self.chains.append(stages)
            self.n = n = len(plans[0])
            self.todo = [self.begin]
            self.todo += [functools.partial(self.reduce_step, i) for i in range(n)]
            self.todo += [functools.partial(self.gather_step, i) for i in range(n - 1, -1, -1)]
            self.todo += [self.last_step]

        def rs(self, c, stage):
            i, axis, bit, half, keep, give, roff = stage
            return pltpu.make_async_remote_copy(
                src_ref=FB.at[self.l, pl.ds(give, half)],
                dst_ref=RB.at[self.l, pl.ds(roff, half)],
                send_sem=ar_ssem.at[self.l, c],
                recv_sem=ar_rsem.at[self.l, c, i],
                device_id=swap(axis, bit),
                device_id_type=MESH,
            )

        def pair(self, c):
            base, rows = spans[c]
            here = FG.at[self.l, side, pl.ds(base, rows)]
            return pltpu.make_async_remote_copy(
                src_ref=here,
                dst_ref=here,
                send_sem=ar_ssem.at[self.l, c],
                recv_sem=ar_rsem.at[self.l, c, 2 * self.n],
                device_id=(me ^ 1, bi),
                device_id_type=MESH,
            )

        def ag(self, c, stage):
            i, axis, bit, half, keep, give, roff = stage
            return pltpu.make_async_remote_copy(
                src_ref=FG.at[self.l, side, pl.ds(keep, half)],
                dst_ref=FG.at[self.l, side, pl.ds(keep, half)],
                send_sem=ar_ssem.at[self.l, c],
                recv_sem=ar_rsem.at[self.l, c, self.n + i],
                device_id=swap(axis, bit),
                device_id_type=MESH,
            )

        def begin(self):
            for c, stages in enumerate(self.chains):
                self.rs(c, stages[0]).start()

        def reduce_step(self, i):
            for c, stages in enumerate(self.chains):
                _, _, _, half, keep, _, roff = stages[i]
                self.rs(c, stages[i]).wait()
                step = math.gcd(half, 64)

                def add(j, _, i=i, keep=keep, roff=roff, step=step):
                    at = pl.ds(pl.multiple_of(keep + j * step, 8), step)
                    total = FB[self.l, at, :] + RB[self.l, pl.ds(pl.multiple_of(roff + j * step, 8), step), :]
                    if i + 1 < self.n:
                        FB[self.l, at, :] = total
                    else:
                        FG[self.l, side, at, :] = total
                    return 0

                lax.fori_loop(0, half // step, add, 0)
                if i + 1 < self.n:
                    self.rs(c, stages[i + 1]).start()
                else:
                    self.ag(c, stages[i]).start()

        def gather_step(self, i):
            for c, stages in enumerate(self.chains):
                self.ag(c, stages[i]).wait()
                if i > 0:
                    self.ag(c, stages[i - 1]).start()
                else:
                    self.pair(c).start()

        def last_step(self):
            for c in range(len(self.chains)):
                self.pair(c).wait()

    def norm_forward(l, src):
        def step(i, _):
            rows = pl.ds(pl.multiple_of(i * CHUNK, CHUNK), CHUNK)
            x = src[rows, :]
            center = x - jnp.mean(x, axis=-1, keepdims=True)
            spread = jnp.mean(center * center, axis=-1, keepdims=True)
            inv = lax.rsqrt(spread + EPSILON)
            xhat = center * inv
            RSTD[l, rows, :] = jnp.broadcast_to(inv, (CHUNK, LANES))
            for g in range(CG):
                XS[l, g, rows, :] = xhat[:, g * LANES : (g + 1) * LANES]
            return 0

        lax.fori_loop(0, TL // CHUNK, step, 0)

    def send_normed(l):
        for q in range(NQ):
            for d in peers:
                j = me ^ d
                seq_copy(0, j, q, XS.at[l, j // NSP, rows_of(q)], XR.at[l, span(me, q)]).start()
        XR[l, tblock(me), :] = XS[l, cg]

    def scan_forward(l):
        gain = gain_ref[l : l + 1, clane]
        o2 = o2_ref[l : l + 1, clane]
        stp = step_ref[l : l + 1, clane]
        skip = skip_ref[l : l + 1, clane] * first_part
        first_row = lax.broadcasted_iota(jnp.int32, (TB, LANES), 0) == 0
        SIG[l, 0] = jnp.zeros((NL, LANES), F32)

        def block(b, carry):
            sig, last = carry
            k, q = b // NQ, lax.rem(b, NQ)
            here, t0 = span(k, q), b * TB

            @pl.when(k != me)
            def _():
                seq_wait(0, k, q, XR.at[l, here])

            normed = XR[l, here, :] * gain
            prev = jnp.where(first_row, last, pltpu.roll(normed, 1, 0))
            U[here, :] = normed + o2 * normed * prev
            z = stp * normed
            R[l, here, :] = jnp.maximum(z, 0.0) + jnp.log1p(jnp.exp(-jnp.abs(z)))
            na, wt = NA[l], WT[l]

            def inner(i, sig):
                for s in range(UN):
                    t = i * UN + s
                    at = pl.ds(t0 + t, 1)
                    sig = jnp.exp2(na * R[l, at, :]) * sig + U[at, :]
                    SIG[l, t0 + t + 1] = sig
                    P1[pl.ds(pl.multiple_of(t * 8, 8), 8), :] = rows8(wt * sig)
                return sig

            sig = lax.fori_loop(0, TB // UN, inner, sig)
            for j in range(TB // 8):
                total = P1[pl.ds(j * 64, 8, stride=8), :]
                for s in range(1, 8):
                    total = total + P1[pl.ds(j * 64 + s, 8, stride=8), :]
                at = pl.ds(pl.multiple_of(t0 + j * 8, 8), 8)
                Y[at, :] = total + skip * U[at, :]

            @pl.when(k == me)
            def _():
                YR[l, me, rows_of(q), :] = Y[here, :]

            @pl.when(k != me)
            def _():
                seq_copy(0, k, q, XS.at[l, 0, rows_of(q)], XR.at[l, here]).wait_send()
                seq_copy(1, k, q, Y.at[here], YR.at[l, me, rows_of(q)]).start()

            return sig, normed[TB - 1 : TB, :]

        lax.fori_loop(0, S * NQ, block, (jnp.zeros((NL, LANES), F32), jnp.zeros((1, LANES), F32)))
        for q in range(NQ):
            for d in peers:
                here = span(me ^ d, q)
                sends.append(seq_copy(1, me ^ d, q, Y.at[here], YR.at[l, me, rows_of(q)]).wait_send)

    def mixed_of(l, g, rows):
        m = YR[l, g * NSP, rows, :]
        for h in range(1, NSP):
            m = m + YR[l, g * NSP + h, rows, :]
        return m

    def valid_of(i):
        pos = me * TL + i * CHUNK + lax.broadcasted_iota(jnp.int32, (CHUNK, 1), 0)
        return (pos < len_ref[0]).astype(F32)

    def glu_forward(l, src, dst):
        for q in range(NQ):
            for d in peers:
                seq_wait(1, me ^ d, q, YR.at[l, me ^ d, rows_of(q)])

        def act(i, sq):
            rows = pl.ds(pl.multiple_of(i * CHUNK, CHUNK), CHUNK)
            valid = valid_of(i)
            for g in range(CG):
                m = mixed_of(l, g, rows)
                a = 0.5 * m * (1.0 + gelu_parts(m))
                low = a.astype(BF16)
                LA[l, rows, g * LANES : (g + 1) * LANES] = low
                AF[rows, g * LANES : (g + 1) * LANES] = low.astype(F32)
                sq = sq + rows8(a * a * valid)
            return sq

        zero = jnp.zeros((8, LANES), F32)
        if l:
            act_copy(l - 1).wait_send()
        sq_act = lax.fori_loop(0, TL // CHUNK, act, zero)
        act_copy(l).start()
        PJ[l] = jnp.dot(LA[l], W[l], preferred_element_type=F32) + bias_ref[l : l + 1, :]

        def gate(i, sq):
            sq_b, sq_s, cnt = sq
            rows = pl.ds(pl.multiple_of(i * CHUNK, CHUNK), CHUNK)
            valid = valid_of(i)
            for g in range(CG):
                cols = slice(g * LANES, (g + 1) * LANES)
                gcols = slice(D + g * LANES, D + (g + 1) * LANES)
                branch = PJ[l, rows, cols] * sigmoid(PJ[l, rows, gcols]) * valid
                out = src[rows, cols] + branch
                dst[rows, cols] = out
                sq_b = sq_b + rows8(branch * branch)
                sq_s = sq_s + rows8(out * out * valid)
            cnt = cnt + rows8(jnp.broadcast_to(valid, (CHUNK, LANES)))
            return sq_b, sq_s, cnt

        sq_b, sq_s, cnt = lax.fori_loop(0, TL // CHUNK, gate, (zero, zero, zero))
        for k, v in enumerate((sq_act, sq_b, sq_s, cnt)):
            ST[l, k] = v

    def gate_backward(l, gsrc):
        def gate(i, acc):
            rows = pl.ds(pl.multiple_of(i * CHUNK, CHUNK), CHUNK)
            valid = valid_of(i)
            out = []
            for g in range(CG):
                cols = slice(g * LANES, (g + 1) * LANES)
                gcols = slice(D + g * LANES, D + (g + 1) * LANES)
                gb = gsrc[rows, cols] * valid
                s = sigmoid(PJ[l, rows, gcols])
                one = gb * s
                two = one * PJ[l, rows, cols] * (1.0 - s)
                low_one, low_two = one.astype(BF16), two.astype(BF16)
                LG[rows, cols] = low_one
                LG[rows, gcols] = low_two
                GF[0, rows, cols] = low_one.astype(F32)
                GF[1, rows, cols] = low_two.astype(F32)
                out.append((rows8(one), rows8(two)))
            return tuple(a + b for a, b in zip(acc, [o[0] for o in out] + [o[1] for o in out]))

        zero = jnp.zeros((8, LANES), F32)
        if l < L - 1:
            grad_copy(l + 1).wait_send()
        bias = lax.fori_loop(0, TL // CHUNK, gate, (zero,) * CB)
        grad_copy(l).start()
        return bias

    def act_backward(l, bias):
        GA[...] = lax.dot_general(LG[...], W[l], (((1,), (1,)), ((), ())), preferred_element_type=F32)

        def act(i, _):
            rows = pl.ds(pl.multiple_of(i * CHUNK, CHUNK), CHUNK)
            for g in range(CG):
                m = mixed_of(l, g, rows)
                th = gelu_parts(m)
                slope = 0.5 * (1.0 + th) + 0.5 * m * (1.0 - th * th) * GELU_K * (1.0 + 3 * 0.044715 * m * m)
                GS[l, g, rows, :] = GA[rows, g * LANES : (g + 1) * LANES] * slope
            return 0

        lax.fori_loop(0, TL // CHUNK, act, 0)
        extra = [jnp.sum(b, axis=0, keepdims=True) for b in bias]
        extra += [jnp.sum(ST[l, k], axis=0, keepdims=True) for k in range(4)]
        extra += [jnp.zeros((EXTRA - len(extra), LANES), F32)]
        extra = jnp.concatenate(extra, axis=0)
        for g in range(CG):
            GS[l, g, TL : TL + EXTRA, :] = extra
        for q in range(NQ - 1, -1, -1):
            rows = rows_of(q, EXTRA if q == NQ - 1 else 0)
            for d in peers:
                j = me ^ d
                seq_copy(2, j, q, GS.at[l, j // NSP, rows], GMR.at[l, me, rows]).start()
        GMR[l, me] = GS[l, cg]

    def weight_grad(l):
        if l == L - 1:
            act_copy(l).wait_send()
        act_copy(l).wait_recv()
        grad_copy(l).wait_recv()

        def cast(i, _):
            rows = pl.ds(pl.multiple_of(i * CHUNK, CHUNK), CHUNK)
            also = pl.ds(pl.multiple_of(TL + i * CHUNK, CHUNK), CHUNK)
            LA2[rows, :] = LA[l, rows, :]
            LA2[also, :] = AR[l, rows, :].astype(BF16)
            LG2[rows, :] = GF[side, rows, :].astype(BF16)
            LG2[also, :] = GFR[l, rows, :].astype(BF16)
            return 0

        lax.fori_loop(0, TL // CHUNK, cast, 0)
        half = lax.dot_general(LA2[...], LG2[...], (((0,), (0,)), ((), ())), preferred_element_type=F32)
        for q in range(CB // 2):
            FB[l, pl.ds(q * D, D), :] = half[:, q * LANES : (q + 1) * LANES]

    def scan_backward(l, steps):
        gain = gain_ref[l : l + 1, clane]
        o2 = o2_ref[l : l + 1, clane]
        stp = step_ref[l : l + 1, clane]
        skip = skip_ref[l : l + 1, clane]
        row_id = lax.broadcasted_iota(jnp.int32, (TB, LANES), 0)
        zero8 = jnp.zeros((8, LANES), F32)
        zeros = jnp.zeros((NL, LANES), F32)
        for v in range(4):
            VEC[v] = zero8

        def with_grads(k, q, what):
            for last in (False, True):

                @pl.when((k != me) & ((q == NQ - 1) == last))
                def _():
                    what(rows_of(NQ - 1, EXTRA) if last else rows_of(q))

        def block(bb, carry):
            nu, acc, gdc, after = carry
            b = S * NQ - 1 - bb
            k, q = b // NQ, lax.rem(b, NQ)
            here, t0 = span(k, q), b * TB
            with_grads(k, q, lambda rows: seq_wait(2, k, q, GMR.at[l, k, rows]))
            na, wt = NA[l], WT[l]

            def inner(ii, c):
                nu, acc, gdc = c
                i = TB // UN - 1 - ii
                for s in range(UN - 1, -1, -1):
                    t = i * UN + s
                    logs = na * R[l, pl.ds(t0 + t, 1), :]
                    gm = GMR[l, k, pl.ds(q * TB + t, 1), :]
                    mu = wt * gm + nu
                    if l == 0:
                        acc = acc + gm * SIG[l, t0 + t + 1]
                    at = pl.ds(pl.multiple_of(t * 8, 8), 8)
                    P1[at, :] = rows8(mu)
                    nu = jnp.exp2(logs) * mu
                    part = nu * SIG[l, t0 + t] * logs
                    gdc = gdc + part
                    P2[at, :] = rows8(part)
                return nu, acc, gdc

            nu, acc, gdc = lax.fori_loop(0, TB // UN, inner, (nu, acc, gdc))
            for j in range(TB // 8):
                one = P1[pl.ds(j * 64, 8, stride=8), :]
                two = P2[pl.ds(j * 64, 8, stride=8), :]
                for s in range(1, 8):
                    one = one + P1[pl.ds(j * 64 + s, 8, stride=8), :]
                    two = two + P2[pl.ds(j * 64 + s, 8, stride=8), :]
                GX[pl.ds(pl.multiple_of(t0 + j * 8, 8), 8), :] = one
                GA[j * 8 : j * 8 + 8, 0:LANES] = two
            xhat = XR[l, here, :]
            normed = xhat * gain
            before = XR[l, pl.ds(jnp.maximum(t0 - 1, 0), 1), :] * gain
            before = jnp.where(b == 0, 0.0, before)
            prev = jnp.where(row_id == 0, before, pltpu.roll(normed, 1, 0))
            gm = GMR[l, k, rows_of(q), :] * first_part
            gdrv = GX[here, :] + skip * gm
            both = gdrv * normed
            h = o2 * both
            later = jnp.where(row_id == TB - 1, after, pltpu.roll(h, TB - 1, 0))
            rate = R[l, here, :]
            some = rate > 1e-30
            ratio = jnp.where(some, sigmoid(stp * normed) / jnp.where(some, rate, 1.0), 1.0)
            slope = GA[0:TB, 0:LANES] * LN2 * ratio
            gnormed = gdrv * (1.0 + o2 * prev) + later + slope * stp
            GX[here, :] = gnormed * gain
            VEC[0] = VEC[0] + rows8(gm * (normed + o2 * normed * prev))
            VEC[1] = VEC[1] + rows8(both * prev)
            VEC[2] = VEC[2] + rows8(slope * normed)
            VEC[3] = VEC[3] + rows8(gnormed * xhat)

            @pl.when(k == me)
            def _():
                GXR[l, me, rows_of(q), :] = GX[here, :]

            with_grads(k, q, lambda rows: seq_copy(2, k, q, GS.at[l, 0, rows], GMR.at[l, me, rows]).wait_send())

            @pl.when(k != me)
            def _():
                seq_copy(3, k, q, GX.at[here], GXR.at[l, me, rows_of(q)]).start()

            for place in sorted(steps):

                @pl.when(bb == place)
                def _(todo=steps[place]):
                    for step in todo:
                        step()

            return nu, acc, gdc, h[0:1, :]

        carry = (zeros, zeros, zeros, jnp.zeros((1, LANES), F32))
        _, acc, gdc, _ = lax.fori_loop(0, S * NQ, block, carry)
        for q in range(NQ):
            for d in peers:
                here = span(me ^ d, q)
                sends.append(seq_copy(3, me ^ d, q, GX.at[here], GXR.at[l, me, rows_of(q)]).wait_send)
        gdc = gdc / NA[l]
        base = l * SB_LAYER
        SBW[base + NL : base + 2 * NL, :] = gdc
        if l == 0:
            SBW[base : base + NL, :] = acc
        vec = [jnp.sum(VEC[v], axis=0, keepdims=True) for v in range(4)]
        SBW[base + 2 * NL : base + 2 * NL + 4, :] = jnp.concatenate(vec, axis=0)
        extra = GMR[l, 0, TL : TL + 12, :]
        for k in range(1, S):
            extra = extra + GMR[l, k, TL : TL + 12, :]
        SBW[base + 2 * NL + 4 : base + SB_LAYER, :] = extra

    def late_sum(l):
        def step(i, acc):
            for s in range(8):
                t = i * 8 + s
                acc = acc + GMR[l, i // (TL // 8), pl.ds(lax.rem(i, TL // 8) * 8 + s, 1), :] * SIG[l, t + 1]
            return acc

        SBW[l * SB_LAYER : l * SB_LAYER + NL, :] = lax.fori_loop(0, S * TL // 8, step, jnp.zeros((NL, LANES), F32))

    class Small:
        def __init__(self, first):
            self.after = [(first, first.n)]
            self.todo = [self.begin, self.join, self.across]
            self.todo += [functools.partial(self.along, i) for i in range(len(bits_of(S)))]

        def part(self, j):
            return pl.ds(pl.multiple_of(j * SP, 8), SP)

        def rs(self, j, slot):
            return pltpu.make_async_remote_copy(
                src_ref=SBW.at[self.part(j)],
                dst_ref=SBR.at[slot],
                send_sem=sb_ssem.at[j],
                recv_sem=sb_rsem.at[0, slot],
                device_id=(me, j),
                device_id_type=MESH,
            )

        def ag(self, j, slot):
            rows = self.part(slot)
            return pltpu.make_async_remote_copy(
                src_ref=SBG.at[me, rows],
                dst_ref=SBG.at[me, rows],
                send_sem=sb_ssem.at[j],
                recv_sem=sb_rsem.at[1, slot],
                device_id=(me, j),
                device_id_type=MESH,
            )

        def seq(self, i, slot):
            return pltpu.make_async_remote_copy(
                src_ref=SBG.at[slot],
                dst_ref=SBG.at[slot],
                send_sem=sg_ssem.at[slot],
                recv_sem=sg_rsem.at[slot],
                device_id=(me ^ (S >> (i + 1)), bi),
                device_id_type=MESH,
            )

        def begin(self):
            if SB_ROWS > L * SB_LAYER:
                SBW[L * SB_LAYER :, :] = jnp.zeros((SB_ROWS - L * SB_LAYER, LANES), F32)
            for d in range(B - 1, 0, -1):
                self.rs(bi ^ d, bi).start()
            SBR[bi] = SBW[self.part(bi), :]

        def join(self):
            for d in range(B - 1, 0, -1):
                self.rs(bi ^ d, bi ^ d).wait()
            total = SBR[0]
            for j in range(1, B):
                total = total + SBR[j]
            SBG[me, self.part(bi), :] = total
            for d in range(B - 1, 0, -1):
                self.ag(bi ^ d, bi).start()

        def across(self):
            for d in range(B - 1, 0, -1):
                self.ag(bi ^ d, bi ^ d).wait()
            self.seq(0, me).start()

        def slots(self, i):
            held = [me]
            for k in range(i):
                held = held + [slot ^ (S >> (k + 1)) for slot in held]
            return held

        def along(self, i):
            step = S >> (i + 1)
            for slot in self.slots(i):
                self.seq(i, slot).wait_send()
                self.seq(i, slot ^ step).wait_recv()
            if i + 1 < len(bits_of(S)):
                for slot in self.slots(i + 1):
                    self.seq(i + 1, slot).start()
            else:
                for l in range(L):
                    self.gathered(l)

        def gathered(self, l):
            base = l * SB_LAYER
            for g in range(CG):
                cols = slice(g * LANES, (g + 1) * LANES)
                vec = None
                for h in range(NSP):
                    slot = g * NSP + h
                    rows = slice(h * NL, (h + 1) * NL)
                    acc = SBG[slot, base : base + NL, :]
                    gin_out[l, rows, cols] = OUTM[l, rows, cols] * acc
                    gout_out[l, rows, cols] = INM[l, rows, cols] * acc
                    gdec_out[l, rows, cols] = -SBG[slot, base + NL : base + 2 * NL, :]
                    part = SBG[slot, base + 2 * NL : base + 2 * NL + 4, :]
                    vec = part if vec is None else vec + part
                gskip_out[l : l + 1, cols] = vec[0:1]
                go2_out[l : l + 1, cols] = vec[1:2]
                gstep_out[l : l + 1, cols] = vec[2:3]
                ggain_out[l : l + 1, cols] = vec[3:4]
            base += 2 * NL + 4
            for q in range(CB):
                gbias_out[l : l + 1, q * LANES : (q + 1) * LANES] = SBG[0, base + q : base + q + 1, :]
            sq = jnp.sum(SBG[0, base + CB : base + CB + 4, :], axis=1, keepdims=True)
            count = sq[3:4] * (1.0 / LANES)
            root = jnp.sqrt(sq[0:3] / (count * D))
            col = lax.broadcasted_iota(jnp.int32, (1, 3), 1)
            stats_out[l : l + 1, :] = jnp.where(col == 0, root[0:1], jnp.where(col == 1, root[1:2], root[2:3]))

    def norm_backward(l, gsrc, gdst):
        for q in range(NQ):
            for d in peers:
                seq_wait(3, me ^ d, q, GXR.at[l, me ^ d, rows_of(q)])

        def step(i, _):
            rows = pl.ds(pl.multiple_of(i * CHUNK, CHUNK), CHUNK)
            inv = RSTD[l, rows, :]
            gx, xh = [], []
            s1 = s2 = None
            for g in range(CG):
                v = GXR[l, g * NSP, rows, :]
                for h in range(1, NSP):
                    v = v + GXR[l, g * NSP + h, rows, :]
                x = XS[l, g, rows, :]
                gx.append(v)
                xh.append(x)
                s1 = v if s1 is None else s1 + v
                s2 = v * x if s2 is None else s2 + v * x
            m1 = jnp.sum(s1, axis=-1, keepdims=True) * (1.0 / D)
            m2 = jnp.sum(s2, axis=-1, keepdims=True) * (1.0 / D)
            for g in range(CG):
                cols = slice(g * LANES, (g + 1) * LANES)
                gdst[rows, cols] = gsrc[rows, cols] + inv * (gx[g] - m1 - xh[g] * m2)
            return 0

        lax.fori_loop(0, TL // CHUNK, step, 0)

    loads[0].wait()
    norm_forward(0, x_ref)
    pl.semaphore_wait(barrier, len(partners))
    send_normed(0)
    for c in loads[1:]:
        c.wait()
    nrows = pl.ds(pl.multiple_of(n0, 8), NL)
    for l in range(L):
        NA[l] = DEC[l, nrows, clane] * (-LOG2E)
        WT[l] = INM[l, nrows, clane] * OUTM[l, nrows, clane]
    streams = [x_ref] + [STR.at[l] for l in range(L - 1)] + [y_out]
    for l in range(L):
        if l:
            norm_forward(l, streams[l])
            send_normed(l)
        scan_forward(l)
        glu_forward(l, streams[l], streams[l + 1])
        sent()

    grads = [gx_out] + [GRD.at[l] for l in range(L - 1)] + [ct_ref]
    def take(things):
        steps = []
        for t in things:
            if t.todo and all(len(a.todo) <= left for a, left in t.after):
                steps.append(t.todo.pop(0))
        return steps

    def run(*things):
        for step in take(things):
            step()

    def places(plan):
        return {(i + 1) * S * NQ // len(plan) - 1: take(things) for i, things in enumerate(plan) if things}

    bigs = []
    for l in range(L - 1, -1, -1):
        bias = gate_backward(l, grads[l + 1])
        act_backward(l, bias)
        weight_grad(l)
        above = list(bigs)
        bigs.insert(0, Reduce(l))
        run(bigs[0])
        if above:
            late_sum(l + 1)
            scan_backward(l, places([above, bigs[:1], above, bigs[:1], above, [], [], bigs[:1]]))
        else:
            scan_backward(l, places([[], bigs, [], []]))
        if l == 0:
            small = Small(bigs[-1])
            run(small)
        norm_backward(l, grads[l + 1], grads[l])
        sent()
        run(*bigs)
    grad_copy(0).wait_send()
    while any(t.todo for t in bigs + [small]):
        run(bigs[0], small, *bigs[1:])


def hand_on(*refs):
    n = (len(refs) - 2) // 2
    sem, block_sem = refs[-2], refs[-1]
    copies = []
    for i, (a, o) in enumerate(zip(refs[:n], refs[n : 2 * n])):
        if a.shape == o.shape:
            copies.append(pltpu.make_async_copy(a, o, sem.at[i]))
            continue
        layers, rows, columns = o.shape
        for l in range(layers):
            for c in range(columns // LANES):
                block = o.at[l, :, pl.ds(c * LANES, LANES)]
                side, at = divmod(c * rows, a.shape[2])
                copies.append(pltpu.make_async_copy(a.at[l, side, pl.ds(at, rows)], block, block_sem.at[l, c]))
    for c in copies:
        c.start()
    for c in copies:
        c.wait()


def per_device(
    stream_in, cotangent, lengths, norm_gain, decay_rate, in_map, out_map, skip_gain, order_two, step_gain, glu_weight, glu_bias
):
    S, B = lax.axis_size("seq"), lax.axis_size("batch")
    _, TL, D = stream_in.shape
    L, NS = decay_rate.shape[:2]
    UN = math.gcd(TL // PIECES, 32)
    CG, E2 = D // LANES, 2 * D
    NL = NS // (S // CG)
    TA = S * TL
    CB = E2 // LANES
    GROWS = D * CB
    SBR = small_rows(L, NL, B)
    NB, NST = len(bits_of(B)), len(bits_of(B)) + len(bits_of(S))
    shape = jax.ShapeDtypeStruct
    vmem = pl.BlockSpec(memory_space=pltpu.VMEM)
    hbm = pl.BlockSpec(memory_space=pl.ANY)
    buf = pltpu.VMEM
    dma = pltpu.SemaphoreType.DMA
    outs = pl.pallas_call(
        functools.partial(kernel, (S, B, TL, D, NS, L, UN)),
        out_shape=[
            buf((TL, D), F32), buf((TL, D), F32), buf((L, D), F32),
            buf((L, NS, D), F32), buf((L, NS, D), F32), buf((L, NS, D), F32),
            buf((L, D), F32), buf((L, D), F32), buf((L, D), F32),
            buf((L, 2, GROWS // 2, LANES), F32), buf((L, E2), F32), buf((L, 3), F32),
        ],
        in_specs=[hbm] * 12,
        out_specs=[vmem] * 12,
        scratch_shapes=[
            buf((TL, D), F32), buf((TL, D), F32), pltpu.SMEM((1,), jnp.int32), buf((L, D), F32),
            buf((L, NS, D), F32), buf((L, NS, D), F32), buf((L, NS, D), F32),
            buf((L, D), F32), buf((L, D), F32), buf((L, D), F32), buf((L, D, E2), BF16), buf((L, E2), F32),
            buf((L, NL, LANES), F32), buf((L, NL, LANES), F32),
            buf((L, CG, TL, LANES), F32), buf((L, TA, LANES), F32), buf((L, TL, LANES), F32),
            buf((L, TA, LANES), F32), buf((TA, LANES), F32),
            buf((L, S, TL, LANES), F32), buf((L, CG, TL + EXTRA, LANES), F32), buf((L, S, TL + EXTRA, LANES), F32),
            buf((L, S, TL, LANES), F32),
            buf((L, TA + 1, NL, LANES), F32), buf((TL * 8, LANES), F32), buf((max(TL * 8, TA), LANES), F32),
            buf((L, TL, D), BF16), buf((L, TL, E2), F32), buf((TL, E2), BF16), buf((TL, D), F32),
            buf((L - 1, TL, D), F32), buf((L - 1, TL, D), F32), buf((L, 4, 8, LANES), F32),
            buf((L, GROWS // 2, LANES), F32), buf((L, GROWS // 2, LANES), F32),
            buf((TL, D), F32), buf((L, TL, D), F32), buf((2, TL, D), F32), buf((L, TL, D), F32), buf((2 * TL, D), BF16), buf((2 * TL, D), BF16),
            buf((SBR, LANES), F32), buf((B, SBR // B, LANES), F32), buf((S, SBR, LANES), F32),
            buf((4, 8, LANES), F32),
            dma((12,)), dma((S, PIECES)), dma((2, S, PIECES)), dma((L, CHAINS)), dma((L, CHAINS, 2 * NST - 1)),
            dma((B,)), dma((2, B)), dma((S,)), dma((S,)), dma((2,)), dma((2, L)),
        ],
        compiler_params=pltpu.CompilerParams(
            collective_id=0, has_side_effects=True, vmem_limit_bytes=57 * 2**20
        ),
        name="liquid_layers",
    )(
        stream_in[0], cotangent[0], lengths, norm_gain, decay_rate, in_map, out_map,
        skip_gain, order_two, step_gain, glu_weight, glu_bias,
    )
    outs = pl.pallas_call(
        hand_on,
        out_shape=[shape((L, D, E2), F32) if o.ndim == 4 else shape(o.shape, F32) for o in outs],
        in_specs=[vmem] * len(outs),
        out_specs=[hbm] * len(outs),
        scratch_shapes=[dma((len(outs),)), dma((L, CB))],
        compiler_params=pltpu.CompilerParams(vmem_limit_bytes=2**20),
        name="results",
    )(*outs)
    return (outs[0][None], outs[1][None], *outs[2:])


def solution(mesh):
    split = P("batch", "seq", None)
    in_specs = (split, split, P("batch")) + (P(),) * 9
    out_specs = (split, split) + (P(),) * 10
    return jax.shard_map(per_device, mesh=mesh, in_specs=in_specs, out_specs=out_specs, check_vma=False)
```

```python
import functools
import math

import jax
import jax.numpy as jnp
from jax import lax
from jax.experimental import pallas as pl
from jax.experimental.pallas import tpu as pltpu
from jax.sharding import PartitionSpec as P

MESH = pl.DeviceIdType.MESH
EPSILON = 1e-05
LOG2E = 1.4426950408889634
LN2 = 0.6931471805599453
GELU_K = math.sqrt(2.0 / math.pi)
F32 = jnp.float32
BF16 = jnp.bfloat16
LANES = 128
CHUNK = 32
CHAINS = 6
UROWS = 256
PIECES = 4
EXTRA = 16


def rows8(v):
    return v.reshape(v.shape[0] // 8, 8, v.shape[1]).sum(0)


def sigmoid(v):
    return 1.0 / (1.0 + jnp.exp(-v))


def gelu_parts(m):
    th = jnp.tanh(GELU_K * (m + 0.044715 * m * m * m))
    return th


def bits_of(n):
    return [i for i in range(n.bit_length() - 1)]


def orders(seq, batch, chains, upper):
    s = [("seq", b) for b in bits_of(seq)]
    b = [("batch", b) for b in bits_of(batch)]
    x, y, z, rest = s[1:2], b[:1], b[1:2], b[2:] + s[2:]
    kinds = [y + z + x, z + y + x] if upper else [x + y + z, y + z + x, z + x + y]
    return [kinds[c % len(kinds)] + rest for c in range(chains)]


def chain_rows(rows, devices, most):
    unit = 8 * devices
    units = rows // unit
    chains = min(most, units)
    cut = [units // chains + (1 if c < units % chains else 0) for c in range(chains)]
    return [(sum(cut[:c]) * unit, cut[c] * unit) for c in range(chains)]


def small_rows(layers, states, batch):
    unit = 8 * batch
    return -(-layers * (2 * states + EXTRA) // unit) * unit


def kernel(cfg, *refs):
    S, B, TL, D, NS, L, UN = cfg
    CG = D // LANES
    NSP = S // CG
    NL = NS // NSP
    E2 = 2 * D
    CB = E2 // LANES
    GROWS = D * CB
    NQ = PIECES
    TB = TL // NQ
    SB_LAYER = 2 * NL + EXTRA
    SB_ROWS = small_rows(L, NL, B)
    SP = SB_ROWS // B
    spans = chain_rows(GROWS // 2, S * B // 2, CHAINS)
    (
        x_hbm, ct_hbm, len_hbm, gain_hbm, dec_hbm, in_hbm, out_hbm, skip_hbm, o2_hbm, step_hbm, w_hbm, bias_hbm,
        y_out, gx_out, ggain_out, gdec_out, gin_out, gout_out, gskip_out, go2_out, gstep_out, FG, gbias_out, stats_out,
        x_ref, ct_ref, len_ref, gain_ref, DEC, INM, OUTM, skip_ref, o2_ref, step_ref, W, bias_ref, NA, WT,
        XS, XR, RSTD, R, Y, YR, GS, GMR, GXR,
        SIG, P1, P2, LA, PJ, LG, GA, STR, GRD, ST,
        FB, RB, AF, AR, GF, GFR, LA2, LG2, SBW, SBR, SBG, VEC,
        load_sem, send_sem, recv_sem, ar_ssem, ar_rsem, sb_ssem, sb_rsem, sg_ssem, sg_rsem, pair_ssem, pair_rsem,
    ) = refs
    U, GX = P2, Y
    me = lax.axis_index("seq")
    bi = lax.axis_index("batch")
    cg = me // NSP
    nh = lax.rem(me, NSP)
    n0 = nh * NL
    first_part = (nh == 0).astype(F32)
    clane = pl.ds(pl.multiple_of(cg * LANES, LANES), LANES)

    sources = (x_hbm, len_hbm, gain_hbm, o2_hbm, step_hbm, dec_hbm, in_hbm, out_hbm, skip_hbm, w_hbm, bias_hbm, ct_hbm)
    targets = (x_ref, len_ref, gain_ref, o2_ref, step_ref, DEC, INM, OUTM, skip_ref, W, bias_ref, ct_ref)
    loads = [pltpu.make_async_copy(h, v, load_sem.at[i]) for i, (h, v) in enumerate(zip(sources, targets))]
    for c in loads:
        c.start()

    barrier = pltpu.get_barrier_semaphore()
    partners = [(me ^ d, bi) for d in range(1, S)]
    partners += [(me ^ 1, bi ^ (1 << b)) for b in bits_of(B)]
    for p in partners:
        pl.semaphore_signal(barrier, inc=1, device_id=p, device_id_type=MESH)

    sends = []

    def sent():
        while sends:
            sends.pop(0)()

    def seq_copy(ph, j, q, src, dst):
        return pltpu.make_async_remote_copy(
            src_ref=src,
            dst_ref=dst,
            send_sem=send_sem.at[j, q],
            recv_sem=recv_sem.at[ph % 2, me, q],
            device_id=(j, bi),
            device_id_type=MESH,
        )

    def seq_wait(ph, k, q, ref):
        pltpu.make_async_remote_copy(
            src_ref=ref,
            dst_ref=ref,
            send_sem=send_sem.at[k, q],
            recv_sem=recv_sem.at[ph % 2, k, q],
            device_id=(k, bi),
            device_id_type=MESH,
        ).wait_recv()

    def rows_of(q):
        return pl.ds(q * TB if isinstance(q, int) else pl.multiple_of(q * TB, TB), TB)

    def span(k, q):
        return pl.ds(pl.multiple_of((k * NQ + q) * TB, TB), TB)

    peers = list(range(S - 1, 0, -1))

    def tblock(k):
        return pl.ds(pl.multiple_of(k * TL, TL), TL)

    def bit_of(v, bit):
        return lax.rem(v // (1 << bit), 2)

    def swap(axis, bit):
        if axis == "batch":
            return (me ^ 1, bi ^ (1 << bit))
        return (me ^ (1 << bit) ^ 1, bi)

    def my_bit(axis, bit):
        return bit_of(me if axis == "seq" else bi, bit)

    side = lax.rem(sum(bit_of(me, i) for i in bits_of(S)) + sum(bit_of(bi, i) for i in bits_of(B)), 2)

    def pair_copy(which, l, src, dst):
        return pltpu.make_async_remote_copy(
            src_ref=src,
            dst_ref=dst,
            send_sem=pair_ssem.at[which],
            recv_sem=pair_rsem.at[which, l],
            device_id=(me ^ 1, bi),
            device_id_type=MESH,
        )

    def act_copy(l):
        return pair_copy(0, l, AF, AR.at[l])

    def grad_copy(l):
        return pair_copy(1, l, GF.at[1 - side], GFR.at[l])

    class Reduce:
        after = ()

        def __init__(self, l):
            self.l = l
            self.chains = []
            plans = orders(S, B, len(spans), l > 0)
            for (base, rows), plan in zip(spans, plans):
                off, size, roff, stages = base, rows, base, []
                for i, (axis, bit) in enumerate(plan):
                    half = size // 2
                    mine = my_bit(axis, bit)
                    keep = pl.multiple_of(off + mine * half, 8)
                    give = pl.multiple_of(off + (1 - mine) * half, 8)
                    stages.append((i, axis, bit, half, keep, give, roff))
                    off, size, roff = keep, half, roff + half
                self.chains.append(stages)
            self.n = n = len(plans[0])
            self.todo = [self.begin]
            self.todo += [functools.partial(self.reduce_step, i) for i in range(n)]
            self.todo += [functools.partial(self.gather_step, i) for i in range(n - 1, -1, -1)]
            self.todo += [self.last_step]

        def rs(self, c, stage):
            i, axis, bit, half, keep, give, roff = stage
            return pltpu.make_async_remote_copy(
                src_ref=FB.at[self.l, pl.ds(give, half)],
                dst_ref=RB.at[self.l, pl.ds(roff, half)],
                send_sem=ar_ssem.at[self.l, c],
                recv_sem=ar_rsem.at[self.l, c, i],
                device_id=swap(axis, bit),
                device_id_type=MESH,
            )

        def pair(self, c):
            base, rows = spans[c]
            here = FG.at[self.l, side, pl.ds(base, rows)]
            return pltpu.make_async_remote_copy(
                src_ref=here,
                dst_ref=here,
                send_sem=ar_ssem.at[self.l, c],
                recv_sem=ar_rsem.at[self.l, c, 2 * self.n],
                device_id=(me ^ 1, bi),
                device_id_type=MESH,
            )

        def ag(self, c, stage):
            i, axis, bit, half, keep, give, roff = stage
            here = FG.at[self.l, side, pl.ds(keep, half)]
            return pltpu.make_async_remote_copy(
                src_ref=here,
                dst_ref=here,
                send_sem=ar_ssem.at[self.l, c],
                recv_sem=ar_rsem.at[self.l, c, self.n + i],
                device_id=swap(axis, bit),
                device_id_type=MESH,
            )

        def begin(self):
            for c, stages in enumerate(self.chains):
                self.rs(c, stages[0]).start()

        def reduce_step(self, i):
            for c, stages in enumerate(self.chains):
                _, _, _, half, keep, _, roff = stages[i]
                self.rs(c, stages[i]).wait()
                step = math.gcd(half, 64)

                def add(j, _, i=i, keep=keep, roff=roff, step=step):
                    at = pl.ds(pl.multiple_of(keep + j * step, 8), step)
                    total = FB[self.l, at, :] + RB[self.l, pl.ds(pl.multiple_of(roff + j * step, 8), step), :]
                    if i + 1 < self.n:
                        FB[self.l, at, :] = total
                    else:
                        FG[self.l, side, at, :] = total
                    return 0

                lax.fori_loop(0, half // step, add, 0)
                if i + 1 < self.n:
                    self.rs(c, stages[i + 1]).start()
                else:
                    self.ag(c, stages[i]).start()

        def gather_step(self, i):
            for c, stages in enumerate(self.chains):
                self.ag(c, stages[i]).wait()
                if i > 0:
                    self.ag(c, stages[i - 1]).start()
                else:
                    self.pair(c).start()

        def last_step(self):
            for c in range(len(self.chains)):
                self.pair(c).wait()

    def norm_forward(l, src):
        def step(i, _):
            rows = pl.ds(pl.multiple_of(i * CHUNK, CHUNK), CHUNK)
            x = src[rows, :]
            center = x - jnp.mean(x, axis=-1, keepdims=True)
            spread = jnp.mean(center * center, axis=-1, keepdims=True)
            inv = lax.rsqrt(spread + EPSILON)
            xhat = center * inv
            RSTD[l, rows, :] = jnp.broadcast_to(inv, (CHUNK, LANES))
            for g in range(CG):
                XS[l, g, rows, :] = xhat[:, g * LANES : (g + 1) * LANES]
            return 0

        lax.fori_loop(0, TL // CHUNK, step, 0)

    def send_normed(l):
        for q in range(NQ):
            for d in peers:
                j = me ^ d
                seq_copy(0, j, q, XS.at[l, j // NSP, rows_of(q)], XR.at[l, span(me, q)]).start()
        XR[l, tblock(me), :] = XS[l, cg]

    def scan_forward(l):
        gain = gain_ref[l : l + 1, clane]
        o2 = o2_ref[l : l + 1, clane]
        stp = step_ref[l : l + 1, clane]
        skip = skip_ref[l : l + 1, clane] * first_part
        first_row = lax.broadcasted_iota(jnp.int32, (TB, LANES), 0) == 0
        SIG[l, 0] = jnp.zeros((NL, LANES), F32)

        def block(b, carry):
            sig, last = carry
            k, q = b // NQ, lax.rem(b, NQ)
            here, t0 = span(k, q), b * TB

            @pl.when(k != me)
            def _():
                seq_wait(0, k, q, XR.at[l, here])

            normed = XR[l, here, :] * gain
            prev = jnp.where(first_row, last, pltpu.roll(normed, 1, 0))
            U[here, :] = normed + o2 * normed * prev
            z = stp * normed
            R[l, here, :] = jnp.maximum(z, 0.0) + jnp.log1p(jnp.exp(-jnp.abs(z)))
            na, wt = NA[l], WT[l]

            def inner(i, sig):
                for s in range(UN):
                    t = i * UN + s
                    at = pl.ds(t0 + t, 1)
                    sig = jnp.exp2(na * R[l, at, :]) * sig + U[at, :]
                    SIG[l, t0 + t + 1] = sig
                    P1[pl.ds(pl.multiple_of(t * 8, 8), 8), :] = rows8(wt * sig)
                return sig

            sig = lax.fori_loop(0, TB // UN, inner, sig)
            for j in range(TB // 8):
                total = P1[pl.ds(j * 64, 8, stride=8), :]
                for s in range(1, 8):
                    total = total + P1[pl.ds(j * 64 + s, 8, stride=8), :]
                at = pl.ds(pl.multiple_of(t0 + j * 8, 8), 8)
                Y[at, :] = total + skip * U[at, :]

            @pl.when(k != me)
            def _():
                seq_copy(0, k, q, XS.at[l, 0, rows_of(q)], XR.at[l, here]).wait_send()
                seq_copy(1, k, q, Y.at[here], YR.at[l, me, rows_of(q)]).start()

            return sig, normed[TB - 1 : TB, :]

        lax.fori_loop(0, S * NQ, block, (jnp.zeros((NL, LANES), F32), jnp.zeros((1, LANES), F32)))
        YR[l, me] = Y[tblock(me), :]
        for q in range(NQ):
            for d in peers:
                here = span(me ^ d, q)
                sends.append(seq_copy(1, me ^ d, q, Y.at[here], YR.at[l, me, rows_of(q)]).wait_send)

    def mixed_of(l, g, rows):
        m = YR[l, g * NSP, rows, :]
        for h in range(1, NSP):
            m = m + YR[l, g * NSP + h, rows, :]
        return m

    def valid_of(i):
        pos = me * TL + i * CHUNK + lax.broadcasted_iota(jnp.int32, (CHUNK, 1), 0)
        return (pos < len_ref[0]).astype(F32)

    def glu_forward(l, src, dst):
        for q in range(NQ):
            for d in peers:
                seq_wait(1, me ^ d, q, YR.at[l, me ^ d, rows_of(q)])

        def act(i, sq):
            rows = pl.ds(pl.multiple_of(i * CHUNK, CHUNK), CHUNK)
            valid = valid_of(i)
            for g in range(CG):
                m = mixed_of(l, g, rows)
                a = 0.5 * m * (1.0 + gelu_parts(m))
                low = a.astype(BF16)
                LA[l, rows, g * LANES : (g + 1) * LANES] = low
                AF[rows, g * LANES : (g + 1) * LANES] = low.astype(F32)
                sq = sq + rows8(a * a * valid)
            return sq

        zero = jnp.zeros((8, LANES), F32)
        if l:
            act_copy(l - 1).wait_send()
        sq_act = lax.fori_loop(0, TL // CHUNK, act, zero)
        act_copy(l).start()
        PJ[l] = jnp.dot(LA[l], W[l], preferred_element_type=F32) + bias_ref[l : l + 1, :]

        def gate(i, sq):
            sq_b, sq_s, cnt = sq
            rows = pl.ds(pl.multiple_of(i * CHUNK, CHUNK), CHUNK)
            valid = valid_of(i)
            for g in range(CG):
                cols = slice(g * LANES, (g + 1) * LANES)
                gcols = slice(D + g * LANES, D + (g + 1) * LANES)
                branch = PJ[l, rows, cols] * sigmoid(PJ[l, rows, gcols]) * valid
                out = src[rows, cols] + branch
                dst[rows, cols] = out
                sq_b = sq_b + rows8(branch * branch)
                sq_s = sq_s + rows8(out * out * valid)
            cnt = cnt + rows8(jnp.broadcast_to(valid, (CHUNK, LANES)))
            return sq_b, sq_s, cnt

        sq_b, sq_s, cnt = lax.fori_loop(0, TL // CHUNK, gate, (zero, zero, zero))
        for k, v in enumerate((sq_act, sq_b, sq_s, cnt)):
            ST[l, k] = v

    def gate_backward(l, gsrc):
        def gate(i, acc):
            rows = pl.ds(pl.multiple_of(i * CHUNK, CHUNK), CHUNK)
            valid = valid_of(i)
            out = []
            for g in range(CG):
                cols = slice(g * LANES, (g + 1) * LANES)
                gcols = slice(D + g * LANES, D + (g + 1) * LANES)
                gb = gsrc[rows, cols] * valid
                s = sigmoid(PJ[l, rows, gcols])
                one = gb * s
                two = one * PJ[l, rows, cols] * (1.0 - s)
                low_one, low_two = one.astype(BF16), two.astype(BF16)
                LG[rows, cols] = low_one
                LG[rows, gcols] = low_two
                GF[0, rows, cols] = low_one.astype(F32)
                GF[1, rows, cols] = low_two.astype(F32)
                out.append((rows8(one), rows8(two)))
            return tuple(a + b for a, b in zip(acc, [o[0] for o in out] + [o[1] for o in out]))

        zero = jnp.zeros((8, LANES), F32)
        if l < L - 1:
            grad_copy(l + 1).wait_send()
        bias = lax.fori_loop(0, TL // CHUNK, gate, (zero,) * CB)
        grad_copy(l).start()
        return bias

    def act_backward(l, bias):
        GA[...] = lax.dot_general(LG[...], W[l], (((1,), (1,)), ((), ())), preferred_element_type=F32)

        def act(i, _):
            rows = pl.ds(pl.multiple_of(i * CHUNK, CHUNK), CHUNK)
            for g in range(CG):
                m = mixed_of(l, g, rows)
                th = gelu_parts(m)
                slope = 0.5 * (1.0 + th) + 0.5 * m * (1.0 - th * th) * GELU_K * (1.0 + 3 * 0.044715 * m * m)
                GS[l, g, rows, :] = GA[rows, g * LANES : (g + 1) * LANES] * slope
            return 0

        lax.fori_loop(0, TL // CHUNK, act, 0)
        for q in range(NQ - 1, -1, -1):
            for d in peers:
                j = me ^ d
                seq_copy(2, j, q, GS.at[l, j // NSP, rows_of(q)], GMR.at[l, me, rows_of(q)]).start()
        GMR[l, me] = GS[l, cg]
        extra = list(bias) + [ST[l, k] for k in range(4)]
        extra = jnp.concatenate([jnp.sum(v, axis=0, keepdims=True) for v in extra], axis=0)
        base = l * SB_LAYER + 2 * NL + 4
        SBW[base : base + len(bias) + 4, :] = extra

    def weight_grad(l):
        if l == L - 1:
            act_copy(l).wait_send()
        act_copy(l).wait_recv()
        grad_copy(l).wait_recv()

        def cast(i, _):
            rows = pl.ds(pl.multiple_of(i * CHUNK, CHUNK), CHUNK)
            also = pl.ds(pl.multiple_of(TL + i * CHUNK, CHUNK), CHUNK)
            LA2[rows, :] = LA[l, rows, :]
            LA2[also, :] = AR[l, rows, :].astype(BF16)
            LG2[rows, :] = GF[side, rows, :].astype(BF16)
            LG2[also, :] = GFR[l, rows, :].astype(BF16)
            return 0

        lax.fori_loop(0, TL // CHUNK, cast, 0)
        half = lax.dot_general(LA2[...], LG2[...], (((0,), (0,)), ((), ())), preferred_element_type=F32)
        for q in range(CB // 2):
            FB[l, pl.ds(q * D, D), :] = half[:, q * LANES : (q + 1) * LANES]

    def scan_backward(l, steps):
        gain = gain_ref[l : l + 1, clane]
        o2 = o2_ref[l : l + 1, clane]
        stp = step_ref[l : l + 1, clane]
        skip = skip_ref[l : l + 1, clane]
        row_id = lax.broadcasted_iota(jnp.int32, (TB, LANES), 0)
        zero8 = jnp.zeros((8, LANES), F32)
        zeros = jnp.zeros((NL, LANES), F32)
        for v in range(4):
            VEC[v] = zero8

        def block(bb, carry):
            nu, acc, gdc, after = carry
            b = S * NQ - 1 - bb
            k, q = b // NQ, lax.rem(b, NQ)
            here, t0 = span(k, q), b * TB

            @pl.when(k != me)
            def _():
                seq_wait(2, k, q, GMR.at[l, k, rows_of(q)])

            na, wt = NA[l], WT[l]

            def inner(ii, c):
                nu, acc, gdc = c
                i = TB // UN - 1 - ii
                for s in range(UN - 1, -1, -1):
                    t = i * UN + s
                    logs = na * R[l, pl.ds(t0 + t, 1), :]
                    gm = GMR[l, k, pl.ds(q * TB + t, 1), :]
                    mu = wt * gm + nu
                    if l == 0:
                        acc = acc + gm * SIG[l, t0 + t + 1]
                    at = pl.ds(pl.multiple_of(t * 8, 8), 8)
                    P1[at, :] = rows8(mu)
                    nu = jnp.exp2(logs) * mu
                    part = nu * SIG[l, t0 + t] * logs
                    gdc = gdc + part
                    P2[at, :] = rows8(part)
                return nu, acc, gdc

            nu, acc, gdc = lax.fori_loop(0, TB // UN, inner, (nu, acc, gdc))
            for j in range(TB // 8):
                one = P1[pl.ds(j * 64, 8, stride=8), :]
                two = P2[pl.ds(j * 64, 8, stride=8), :]
                for s in range(1, 8):
                    one = one + P1[pl.ds(j * 64 + s, 8, stride=8), :]
                    two = two + P2[pl.ds(j * 64 + s, 8, stride=8), :]
                GX[pl.ds(pl.multiple_of(t0 + j * 8, 8), 8), :] = one
                GA[j * 8 : j * 8 + 8, 0:LANES] = two
            xhat = XR[l, here, :]
            normed = xhat * gain
            before = XR[l, pl.ds(jnp.maximum(t0 - 1, 0), 1), :] * gain
            before = jnp.where(b == 0, 0.0, before)
            prev = jnp.where(row_id == 0, before, pltpu.roll(normed, 1, 0))
            gm = GMR[l, k, rows_of(q), :] * first_part
            gdrv = GX[here, :] + skip * gm
            both = gdrv * normed
            h = o2 * both
            later = jnp.where(row_id == TB - 1, after, pltpu.roll(h, TB - 1, 0))
            rate = R[l, here, :]
            some = rate > 1e-30
            ratio = jnp.where(some, sigmoid(stp * normed) / jnp.where(some, rate, 1.0), 1.0)
            slope = GA[0:TB, 0:LANES] * LN2 * ratio
            gnormed = gdrv * (1.0 + o2 * prev) + later + slope * stp
            GX[here, :] = gnormed * gain
            VEC[0] = VEC[0] + rows8(gm * (normed + o2 * normed * prev))
            VEC[1] = VEC[1] + rows8(both * prev)
            VEC[2] = VEC[2] + rows8(slope * normed)
            VEC[3] = VEC[3] + rows8(gnormed * xhat)

            @pl.when(k != me)
            def _():
                seq_copy(2, k, q, GS.at[l, 0, rows_of(q)], GMR.at[l, me, rows_of(q)]).wait_send()
                seq_copy(3, k, q, GX.at[here], GXR.at[l, me, rows_of(q)]).start()

            if steps:
                hit = functools.reduce(jnp.logical_or, [bb == place for place in sorted(steps)])

                @pl.when(hit)
                def _():
                    for place in sorted(steps):

                        @pl.when(bb == place)
                        def _(todo=steps[place]):
                            for step in todo:
                                step()

            return nu, acc, gdc, h[0:1, :]

        carry = (zeros, zeros, zeros, jnp.zeros((1, LANES), F32))
        _, acc, gdc, _ = lax.fori_loop(0, S * NQ, block, carry)
        GXR[l, me] = GX[tblock(me), :]
        for q in range(NQ):
            for d in peers:
                here = span(me ^ d, q)
                sends.append(seq_copy(3, me ^ d, q, GX.at[here], GXR.at[l, me, rows_of(q)]).wait_send)
        gdc = gdc / NA[l]
        base = l * SB_LAYER
        SBW[base + NL : base + 2 * NL, :] = gdc
        if l == 0:
            SBW[base : base + NL, :] = acc
        vec = [jnp.sum(VEC[v], axis=0, keepdims=True) for v in range(4)]
        SBW[base + 2 * NL : base + 2 * NL + 4, :] = jnp.concatenate(vec, axis=0)

    def late_sum(l):
        def step(i, acc):
            for s in range(8):
                t = i * 8 + s
                acc = acc + GMR[l, i // (TL // 8), pl.ds(lax.rem(i, TL // 8) * 8 + s, 1), :] * SIG[l, t + 1]
            return acc

        SBW[l * SB_LAYER : l * SB_LAYER + NL, :] = lax.fori_loop(0, S * TL // 8, step, jnp.zeros((NL, LANES), F32))

    class Small:
        def __init__(self, first):
            self.after = [(first, first.n + 1)]
            self.todo = [self.begin, self.join, self.across]
            self.todo += [functools.partial(self.along, i) for i in range(len(bits_of(S)))]

        def part(self, j):
            return pl.ds(pl.multiple_of(j * SP, 8), SP)

        def rs(self, j, slot):
            return pltpu.make_async_remote_copy(
                src_ref=SBW.at[self.part(j)],
                dst_ref=SBR.at[slot],
                send_sem=sb_ssem.at[j],
                recv_sem=sb_rsem.at[0, slot],
                device_id=(me, j),
                device_id_type=MESH,
            )

        def ag(self, j, slot):
            rows = self.part(slot)
            return pltpu.make_async_remote_copy(
                src_ref=SBG.at[me, rows],
                dst_ref=SBG.at[me, rows],
                send_sem=sb_ssem.at[j],
                recv_sem=sb_rsem.at[1, slot],
                device_id=(me, j),
                device_id_type=MESH,
            )

        def seq(self, i, slot):
            return pltpu.make_async_remote_copy(
                src_ref=SBG.at[slot],
                dst_ref=SBG.at[slot],
                send_sem=sg_ssem.at[slot],
                recv_sem=sg_rsem.at[slot],
                device_id=(me ^ (S >> (i + 1)), bi),
                device_id_type=MESH,
            )

        def begin(self):
            if SB_ROWS > L * SB_LAYER:
                SBW[L * SB_LAYER :, :] = jnp.zeros((SB_ROWS - L * SB_LAYER, LANES), F32)
            for d in range(B - 1, 0, -1):
                self.rs(bi ^ d, bi).start()
            SBR[bi] = SBW[self.part(bi), :]

        def join(self):
            for d in range(B - 1, 0, -1):
                self.rs(bi ^ d, bi ^ d).wait()
            total = SBR[0]
            for j in range(1, B):
                total = total + SBR[j]
            SBG[me, self.part(bi), :] = total
            for d in range(B - 1, 0, -1):
                self.ag(bi ^ d, bi).start()

        def across(self):
            for d in range(B - 1, 0, -1):
                self.ag(bi ^ d, bi ^ d).wait()
            self.seq(0, me).start()

        def slots(self, i):
            held = [me]
            for k in range(i):
                held = held + [slot ^ (S >> (k + 1)) for slot in held]
            return held

        def along(self, i):
            step = S >> (i + 1)
            for slot in self.slots(i):
                self.seq(i, slot).wait_send()
                self.seq(i, slot ^ step).wait_recv()
            if i + 1 < len(bits_of(S)):
                for slot in self.slots(i + 1):
                    self.seq(i + 1, slot).start()
            else:
                for l in range(L):
                    self.gathered(l)

        def gathered(self, l):
            base = l * SB_LAYER
            for g in range(CG):
                cols = slice(g * LANES, (g + 1) * LANES)
                vec = None
                for h in range(NSP):
                    slot = g * NSP + h
                    rows = slice(h * NL, (h + 1) * NL)
                    acc = SBG[slot, base : base + NL, :]
                    gin_out[l, rows, cols] = OUTM[l, rows, cols] * acc
                    gout_out[l, rows, cols] = INM[l, rows, cols] * acc
                    gdec_out[l, rows, cols] = -SBG[slot, base + NL : base + 2 * NL, :]
                    part = SBG[slot, base + 2 * NL : base + 2 * NL + 4, :]
                    vec = part if vec is None else vec + part
                gskip_out[l : l + 1, cols] = vec[0:1]
                go2_out[l : l + 1, cols] = vec[1:2]
                gstep_out[l : l + 1, cols] = vec[2:3]
                ggain_out[l : l + 1, cols] = vec[3:4]
            base += 2 * NL + 4
            extra = SBG[0, base : base + CB + 4, :]
            for k in range(1, S):
                extra = extra + SBG[k, base : base + CB + 4, :]
            for q in range(CB):
                gbias_out[l : l + 1, q * LANES : (q + 1) * LANES] = extra[q : q + 1]
            sq = jnp.sum(extra[CB:], axis=1, keepdims=True)
            count = sq[3:4] * (1.0 / LANES)
            root = jnp.sqrt(sq[0:3] / (count * D))
            col = lax.broadcasted_iota(jnp.int32, (1, 3), 1)
            stats_out[l : l + 1, :] = jnp.where(col == 0, root[0:1], jnp.where(col == 1, root[1:2], root[2:3]))

    def norm_backward(l, gsrc, gdst):
        for q in range(NQ):
            for d in peers:
                seq_wait(3, me ^ d, q, GXR.at[l, me ^ d, rows_of(q)])

        def step(i, _):
            rows = pl.ds(pl.multiple_of(i * CHUNK, CHUNK), CHUNK)
            inv = RSTD[l, rows, :]
            gx, xh = [], []
            s1 = s2 = None
            for g in range(CG):
                v = GXR[l, g * NSP, rows, :]
                for h in range(1, NSP):
                    v = v + GXR[l, g * NSP + h, rows, :]
                x = XS[l, g, rows, :]
                gx.append(v)
                xh.append(x)
                s1 = v if s1 is None else s1 + v
                s2 = v * x if s2 is None else s2 + v * x
            m1 = jnp.sum(s1, axis=-1, keepdims=True) * (1.0 / D)
            m2 = jnp.sum(s2, axis=-1, keepdims=True) * (1.0 / D)
            for g in range(CG):
                cols = slice(g * LANES, (g + 1) * LANES)
                gdst[rows, cols] = gsrc[rows, cols] + inv * (gx[g] - m1 - xh[g] * m2)
            return 0

        lax.fori_loop(0, TL // CHUNK, step, 0)

    loads[0].wait()
    norm_forward(0, x_ref)
    pl.semaphore_wait(barrier, len(partners))
    send_normed(0)
    for c in loads[1:]:
        c.wait()
    nrows = pl.ds(pl.multiple_of(n0, 8), NL)
    for l in range(L):
        NA[l] = DEC[l, nrows, clane] * (-LOG2E)
        WT[l] = INM[l, nrows, clane] * OUTM[l, nrows, clane]
    streams = [x_ref] + [STR.at[l] for l in range(L - 1)] + [y_out]
    for l in range(L):
        if l:
            norm_forward(l, streams[l])
            send_normed(l)
        scan_forward(l)
        glu_forward(l, streams[l], streams[l + 1])
        sent()

    grads = [gx_out] + [GRD.at[l] for l in range(L - 1)] + [ct_ref]
    def take(things):
        steps = []
        for t in things:
            if t.todo and all(len(a.todo) <= left for a, left in t.after):
                steps.append(t.todo.pop(0))
        return steps

    def run(*things):
        for step in take(things):
            step()

    def places(plan):
        return {(i + 1) * S * NQ // 16 - 1: take(plan[i]) for i in sorted(plan)}

    bigs = []
    for l in range(L - 1, -1, -1):
        bias = gate_backward(l, grads[l + 1])
        act_backward(l, bias)
        weight_grad(l)
        above = list(bigs)
        bigs.insert(0, Reduce(l))
        run(bigs[0])
        if above:
            late_sum(l + 1)
            scan_backward(l, places({5: above, 12: above, 13: bigs[:1]}))
        else:
            scan_backward(l, places({11: bigs}))
        if l == 0:
            small = Small(bigs[-1])
            run(small)
        norm_backward(l, grads[l + 1], grads[l])
        sent()
        run(*bigs)
    grad_copy(0).wait_send()
    while any(t.todo for t in bigs + [small]):
        run(bigs[0], small, *bigs[1:])


def hand_on(*refs):
    n = (len(refs) - 2) // 2
    sem, block_sem = refs[-2], refs[-1]
    copies = []
    for i, (a, o) in enumerate(zip(refs[:n], refs[n : 2 * n])):
        if a.shape == o.shape:
            copies.append(pltpu.make_async_copy(a, o, sem.at[i]))
            continue
        layers, rows, columns = o.shape
        for l in range(layers):
            for c in range(columns // LANES):
                block = o.at[l, :, pl.ds(c * LANES, LANES)]
                side, at = divmod(c * rows, a.shape[2])
                copies.append(pltpu.make_async_copy(a.at[l, side, pl.ds(at, rows)], block, block_sem.at[l, c]))
    for c in copies:
        c.start()
    for c in copies:
        c.wait()


def per_device(
    stream_in, cotangent, lengths, norm_gain, decay_rate, in_map, out_map, skip_gain, order_two, step_gain, glu_weight, glu_bias
):
    S, B = lax.axis_size("seq"), lax.axis_size("batch")
    _, TL, D = stream_in.shape
    L, NS = decay_rate.shape[:2]
    UN = math.gcd(TL // PIECES, 32)
    CG, E2 = D // LANES, 2 * D
    NL = NS // (S // CG)
    TA = S * TL
    CB = E2 // LANES
    GROWS = D * CB
    SBR = small_rows(L, NL, B)
    NB, NST = len(bits_of(B)), len(bits_of(B)) + len(bits_of(S))
    shape = jax.ShapeDtypeStruct
    vmem = pl.BlockSpec(memory_space=pltpu.VMEM)
    hbm = pl.BlockSpec(memory_space=pl.ANY)
    buf = pltpu.VMEM
    dma = pltpu.SemaphoreType.DMA
    outs = pl.pallas_call(
        functools.partial(kernel, (S, B, TL, D, NS, L, UN)),
        out_shape=[
            buf((TL, D), F32), buf((TL, D), F32), buf((L, D), F32),
            buf((L, NS, D), F32), buf((L, NS, D), F32), buf((L, NS, D), F32),
            buf((L, D), F32), buf((L, D), F32), buf((L, D), F32),
            buf((L, 2, GROWS // 2, LANES), F32), buf((L, E2), F32), buf((L, 3), F32),
        ],
        in_specs=[hbm] * 12,
        out_specs=[vmem] * 12,
        scratch_shapes=[
            buf((TL, D), F32), buf((TL, D), F32), pltpu.SMEM((1,), jnp.int32), buf((L, D), F32),
            buf((L, NS, D), F32), buf((L, NS, D), F32), buf((L, NS, D), F32),
            buf((L, D), F32), buf((L, D), F32), buf((L, D), F32), buf((L, D, E2), BF16), buf((L, E2), F32),
            buf((L, NL, LANES), F32), buf((L, NL, LANES), F32),
            buf((L, CG, TL, LANES), F32), buf((L, TA, LANES), F32), buf((L, TL, LANES), F32),
            buf((L, TA, LANES), F32), buf((TA, LANES), F32),
            buf((L, S, TL, LANES), F32), buf((L, CG, TL, LANES), F32), buf((L, S, TL, LANES), F32),
            buf((L, S, TL, LANES), F32),
            buf((L, TA + 1, NL, LANES), F32), buf((TL * 8, LANES), F32), buf((max(TL * 8, TA), LANES), F32),
            buf((L, TL, D), BF16), buf((L, TL, E2), F32), buf((TL, E2), BF16), buf((TL, D), F32),
            buf((L - 1, TL, D), F32), buf((L - 1, TL, D), F32), buf((L, 4, 8, LANES), F32),
            buf((L, GROWS // 2, LANES), F32), buf((L, GROWS // 2, LANES), F32),
            buf((TL, D), F32), buf((L, TL, D), F32), buf((2, TL, D), F32), buf((L, TL, D), F32), buf((2 * TL, D), BF16), buf((2 * TL, D), BF16),
            buf((SBR, LANES), F32), buf((B, SBR // B, LANES), F32), buf((S, SBR, LANES), F32),
            buf((4, 8, LANES), F32),
            dma((12,)), dma((S, PIECES)), dma((2, S, PIECES)), dma((L, CHAINS)), dma((L, CHAINS, 2 * NST - 1)),
            dma((B,)), dma((2, B)), dma((S,)), dma((S,)), dma((2,)), dma((2, L)),
        ],
        compiler_params=pltpu.CompilerParams(
            collective_id=0, has_side_effects=True, vmem_limit_bytes=57 * 2**20
        ),
        name="liquid_layers",
    )(
        stream_in[0], cotangent[0], lengths, norm_gain, decay_rate, in_map, out_map,
        skip_gain, order_two, step_gain, glu_weight, glu_bias,
    )
    outs = pl.pallas_call(
        hand_on,
        out_shape=[shape((L, D, E2), F32) if o.ndim == 4 else shape(o.shape, F32) for o in outs],
        in_specs=[vmem] * len(outs),
        out_specs=[hbm] * len(outs),
        scratch_shapes=[dma((len(outs),)), dma((L, CB))],
        compiler_params=pltpu.CompilerParams(vmem_limit_bytes=2**20),
        name="results",
    )(*outs)
    return (outs[0][None], outs[1][None], *outs[2:])


def solution(mesh):
    split = P("batch", "seq", None)
    in_specs = (split, split, P("batch")) + (P(),) * 9
    out_specs = (split, split) + (P(),) * 10
    return jax.shard_map(per_device, mesh=mesh, in_specs=in_specs, out_specs=out_specs, check_vma=False)
```

```python
import functools
import math

import jax
import jax.numpy as jnp
from jax import lax
from jax.experimental import pallas as pl
from jax.experimental.pallas import tpu as pltpu
from jax.sharding import PartitionSpec as P

MESH = pl.DeviceIdType.MESH
EPSILON = 1e-05
LOG2E = 1.4426950408889634
LN2 = 0.6931471805599453
GELU_K = math.sqrt(2.0 / math.pi)
F32 = jnp.float32
BF16 = jnp.bfloat16
LANES = 128
CHUNK = 32
CHAINS = 6
UROWS = 256
PIECES = 4
EXTRA = 16


def rows8(v):
    return v.reshape(v.shape[0] // 8, 8, v.shape[1]).sum(0)


def sigmoid(v):
    return 1.0 / (1.0 + jnp.exp(-v))


def gelu_parts(m):
    th = jnp.tanh(GELU_K * (m + 0.044715 * m * m * m))
    return th


def bits_of(n):
    return [i for i in range(n.bit_length() - 1)]


def orders(seq, batch, chains, upper):
    s = [("seq", b) for b in bits_of(seq)]
    b = [("batch", b) for b in bits_of(batch)]
    x, y, z, rest = s[1:2], b[:1], b[1:2], b[2:] + s[2:]
    kinds = [y + z + x, z + y + x] if upper else [y + z + x, z + x + y, x + y + z]
    return [kinds[c % len(kinds)] + rest for c in range(chains)]


def chain_rows(rows, devices, most):
    unit = 8 * devices
    units = rows // unit
    chains = min(most, units)
    cut = [units // chains + (1 if c < units % chains else 0) for c in range(chains)]
    return [(sum(cut[:c]) * unit, cut[c] * unit) for c in range(chains)]


def small_rows(layers, states, batch):
    unit = 8 * batch
    return -(-layers * (2 * states + EXTRA) // unit) * unit


def kernel(cfg, *refs):
    S, B, TL, D, NS, L, UN = cfg
    CG = D // LANES
    NSP = S // CG
    NL = NS // NSP
    E2 = 2 * D
    CB = E2 // LANES
    GROWS = D * CB
    NQ = PIECES
    TB = TL // NQ
    SB_LAYER = 2 * NL + EXTRA
    SB_ROWS = small_rows(L, NL, B)
    SP = SB_ROWS // B
    spans = chain_rows(GROWS // 2, S * B // 2, CHAINS)
    (
        x_hbm, ct_hbm, len_hbm, gain_hbm, dec_hbm, in_hbm, out_hbm, skip_hbm, o2_hbm, step_hbm, w_hbm, bias_hbm,
        y_out, gx_out, ggain_out, gdec_out, gin_out, gout_out, gskip_out, go2_out, gstep_out, FG, gbias_out, stats_out,
        x_ref, ct_ref, len_ref, gain_ref, DEC, INM, OUTM, skip_ref, o2_ref, step_ref, W, bias_ref, NA, WT,
        XS, XR, RSTD, R, Y, YR, GS, GMR, GXR,
        SIG, P1, P2, LA, PJ, LG, GA, STR, GRD, ST,
        FB, RB, AF, AR, GF, GFR, LA2, LG2, SBW, SBR, SBG, VEC,
        load_sem, send_sem, recv_sem, ar_ssem, ar_rsem, sb_ssem, sb_rsem, sg_ssem, sg_rsem, pair_ssem, pair_rsem,
    ) = refs
    U, GX = P2, Y
    me = lax.axis_index("seq")
    bi = lax.axis_index("batch")
    cg = me // NSP
    nh = lax.rem(me, NSP)
    n0 = nh * NL
    first_part = (nh == 0).astype(F32)
    clane = pl.ds(pl.multiple_of(cg * LANES, LANES), LANES)

    sources = (x_hbm, len_hbm, gain_hbm, o2_hbm, step_hbm, dec_hbm, in_hbm, out_hbm, skip_hbm, w_hbm, bias_hbm, ct_hbm)
    targets = (x_ref, len_ref, gain_ref, o2_ref, step_ref, DEC, INM, OUTM, skip_ref, W, bias_ref, ct_ref)
    loads = [pltpu.make_async_copy(h, v, load_sem.at[i]) for i, (h, v) in enumerate(zip(sources, targets))]
    for c in loads:
        c.start()

    barrier = pltpu.get_barrier_semaphore()
    partners = [(me ^ d, bi) for d in range(1, S)]
    partners += [(me ^ 1, bi ^ (1 << b)) for b in bits_of(B)]
    for p in partners:
        pl.semaphore_signal(barrier, inc=1, device_id=p, device_id_type=MESH)

    sends = []

    def sent():
        while sends:
            sends.pop(0)()

    def seq_copy(ph, j, q, src, dst):
        return pltpu.make_async_remote_copy(
            src_ref=src,
            dst_ref=dst,
            send_sem=send_sem.at[j, q],
            recv_sem=recv_sem.at[ph % 2, me, q],
            device_id=(j, bi),
            device_id_type=MESH,
        )

    def seq_wait(ph, k, q, ref):
        pltpu.make_async_remote_copy(
            src_ref=ref,
            dst_ref=ref,
            send_sem=send_sem.at[k, q],
            recv_sem=recv_sem.at[ph % 2, k, q],
            device_id=(k, bi),
            device_id_type=MESH,
        ).wait_recv()

    def rows_of(q):
        return pl.ds(q * TB if isinstance(q, int) else pl.multiple_of(q * TB, TB), TB)

    def span(k, q):
        return pl.ds(pl.multiple_of((k * NQ + q) * TB, TB), TB)

    peers = list(range(S - 1, 0, -1))

    def tblock(k):
        return pl.ds(pl.multiple_of(k * TL, TL), TL)

    def bit_of(v, bit):
        return lax.rem(v // (1 << bit), 2)

    def swap(axis, bit):
        if axis == "batch":
            return (me ^ 1, bi ^ (1 << bit))
        return (me ^ (1 << bit) ^ 1, bi)

    def my_bit(axis, bit):
        return bit_of(me if axis == "seq" else bi, bit)

    side = lax.rem(sum(bit_of(me, i) for i in bits_of(S)) + sum(bit_of(bi, i) for i in bits_of(B)), 2)

    def pair_copy(which, l, src, dst):
        return pltpu.make_async_remote_copy(
            src_ref=src,
            dst_ref=dst,
            send_sem=pair_ssem.at[which],
            recv_sem=pair_rsem.at[which, l],
            device_id=(me ^ 1, bi),
            device_id_type=MESH,
        )

    def act_copy(l):
        return pair_copy(0, l, AF, AR.at[l])

    def grad_copy(l):
        return pair_copy(1, l, GF.at[1 - side], GFR.at[l])

    class Reduce:
        after = ()

        def __init__(self, l):
            self.l = l
            self.chains = []
            plans = orders(S, B, len(spans), l > 0)
            for (base, rows), plan in zip(spans, plans):
                off, size, roff, stages = base, rows, base, []
                for i, (axis, bit) in enumerate(plan):
                    half = size // 2
                    mine = my_bit(axis, bit)
                    keep = pl.multiple_of(off + mine * half, 8)
                    give = pl.multiple_of(off + (1 - mine) * half, 8)
                    stages.append((i, axis, bit, half, keep, give, roff))
                    off, size, roff = keep, half, roff + half
                self.chains.append(stages)
            self.n = n = len(plans[0])
            self.todo = [self.begin]
            self.todo += [functools.partial(self.reduce_step, i) for i in range(n)]
            self.todo += [functools.partial(self.gather_step, i) for i in range(n - 1, -1, -1)]
            self.todo += [self.last_step]

        def rs(self, c, stage):
            i, axis, bit, half, keep, give, roff = stage
            return pltpu.make_async_remote_copy(
                src_ref=FB.at[self.l, pl.ds(give, half)],
                dst_ref=RB.at[self.l, pl.ds(roff, half)],
                send_sem=ar_ssem.at[self.l, c],
                recv_sem=ar_rsem.at[self.l, c, i],
                device_id=swap(axis, bit),
                device_id_type=MESH,
            )

        def pair(self, c):
            base, rows = spans[c]
            here = FG.at[self.l, side, pl.ds(base, rows)]
            return pltpu.make_async_remote_copy(
                src_ref=here,
                dst_ref=here,
                send_sem=ar_ssem.at[self.l, c],
                recv_sem=ar_rsem.at[self.l, c, self.n + 1],
                device_id=(me ^ 1, bi),
                device_id_type=MESH,
            )

        def ag(self, c, stage):
            i, axis, bit, half, keep, give, roff = stage
            here = FG.at[self.l, side, pl.ds(keep, half)]
            return pltpu.make_async_remote_copy(
                src_ref=here,
                dst_ref=here,
                send_sem=ar_ssem.at[self.l, c],
                recv_sem=ar_rsem.at[self.l, c, i - 1 if i else self.n],
                device_id=swap(axis, bit),
                device_id_type=MESH,
            )

        def begin(self):
            for c, stages in enumerate(self.chains):
                self.rs(c, stages[0]).start()

        def reduce_step(self, i):
            for c, stages in enumerate(self.chains):
                _, _, _, half, keep, _, roff = stages[i]
                self.rs(c, stages[i]).wait()
                step = math.gcd(half, 64)

                def add(j, _, i=i, keep=keep, roff=roff, step=step):
                    at = pl.ds(pl.multiple_of(keep + j * step, 8), step)
                    total = FB[self.l, at, :] + RB[self.l, pl.ds(pl.multiple_of(roff + j * step, 8), step), :]
                    if i + 1 < self.n:
                        FB[self.l, at, :] = total
                    else:
                        FG[self.l, side, at, :] = total
                    return 0

                lax.fori_loop(0, half // step, add, 0)
                if i + 1 < self.n:
                    self.rs(c, stages[i + 1]).start()
                else:
                    self.ag(c, stages[i]).start()

        def gather_step(self, i):
            for c, stages in enumerate(self.chains):
                self.ag(c, stages[i]).wait()
                if i > 0:
                    self.ag(c, stages[i - 1]).start()
                else:
                    self.pair(c).start()

        def last_step(self):
            for c in range(len(self.chains)):
                self.pair(c).wait()

    def norm_forward(l, src):
        def step(i, _):
            rows = pl.ds(pl.multiple_of(i * CHUNK, CHUNK), CHUNK)
            x = src[rows, :]
            center = x - jnp.mean(x, axis=-1, keepdims=True)
            spread = jnp.mean(center * center, axis=-1, keepdims=True)
            inv = lax.rsqrt(spread + EPSILON)
            xhat = center * inv
            RSTD[l, rows, :] = jnp.broadcast_to(inv, (CHUNK, LANES))
            for g in range(CG):
                XS[l, g, rows, :] = xhat[:, g * LANES : (g + 1) * LANES]
            return 0

        lax.fori_loop(0, TL // CHUNK, step, 0)

    def send_normed(l):
        for q in range(NQ):
            for d in peers:
                j = me ^ d
                seq_copy(0, j, q, XS.at[l, j // NSP, rows_of(q)], XR.at[l, span(me, q)]).start()
        XR[l, tblock(me), :] = XS[l, cg]

    def scan_forward(l):
        gain = gain_ref[l : l + 1, clane]
        o2 = o2_ref[l : l + 1, clane]
        stp = step_ref[l : l + 1, clane]
        skip = skip_ref[l : l + 1, clane] * first_part
        first_row = lax.broadcasted_iota(jnp.int32, (TB, LANES), 0) == 0
        SIG[l, 0] = jnp.zeros((NL, LANES), F32)

        def block(b, carry):
            sig, last = carry
            k, q = b // NQ, lax.rem(b, NQ)
            here, t0 = span(k, q), b * TB

            @pl.when(k != me)
            def _():
                seq_wait(0, k, q, XR.at[l, here])

            normed = XR[l, here, :] * gain
            prev = jnp.where(first_row, last, pltpu.roll(normed, 1, 0))
            U[here, :] = normed + o2 * normed * prev
            z = stp * normed
            R[l, here, :] = jnp.maximum(z, 0.0) + jnp.log1p(jnp.exp(-jnp.abs(z)))
            na, wt = NA[l], WT[l]

            def inner(i, sig):
                for s in range(UN):
                    t = i * UN + s
                    at = pl.ds(t0 + t, 1)
                    sig = jnp.exp2(na * R[l, at, :]) * sig + U[at, :]
                    SIG[l, t0 + t + 1] = sig
                    P1[pl.ds(pl.multiple_of(t * 8, 8), 8), :] = rows8(wt * sig)
                return sig

            sig = lax.fori_loop(0, TB // UN, inner, sig)
            for j in range(TB // 8):
                total = P1[pl.ds(j * 64, 8, stride=8), :]
                for s in range(1, 8):
                    total = total + P1[pl.ds(j * 64 + s, 8, stride=8), :]
                at = pl.ds(pl.multiple_of(t0 + j * 8, 8), 8)
                Y[at, :] = total + skip * U[at, :]

            @pl.when(k != me)
            def _():
                seq_copy(0, k, q, XS.at[l, 0, rows_of(q)], XR.at[l, here]).wait_send()
                seq_copy(1, k, q, Y.at[here], YR.at[l, me, rows_of(q)]).start()

            return sig, normed[TB - 1 : TB, :]

        lax.fori_loop(0, S * NQ, block, (jnp.zeros((NL, LANES), F32), jnp.zeros((1, LANES), F32)))
        YR[l, me] = Y[tblock(me), :]
        for q in range(NQ):
            for d in peers:
                here = span(me ^ d, q)
                sends.append(seq_copy(1, me ^ d, q, Y.at[here], YR.at[l, me, rows_of(q)]).wait_send)

    def mixed_of(l, g, rows):
        m = YR[l, g * NSP, rows, :]
        for h in range(1, NSP):
            m = m + YR[l, g * NSP + h, rows, :]
        return m

    def valid_of(i):
        pos = me * TL + i * CHUNK + lax.broadcasted_iota(jnp.int32, (CHUNK, 1), 0)
        return (pos < len_ref[0]).astype(F32)

    def glu_forward(l, src, dst):
        for q in range(NQ):
            for d in peers:
                seq_wait(1, me ^ d, q, YR.at[l, me ^ d, rows_of(q)])

        def act(i, sq):
            rows = pl.ds(pl.multiple_of(i * CHUNK, CHUNK), CHUNK)
            valid = valid_of(i)
            for g in range(CG):
                m = mixed_of(l, g, rows)
                a = 0.5 * m * (1.0 + gelu_parts(m))
                low = a.astype(BF16)
                LA[l, rows, g * LANES : (g + 1) * LANES] = low
                AF[rows, g * LANES : (g + 1) * LANES] = low.astype(F32)
                sq = sq + rows8(a * a * valid)
            return sq

        zero = jnp.zeros((8, LANES), F32)
        if l:
            act_copy(l - 1).wait_send()
        sq_act = lax.fori_loop(0, TL // CHUNK, act, zero)
        act_copy(l).start()
        PJ[l] = jnp.dot(LA[l], W[l], preferred_element_type=F32) + bias_ref[l : l + 1, :]

        def gate(i, sq):
            sq_b, sq_s, cnt = sq
            rows = pl.ds(pl.multiple_of(i * CHUNK, CHUNK), CHUNK)
            valid = valid_of(i)
            for g in range(CG):
                cols = slice(g * LANES, (g + 1) * LANES)
                gcols = slice(D + g * LANES, D + (g + 1) * LANES)
                branch = PJ[l, rows, cols] * sigmoid(PJ[l, rows, gcols]) * valid
                out = src[rows, cols] + branch
                dst[rows, cols] = out
                sq_b = sq_b + rows8(branch * branch)
                sq_s = sq_s + rows8(out * out * valid)
            cnt = cnt + rows8(jnp.broadcast_to(valid, (CHUNK, LANES)))
            return sq_b, sq_s, cnt

        sq_b, sq_s, cnt = lax.fori_loop(0, TL // CHUNK, gate, (zero, zero, zero))
        for k, v in enumerate((sq_act, sq_b, sq_s, cnt)):
            ST[l, k] = v

    def gate_backward(l, gsrc):
        def gate(i, acc):
            rows = pl.ds(pl.multiple_of(i * CHUNK, CHUNK), CHUNK)
            valid = valid_of(i)
            out = []
            for g in range(CG):
                cols = slice(g * LANES, (g + 1) * LANES)
                gcols = slice(D + g * LANES, D + (g + 1) * LANES)
                gb = gsrc[rows, cols] * valid
                s = sigmoid(PJ[l, rows, gcols])
                one = gb * s
                two = one * PJ[l, rows, cols] * (1.0 - s)
                low_one, low_two = one.astype(BF16), two.astype(BF16)
                LG[rows, cols] = low_one
                LG[rows, gcols] = low_two
                GF[0, rows, cols] = low_one.astype(F32)
                GF[1, rows, cols] = low_two.astype(F32)
                out.append((rows8(one), rows8(two)))
            return tuple(a + b for a, b in zip(acc, [o[0] for o in out] + [o[1] for o in out]))

        zero = jnp.zeros((8, LANES), F32)
        if l < L - 1:
            grad_copy(l + 1).wait_send()
        bias = lax.fori_loop(0, TL // CHUNK, gate, (zero,) * CB)
        grad_copy(l).start()
        return bias

    def act_backward(l, bias):
        GA[...] = lax.dot_general(LG[...], W[l], (((1,), (1,)), ((), ())), preferred_element_type=F32)

        def act(i, _):
            rows = pl.ds(pl.multiple_of(i * CHUNK, CHUNK), CHUNK)
            for g in range(CG):
                m = mixed_of(l, g, rows)
                th = gelu_parts(m)
                slope = 0.5 * (1.0 + th) + 0.5 * m * (1.0 - th * th) * GELU_K * (1.0 + 3 * 0.044715 * m * m)
                GS[l, g, rows, :] = GA[rows, g * LANES : (g + 1) * LANES] * slope
            return 0

        lax.fori_loop(0, TL // CHUNK, act, 0)
        for q in range(NQ - 1, -1, -1):
            for d in peers:
                j = me ^ d
                seq_copy(2, j, q, GS.at[l, j // NSP, rows_of(q)], GMR.at[l, me, rows_of(q)]).start()
        GMR[l, me] = GS[l, cg]
        extra = list(bias) + [ST[l, k] for k in range(4)]
        extra = jnp.concatenate([jnp.sum(v, axis=0, keepdims=True) for v in extra], axis=0)
        base = l * SB_LAYER + 2 * NL + 4
        SBW[base : base + len(bias) + 4, :] = extra

    def weight_grad(l):
        if l == L - 1:
            act_copy(l).wait_send()
        act_copy(l).wait_recv()
        grad_copy(l).wait_recv()

        def cast(i, _):
            rows = pl.ds(pl.multiple_of(i * CHUNK, CHUNK), CHUNK)
            also = pl.ds(pl.multiple_of(TL + i * CHUNK, CHUNK), CHUNK)
            LA2[rows, :] = LA[l, rows, :]
            LA2[also, :] = AR[l, rows, :].astype(BF16)
            LG2[rows, :] = GF[side, rows, :].astype(BF16)
            LG2[also, :] = GFR[l, rows, :].astype(BF16)
            return 0

        lax.fori_loop(0, TL // CHUNK, cast, 0)
        half = lax.dot_general(LA2[...], LG2[...], (((0,), (0,)), ((), ())), preferred_element_type=F32)
        for q in range(CB // 2):
            FB[l, pl.ds(q * D, D), :] = half[:, q * LANES : (q + 1) * LANES]

    def scan_backward(l, steps):
        gain = gain_ref[l : l + 1, clane]
        o2 = o2_ref[l : l + 1, clane]
        stp = step_ref[l : l + 1, clane]
        skip = skip_ref[l : l + 1, clane]
        row_id = lax.broadcasted_iota(jnp.int32, (TB, LANES), 0)
        zero8 = jnp.zeros((8, LANES), F32)
        zeros = jnp.zeros((NL, LANES), F32)
        for v in range(4):
            VEC[v] = zero8

        def block(bb, carry):
            nu, acc, gdc, after = carry
            b = S * NQ - 1 - bb
            k, q = b // NQ, lax.rem(b, NQ)
            here, t0 = span(k, q), b * TB

            @pl.when(k != me)
            def _():
                seq_wait(2, k, q, GMR.at[l, k, rows_of(q)])

            na, wt = NA[l], WT[l]

            def inner(ii, c):
                nu, acc, gdc = c
                i = TB // UN - 1 - ii
                for s in range(UN - 1, -1, -1):
                    t = i * UN + s
                    logs = na * R[l, pl.ds(t0 + t, 1), :]
                    gm = GMR[l, k, pl.ds(q * TB + t, 1), :]
                    mu = wt * gm + nu
                    if l == 0:
                        acc = acc + gm * SIG[l, t0 + t + 1]
                    at = pl.ds(pl.multiple_of(t * 8, 8), 8)
                    P1[at, :] = rows8(mu)
                    nu = jnp.exp2(logs) * mu
                    part = nu * SIG[l, t0 + t] * logs
                    gdc = gdc + part
                    P2[at, :] = rows8(part)
                return nu, acc, gdc

            nu, acc, gdc = lax.fori_loop(0, TB // UN, inner, (nu, acc, gdc))
            for j in range(TB // 8):
                one = P1[pl.ds(j * 64, 8, stride=8), :]
                two = P2[pl.ds(j * 64, 8, stride=8), :]
                for s in range(1, 8):
                    one = one + P1[pl.ds(j * 64 + s, 8, stride=8), :]
                    two = two + P2[pl.ds(j * 64 + s, 8, stride=8), :]
                GX[pl.ds(pl.multiple_of(t0 + j * 8, 8), 8), :] = one
                GA[j * 8 : j * 8 + 8, 0:LANES] = two
            xhat = XR[l, here, :]
            normed = xhat * gain
            before = XR[l, pl.ds(jnp.maximum(t0 - 1, 0), 1), :] * gain
            before = jnp.where(b == 0, 0.0, before)
            prev = jnp.where(row_id == 0, before, pltpu.roll(normed, 1, 0))
            gm = GMR[l, k, rows_of(q), :] * first_part
            gdrv = GX[here, :] + skip * gm
            both = gdrv * normed
            h = o2 * both
            later = jnp.where(row_id == TB - 1, after, pltpu.roll(h, TB - 1, 0))
            rate = R[l, here, :]
            some = rate > 1e-30
            ratio = jnp.where(some, sigmoid(stp * normed) / jnp.where(some, rate, 1.0), 1.0)
            slope = GA[0:TB, 0:LANES] * LN2 * ratio
            gnormed = gdrv * (1.0 + o2 * prev) + later + slope * stp
            GX[here, :] = gnormed * gain
            VEC[0] = VEC[0] + rows8(gm * (normed + o2 * normed * prev))
            VEC[1] = VEC[1] + rows8(both * prev)
            VEC[2] = VEC[2] + rows8(slope * normed)
            VEC[3] = VEC[3] + rows8(gnormed * xhat)

            @pl.when(k != me)
            def _():
                seq_copy(2, k, q, GS.at[l, 0, rows_of(q)], GMR.at[l, me, rows_of(q)]).wait_send()
                seq_copy(3, k, q, GX.at[here], GXR.at[l, me, rows_of(q)]).start()

            if steps:
                hit = functools.reduce(jnp.logical_or, [bb == place for place in sorted(steps)])

                @pl.when(hit)
                def _():
                    for place in sorted(steps):

                        @pl.when(bb == place)
                        def _(todo=steps[place]):
                            for step in todo:
                                step()

            return nu, acc, gdc, h[0:1, :]

        carry = (zeros, zeros, zeros, jnp.zeros((1, LANES), F32))
        _, acc, gdc, _ = lax.fori_loop(0, S * NQ, block, carry)
        GXR[l, me] = GX[tblock(me), :]
        for q in range(NQ):
            for d in peers:
                here = span(me ^ d, q)
                sends.append(seq_copy(3, me ^ d, q, GX.at[here], GXR.at[l, me, rows_of(q)]).wait_send)
        gdc = gdc / NA[l]
        base = l * SB_LAYER
        SBW[base + NL : base + 2 * NL, :] = gdc
        if l == 0:
            SBW[base : base + NL, :] = acc
        vec = [jnp.sum(VEC[v], axis=0, keepdims=True) for v in range(4)]
        SBW[base + 2 * NL : base + 2 * NL + 4, :] = jnp.concatenate(vec, axis=0)

    def late_sum(l):
        def step(i, acc):
            for s in range(8):
                t = i * 8 + s
                acc = acc + GMR[l, i // (TL // 8), pl.ds(lax.rem(i, TL // 8) * 8 + s, 1), :] * SIG[l, t + 1]
            return acc

        SBW[l * SB_LAYER : l * SB_LAYER + NL, :] = lax.fori_loop(0, S * TL // 8, step, jnp.zeros((NL, LANES), F32))

    class Small:
        def __init__(self, first):
            self.after = [(first, first.n + 1)]
            self.todo = [self.begin, self.join, self.across]
            self.todo += [functools.partial(self.along, i) for i in range(len(bits_of(S)))]

        def part(self, j):
            return pl.ds(pl.multiple_of(j * SP, 8), SP)

        def rs(self, j, slot):
            return pltpu.make_async_remote_copy(
                src_ref=SBW.at[self.part(j)],
                dst_ref=SBR.at[slot],
                send_sem=sb_ssem.at[j],
                recv_sem=sb_rsem.at[0, slot],
                device_id=(me, j),
                device_id_type=MESH,
            )

        def ag(self, j, slot):
            rows = self.part(slot)
            return pltpu.make_async_remote_copy(
                src_ref=SBG.at[me, rows],
                dst_ref=SBG.at[me, rows],
                send_sem=sb_ssem.at[j],
                recv_sem=sb_rsem.at[1, slot],
                device_id=(me, j),
                device_id_type=MESH,
            )

        def seq(self, i, slot):
            return pltpu.make_async_remote_copy(
                src_ref=SBG.at[slot],
                dst_ref=SBG.at[slot],
                send_sem=sg_ssem.at[slot],
                recv_sem=sg_rsem.at[slot],
                device_id=(me ^ (S >> (i + 1)), bi),
                device_id_type=MESH,
            )

        def begin(self):
            if SB_ROWS > L * SB_LAYER:
                SBW[L * SB_LAYER :, :] = jnp.zeros((SB_ROWS - L * SB_LAYER, LANES), F32)
            for d in range(B - 1, 0, -1):
                self.rs(bi ^ d, bi).start()
            SBR[bi] = SBW[self.part(bi), :]

        def join(self):
            for d in range(B - 1, 0, -1):
                self.rs(bi ^ d, bi ^ d).wait()
            total = SBR[0]
            for j in range(1, B):
                total = total + SBR[j]
            SBG[me, self.part(bi), :] = total
            for d in range(B - 1, 0, -1):
                self.ag(bi ^ d, bi).start()

        def across(self):
            for d in range(B - 1, 0, -1):
                self.ag(bi ^ d, bi ^ d).wait()
            self.seq(0, me).start()

        def slots(self, i):
            held = [me]
            for k in range(i):
                held = held + [slot ^ (S >> (k + 1)) for slot in held]
            return held

        def along(self, i):
            step = S >> (i + 1)
            for slot in self.slots(i):
                self.seq(i, slot).wait_send()
                self.seq(i, slot ^ step).wait_recv()
            if i + 1 < len(bits_of(S)):
                for slot in self.slots(i + 1):
                    self.seq(i + 1, slot).start()
            else:
                for l in range(L):
                    self.gathered(l)

        def gathered(self, l):
            base = l * SB_LAYER
            for g in range(CG):
                cols = slice(g * LANES, (g + 1) * LANES)
                vec = None
                for h in range(NSP):
                    slot = g * NSP + h
                    rows = slice(h * NL, (h + 1) * NL)
                    acc = SBG[slot, base : base + NL, :]
                    gin_out[l, rows, cols] = OUTM[l, rows, cols] * acc
                    gout_out[l, rows, cols] = INM[l, rows, cols] * acc
                    gdec_out[l, rows, cols] = -SBG[slot, base + NL : base + 2 * NL, :]
                    part = SBG[slot, base + 2 * NL : base + 2 * NL + 4, :]
                    vec = part if vec is None else vec + part
                gskip_out[l : l + 1, cols] = vec[0:1]
                go2_out[l : l + 1, cols] = vec[1:2]
                gstep_out[l : l + 1, cols] = vec[2:3]
                ggain_out[l : l + 1, cols] = vec[3:4]
            base += 2 * NL + 4
            extra = SBG[0, base : base + CB + 4, :]
            for k in range(1, S):
                extra = extra + SBG[k, base : base + CB + 4, :]
            for q in range(CB):
                gbias_out[l : l + 1, q * LANES : (q + 1) * LANES] = extra[q : q + 1]
            sq = jnp.sum(extra[CB:], axis=1, keepdims=True)
            count = sq[3:4] * (1.0 / LANES)
            root = jnp.sqrt(sq[0:3] / (count * D))
            col = lax.broadcasted_iota(jnp.int32, (1, 3), 1)
            stats_out[l : l + 1, :] = jnp.where(col == 0, root[0:1], jnp.where(col == 1, root[1:2], root[2:3]))

    def norm_backward(l, gsrc, gdst):
        for q in range(NQ):
            for d in peers:
                seq_wait(3, me ^ d, q, GXR.at[l, me ^ d, rows_of(q)])

        def step(i, _):
            rows = pl.ds(pl.multiple_of(i * CHUNK, CHUNK), CHUNK)
            inv = RSTD[l, rows, :]
            gx, xh = [], []
            s1 = s2 = None
            for g in range(CG):
                v = GXR[l, g * NSP, rows, :]
                for h in range(1, NSP):
                    v = v + GXR[l, g * NSP + h, rows, :]
                x = XS[l, g, rows, :]
                gx.append(v)
                xh.append(x)
                s1 = v if s1 is None else s1 + v
                s2 = v * x if s2 is None else s2 + v * x
            m1 = jnp.sum(s1, axis=-1, keepdims=True) * (1.0 / D)
            m2 = jnp.sum(s2, axis=-1, keepdims=True) * (1.0 / D)
            for g in range(CG):
                cols = slice(g * LANES, (g + 1) * LANES)
                gdst[rows, cols] = gsrc[rows, cols] + inv * (gx[g] - m1 - xh[g] * m2)
            return 0

        lax.fori_loop(0, TL // CHUNK, step, 0)

    loads[0].wait()
    norm_forward(0, x_ref)
    pl.semaphore_wait(barrier, len(partners))
    send_normed(0)
    for c in loads[1:]:
        c.wait()
    nrows = pl.ds(pl.multiple_of(n0, 8), NL)
    for l in range(L):
        NA[l] = DEC[l, nrows, clane] * (-LOG2E)
        WT[l] = INM[l, nrows, clane] * OUTM[l, nrows, clane]
    streams = [x_ref] + [STR.at[l] for l in range(L - 1)] + [y_out]
    for l in range(L):
        if l:
            norm_forward(l, streams[l])
            send_normed(l)
        scan_forward(l)
        glu_forward(l, streams[l], streams[l + 1])
        sent()

    grads = [gx_out] + [GRD.at[l] for l in range(L - 1)] + [ct_ref]
    def take(things):
        steps = []
        for t in things:
            if t.todo and all(len(a.todo) <= left for a, left in t.after):
                steps.append(t.todo.pop(0))
        return steps

    def run(*things):
        for step in take(things):
            step()

    def places(plan):
        return {(i + 1) * S * NQ // 16 - 1: take(plan[i]) for i in sorted(plan)}

    bigs = []
    for l in range(L - 1, -1, -1):
        bias = gate_backward(l, grads[l + 1])
        act_backward(l, bias)
        weight_grad(l)
        above = list(bigs)
        bigs.insert(0, Reduce(l))
        run(bigs[0])
        if above:
            late_sum(l + 1)
            scan_backward(l, places({5: above, 12: above, 13: bigs[:1]}))
        else:
            scan_backward(l, places({11: bigs}))
        if l == 0:
            small = Small(bigs[-1])
            run(small)
        norm_backward(l, grads[l + 1], grads[l])
        sent()
        run(*bigs)
    grad_copy(0).wait_send()
    while any(t.todo for t in bigs + [small]):
        run(bigs[0], small, *bigs[1:])


def hand_on(*refs):
    n = (len(refs) - 2) // 2
    sem, block_sem = refs[-2], refs[-1]
    copies = []
    for i, (a, o) in enumerate(zip(refs[:n], refs[n : 2 * n])):
        if a.shape == o.shape:
            copies.append(pltpu.make_async_copy(a, o, sem.at[i]))
            continue
        layers, rows, columns = o.shape
        for l in range(layers):
            for c in range(columns // LANES):
                block = o.at[l, :, pl.ds(c * LANES, LANES)]
                side, at = divmod(c * rows, a.shape[2])
                copies.append(pltpu.make_async_copy(a.at[l, side, pl.ds(at, rows)], block, block_sem.at[l, c]))
    for c in copies:
        c.start()
    for c in copies:
        c.wait()


def per_device(
    stream_in, cotangent, lengths, norm_gain, decay_rate, in_map, out_map, skip_gain, order_two, step_gain, glu_weight, glu_bias
):
    S, B = lax.axis_size("seq"), lax.axis_size("batch")
    _, TL, D = stream_in.shape
    L, NS = decay_rate.shape[:2]
    UN = math.gcd(TL // PIECES, 32)
    CG, E2 = D // LANES, 2 * D
    NL = NS // (S // CG)
    TA = S * TL
    CB = E2 // LANES
    GROWS = D * CB
    SBR = small_rows(L, NL, B)
    NB, NST = len(bits_of(B)), len(bits_of(B)) + len(bits_of(S))
    shape = jax.ShapeDtypeStruct
    vmem = pl.BlockSpec(memory_space=pltpu.VMEM)
    hbm = pl.BlockSpec(memory_space=pl.ANY)
    buf = pltpu.VMEM
    dma = pltpu.SemaphoreType.DMA
    outs = pl.pallas_call(
        functools.partial(kernel, (S, B, TL, D, NS, L, UN)),
        out_shape=[
            buf((TL, D), F32), buf((TL, D), F32), buf((L, D), F32),
            buf((L, NS, D), F32), buf((L, NS, D), F32), buf((L, NS, D), F32),
            buf((L, D), F32), buf((L, D), F32), buf((L, D), F32),
            buf((L, 2, GROWS // 2, LANES), F32), buf((L, E2), F32), buf((L, 3), F32),
        ],
        in_specs=[hbm] * 12,
        out_specs=[vmem] * 12,
        scratch_shapes=[
            buf((TL, D), F32), buf((TL, D), F32), pltpu.SMEM((1,), jnp.int32), buf((L, D), F32),
            buf((L, NS, D), F32), buf((L, NS, D), F32), buf((L, NS, D), F32),
            buf((L, D), F32), buf((L, D), F32), buf((L, D), F32), buf((L, D, E2), BF16), buf((L, E2), F32),
            buf((L, NL, LANES), F32), buf((L, NL, LANES), F32),
            buf((L, CG, TL, LANES), F32), buf((L, TA, LANES), F32), buf((L, TL, LANES), F32),
            buf((L, TA, LANES), F32), buf((TA, LANES), F32),
            buf((L, S, TL, LANES), F32), buf((L, CG, TL, LANES), F32), buf((L, S, TL, LANES), F32),
            buf((L, S, TL, LANES), F32),
            buf((L, TA + 1, NL, LANES), F32), buf((TL * 8, LANES), F32), buf((max(TL * 8, TA), LANES), F32),
            buf((L, TL, D), BF16), buf((L, TL, E2), F32), buf((TL, E2), BF16), buf((TL, D), F32),
            buf((L - 1, TL, D), F32), buf((L - 1, TL, D), F32), buf((L, 4, 8, LANES), F32),
            buf((L, GROWS // 2, LANES), F32), buf((L, GROWS // 2, LANES), F32),
            buf((TL, D), F32), buf((L, TL, D), F32), buf((2, TL, D), F32), buf((L, TL, D), F32), buf((2 * TL, D), BF16), buf((2 * TL, D), BF16),
            buf((SBR, LANES), F32), buf((B, SBR // B, LANES), F32), buf((S, SBR, LANES), F32),
            buf((4, 8, LANES), F32),
            dma((12,)), dma((S, PIECES)), dma((2, S, PIECES)), dma((L, CHAINS)), dma((L, CHAINS, NST + 1)),
            dma((B,)), dma((2, B)), dma((S,)), dma((S,)), dma((2,)), dma((2, L)),
        ],
        compiler_params=pltpu.CompilerParams(
            collective_id=0, has_side_effects=True, vmem_limit_bytes=57 * 2**20
        ),
        name="liquid_layers",
    )(
        stream_in[0], cotangent[0], lengths, norm_gain, decay_rate, in_map, out_map,
        skip_gain, order_two, step_gain, glu_weight, glu_bias,
    )
    outs = pl.pallas_call(
        hand_on,
        out_shape=[shape((L, D, E2), F32) if o.ndim == 4 else shape(o.shape, F32) for o in outs],
        in_specs=[vmem] * len(outs),
        out_specs=[hbm] * len(outs),
        scratch_shapes=[dma((len(outs),)), dma((L, CB))],
        compiler_params=pltpu.CompilerParams(vmem_limit_bytes=2**20),
        name="results",
    )(*outs)
    return (outs[0][None], outs[1][None], *outs[2:])


def solution(mesh):
    split = P("batch", "seq", None)
    in_specs = (split, split, P("batch")) + (P(),) * 9
    out_specs = (split, split) + (P(),) * 10
    return jax.shard_map(per_device, mesh=mesh, in_specs=in_specs, out_specs=out_specs, check_vma=False)
```

```python
import functools
import math

import jax
import jax.numpy as jnp
from jax import lax
from jax.experimental import pallas as pl
from jax.experimental.pallas import tpu as pltpu
from jax.sharding import PartitionSpec as P

MESH = pl.DeviceIdType.MESH
EPSILON = 1e-05
LOG2E = 1.4426950408889634
LN2 = 0.6931471805599453
GELU_K = math.sqrt(2.0 / math.pi)
F32 = jnp.float32
BF16 = jnp.bfloat16
LANES = 128
CHUNK = 32
CHAINS = 6
UROWS = 256
PIECES = 4
EXTRA = 16


def rows8(v):
    return v.reshape(v.shape[0] // 8, 8, v.shape[1]).sum(0)


def sigmoid(v):
    return 1.0 / (1.0 + jnp.exp(-v))


def gelu_parts(m):
    th = jnp.tanh(GELU_K * (m + 0.044715 * m * m * m))
    return th


def bits_of(n):
    return [i for i in range(n.bit_length() - 1)]


def orders(seq, batch, chains, upper):
    s = [("seq", b) for b in bits_of(seq)]
    b = [("batch", b) for b in bits_of(batch)]
    x, y, z, rest = s[1:2], b[:1], b[1:2], b[2:] + s[2:]
    kinds = [y + z + x, z + y + x] if upper else [y + z + x, z + x + y, x + y + z]
    return [kinds[c % len(kinds)] + rest for c in range(chains)]


def chain_rows(rows, devices, most):
    unit = 8 * devices
    units = rows // unit
    chains = min(most, units)
    cut = [units // chains + (1 if c < units % chains else 0) for c in range(chains)]
    return [(sum(cut[:c]) * unit, cut[c] * unit) for c in range(chains)]


def small_rows(layers, states, batch):
    unit = 8 * batch
    return -(-layers * (2 * states + EXTRA) // unit) * unit


def kernel(cfg, *refs):
    S, B, TL, D, NS, L, UN = cfg
    CG = D // LANES
    NSP = S // CG
    NL = NS // NSP
    E2 = 2 * D
    CB = E2 // LANES
    GROWS = D * CB
    NQ = PIECES
    TB = TL // NQ
    SB_LAYER = 2 * NL + EXTRA
    SB_ROWS = small_rows(L, NL, B)
    SP = SB_ROWS // B
    spans = chain_rows(GROWS // 2, S * B // 2, CHAINS)
    (
        x_hbm, ct_hbm, len_hbm, gain_hbm, dec_hbm, in_hbm, out_hbm, skip_hbm, o2_hbm, step_hbm, w_hbm, bias_hbm,
        y_out, gx_out, ggain_out, gdec_out, gin_out, gout_out, gskip_out, go2_out, gstep_out, FG, gbias_out, stats_out,
        x_ref, ct_ref, len_ref, gain_ref, DEC, INM, OUTM, skip_ref, o2_ref, step_ref, W, bias_ref, NA, WT,
        XS, XR, RSTD, R, Y, YR, GS, GMR, GXR,
        SIG, P1, P2, LA, PJ, LG, GA, STR, GRD, ST,
        FB, RB, AF, AR, GF, GFR, LA2, LG2, SBW, SBR, SBG, VEC,
        load_sem, send_sem, recv_sem, ar_ssem, ar_rsem, sb_ssem, sb_rsem, sg_ssem, sg_rsem, pair_ssem, pair_rsem,
    ) = refs
    U, GX = P2, Y
    me = lax.axis_index("seq")
    bi = lax.axis_index("batch")
    cg = me // NSP
    nh = lax.rem(me, NSP)
    n0 = nh * NL
    first_part = (nh == 0).astype(F32)
    clane = pl.ds(pl.multiple_of(cg * LANES, LANES), LANES)

    sources = (x_hbm, len_hbm, gain_hbm, o2_hbm, step_hbm, dec_hbm, in_hbm, out_hbm, skip_hbm, w_hbm, bias_hbm, ct_hbm)
    targets = (x_ref, len_ref, gain_ref, o2_ref, step_ref, DEC, INM, OUTM, skip_ref, W, bias_ref, ct_ref)
    loads = [pltpu.make_async_copy(h, v, load_sem.at[i]) for i, (h, v) in enumerate(zip(sources, targets))]
    for c in loads:
        c.start()

    barrier = pltpu.get_barrier_semaphore()
    partners = [(me ^ d, bi) for d in range(1, S)]
    partners += [(me ^ 1, bi ^ (1 << b)) for b in bits_of(B)]
    for p in partners:
        pl.semaphore_signal(barrier, inc=1, device_id=p, device_id_type=MESH)

    sends = []

    def sent():
        while sends:
            sends.pop(0)()

    def seq_copy(ph, j, q, src, dst):
        return pltpu.make_async_remote_copy(
            src_ref=src,
            dst_ref=dst,
            send_sem=send_sem.at[j, q],
            recv_sem=recv_sem.at[ph % 2, me, q],
            device_id=(j, bi),
            device_id_type=MESH,
        )

    def seq_wait(ph, k, q, ref):
        pltpu.make_async_remote_copy(
            src_ref=ref,
            dst_ref=ref,
            send_sem=send_sem.at[k, q],
            recv_sem=recv_sem.at[ph % 2, k, q],
            device_id=(k, bi),
            device_id_type=MESH,
        ).wait_recv()

    def rows_of(q):
        return pl.ds(q * TB if isinstance(q, int) else pl.multiple_of(q * TB, TB), TB)

    def span(k, q):
        return pl.ds(pl.multiple_of((k * NQ + q) * TB, TB), TB)

    peers = list(range(S - 1, 0, -1))

    def tblock(k):
        return pl.ds(pl.multiple_of(k * TL, TL), TL)

    def bit_of(v, bit):
        return lax.rem(v // (1 << bit), 2)

    def swap(axis, bit):
        if axis == "batch":
            return (me ^ 1, bi ^ (1 << bit))
        return (me ^ (1 << bit) ^ 1, bi)

    def my_bit(axis, bit):
        return bit_of(me if axis == "seq" else bi, bit)

    side = lax.rem(sum(bit_of(me, i) for i in bits_of(S)) + sum(bit_of(bi, i) for i in bits_of(B)), 2)

    def pair_copy(which, l, src, dst):
        return pltpu.make_async_remote_copy(
            src_ref=src,
            dst_ref=dst,
            send_sem=pair_ssem.at[which],
            recv_sem=pair_rsem.at[which, l],
            device_id=(me ^ 1, bi),
            device_id_type=MESH,
        )

    def act_copy(l):
        return pair_copy(0, l, AF, AR.at[l])

    def grad_copy(l):
        return pair_copy(1, l, GF.at[1 - side], GFR.at[l])

    class Reduce:
        after = ()

        def __init__(self, l):
            self.l = l
            self.chains = []
            plans = orders(S, B, len(spans), l > 0)
            for (base, rows), plan in zip(spans, plans):
                off, size, roff, stages = base, rows, base, []
                for i, (axis, bit) in enumerate(plan):
                    half = size // 2
                    mine = my_bit(axis, bit)
                    keep = pl.multiple_of(off + mine * half, 8)
                    give = pl.multiple_of(off + (1 - mine) * half, 8)
                    stages.append((i, axis, bit, half, keep, give, roff))
                    off, size, roff = keep, half, roff + half
                self.chains.append(stages)
            self.n = n = len(plans[0])
            self.todo = [self.begin]
            self.todo += [functools.partial(self.reduce_step, i) for i in range(n)]
            self.todo += [functools.partial(self.gather_step, i) for i in range(n - 1, -1, -1)]
            self.todo += [self.last_step]

        def rs(self, c, stage):
            i, axis, bit, half, keep, give, roff = stage
            return pltpu.make_async_remote_copy(
                src_ref=FB.at[self.l, pl.ds(give, half)],
                dst_ref=RB.at[self.l, pl.ds(roff, half)],
                send_sem=ar_ssem.at[self.l, c],
                recv_sem=ar_rsem.at[self.l, c, i],
                device_id=swap(axis, bit),
                device_id_type=MESH,
            )

        def pair(self, c):
            base, rows = spans[c]
            here = FG.at[self.l, side, pl.ds(base, rows)]
            return pltpu.make_async_remote_copy(
                src_ref=here,
                dst_ref=here,
                send_sem=ar_ssem.at[self.l, c],
                recv_sem=ar_rsem.at[self.l, c, self.n + 1],
                device_id=(me ^ 1, bi),
                device_id_type=MESH,
            )

        def ag(self, c, stage):
            i, axis, bit, half, keep, give, roff = stage
            here = FG.at[self.l, side, pl.ds(keep, half)]
            return pltpu.make_async_remote_copy(
                src_ref=here,
                dst_ref=here,
                send_sem=ar_ssem.at[self.l, c],
                recv_sem=ar_rsem.at[self.l, c, i - 1 if i else self.n],
                device_id=swap(axis, bit),
                device_id_type=MESH,
            )

        def begin(self):
            for c, stages in enumerate(self.chains):
                self.rs(c, stages[0]).start()

        def reduce_step(self, i):
            for c, stages in enumerate(self.chains):
                _, _, _, half, keep, _, roff = stages[i]
                self.rs(c, stages[i]).wait()
                step = math.gcd(half, 64)

                def add(j, _, i=i, keep=keep, roff=roff, step=step):
                    at = pl.ds(pl.multiple_of(keep + j * step, 8), step)
                    total = FB[self.l, at, :] + RB[self.l, pl.ds(pl.multiple_of(roff + j * step, 8), step), :]
                    if i + 1 < self.n:
                        FB[self.l, at, :] = total
                    else:
                        FG[self.l, side, at, :] = total
                    return 0

                lax.fori_loop(0, half // step, add, 0)
                if i + 1 < self.n:
                    self.rs(c, stages[i + 1]).start()
                else:
                    self.ag(c, stages[i]).start()

        def gather_step(self, i):
            for c, stages in enumerate(self.chains):
                self.ag(c, stages[i]).wait()
                if i > 0:
                    self.ag(c, stages[i - 1]).start()
                else:
                    self.pair(c).start()

        def last_step(self):
            for c in range(len(self.chains)):
                self.pair(c).wait()

    def norm_forward(l, src, done=lambda q: None):
        def step(i):
            rows = pl.ds(i * CHUNK, CHUNK)
            x = src[rows, :]
            center = x - jnp.mean(x, axis=-1, keepdims=True)
            spread = jnp.mean(center * center, axis=-1, keepdims=True)
            inv = lax.rsqrt(spread + EPSILON)
            xhat = center * inv
            RSTD[l, rows, :] = jnp.broadcast_to(inv, (CHUNK, LANES))
            for g in range(CG):
                XS[l, g, rows, :] = xhat[:, g * LANES : (g + 1) * LANES]

        for q in range(NQ):
            for i in range(q * TB // CHUNK, (q + 1) * TB // CHUNK):
                step(i)
            done(q)

    def send_normed(l, q):
        for d in peers:
            j = me ^ d
            seq_copy(0, j, q, XS.at[l, j // NSP, rows_of(q)], XR.at[l, span(me, q)]).start()
        XR[l, span(me, q), :] = XS[l, cg, rows_of(q), :]

    def scan_forward(l):
        gain = gain_ref[l : l + 1, clane]
        o2 = o2_ref[l : l + 1, clane]
        stp = step_ref[l : l + 1, clane]
        skip = skip_ref[l : l + 1, clane] * first_part
        first_row = lax.broadcasted_iota(jnp.int32, (TB, LANES), 0) == 0
        SIG[l, 0] = jnp.zeros((NL, LANES), F32)

        def block(b, carry):
            sig, last = carry
            k, q = b // NQ, lax.rem(b, NQ)
            here, t0 = span(k, q), b * TB

            @pl.when(k != me)
            def _():
                seq_wait(0, k, q, XR.at[l, here])

            normed = XR[l, here, :] * gain
            prev = jnp.where(first_row, last, pltpu.roll(normed, 1, 0))
            U[here, :] = normed + o2 * normed * prev
            z = stp * normed
            R[l, here, :] = jnp.maximum(z, 0.0) + jnp.log1p(jnp.exp(-jnp.abs(z)))
            na, wt = NA[l], WT[l]

            def inner(i, sig):
                for s in range(UN):
                    t = i * UN + s
                    at = pl.ds(t0 + t, 1)
                    sig = jnp.exp2(na * R[l, at, :]) * sig + U[at, :]
                    SIG[l, t0 + t + 1] = sig
                    P1[pl.ds(pl.multiple_of(t * 8, 8), 8), :] = rows8(wt * sig)
                return sig

            sig = lax.fori_loop(0, TB // UN, inner, sig)
            for j in range(TB // 8):
                total = P1[pl.ds(j * 64, 8, stride=8), :]
                for s in range(1, 8):
                    total = total + P1[pl.ds(j * 64 + s, 8, stride=8), :]
                at = pl.ds(pl.multiple_of(t0 + j * 8, 8), 8)
                Y[at, :] = total + skip * U[at, :]

            @pl.when(k != me)
            def _():
                seq_copy(0, k, q, XS.at[l, 0, rows_of(q)], XR.at[l, here]).wait_send()
                seq_copy(1, k, q, Y.at[here], YR.at[l, me, rows_of(q)]).start()

            return sig, normed[TB - 1 : TB, :]

        lax.fori_loop(0, S * NQ, block, (jnp.zeros((NL, LANES), F32), jnp.zeros((1, LANES), F32)))
        YR[l, me] = Y[tblock(me), :]
        for q in range(NQ):
            for d in peers:
                here = span(me ^ d, q)
                sends.append(seq_copy(1, me ^ d, q, Y.at[here], YR.at[l, me, rows_of(q)]).wait_send)

    def mixed_of(l, g, rows):
        m = YR[l, g * NSP, rows, :]
        for h in range(1, NSP):
            m = m + YR[l, g * NSP + h, rows, :]
        return m

    def valid_of(i):
        pos = me * TL + i * CHUNK + lax.broadcasted_iota(jnp.int32, (CHUNK, 1), 0)
        return (pos < len_ref[0]).astype(F32)

    def glu_forward(l, src, dst):
        for q in range(NQ):
            for d in peers:
                seq_wait(1, me ^ d, q, YR.at[l, me ^ d, rows_of(q)])

        def act(i, sq):
            rows = pl.ds(pl.multiple_of(i * CHUNK, CHUNK), CHUNK)
            valid = valid_of(i)
            for g in range(CG):
                m = mixed_of(l, g, rows)
                a = 0.5 * m * (1.0 + gelu_parts(m))
                low = a.astype(BF16)
                LA[l, rows, g * LANES : (g + 1) * LANES] = low
                AF[rows, g * LANES : (g + 1) * LANES] = low.astype(F32)
                sq = sq + rows8(a * a * valid)
            return sq

        zero = jnp.zeros((8, LANES), F32)
        if l:
            act_copy(l - 1).wait_send()
        sq_act = lax.fori_loop(0, TL // CHUNK, act, zero)
        act_copy(l).start()
        PJ[l] = jnp.dot(LA[l], W[l], preferred_element_type=F32) + bias_ref[l : l + 1, :]

        def gate(i, sq):
            sq_b, sq_s, cnt = sq
            rows = pl.ds(pl.multiple_of(i * CHUNK, CHUNK), CHUNK)
            valid = valid_of(i)
            for g in range(CG):
                cols = slice(g * LANES, (g + 1) * LANES)
                gcols = slice(D + g * LANES, D + (g + 1) * LANES)
                branch = PJ[l, rows, cols] * sigmoid(PJ[l, rows, gcols]) * valid
                out = src[rows, cols] + branch
                dst[rows, cols] = out
                sq_b = sq_b + rows8(branch * branch)
                sq_s = sq_s + rows8(out * out * valid)
            cnt = cnt + rows8(jnp.broadcast_to(valid, (CHUNK, LANES)))
            return sq_b, sq_s, cnt

        sq_b, sq_s, cnt = lax.fori_loop(0, TL // CHUNK, gate, (zero, zero, zero))
        for k, v in enumerate((sq_act, sq_b, sq_s, cnt)):
            ST[l, k] = v

    def gate_backward(l, gsrc):
        def gate(i, acc):
            rows = pl.ds(pl.multiple_of(i * CHUNK, CHUNK), CHUNK)
            valid = valid_of(i)
            out = []
            for g in range(CG):
                cols = slice(g * LANES, (g + 1) * LANES)
                gcols = slice(D + g * LANES, D + (g + 1) * LANES)
                gb = gsrc[rows, cols] * valid
                s = sigmoid(PJ[l, rows, gcols])
                one = gb * s
                two = one * PJ[l, rows, cols] * (1.0 - s)
                low_one, low_two = one.astype(BF16), two.astype(BF16)
                LG[rows, cols] = low_one
                LG[rows, gcols] = low_two
                GF[0, rows, cols] = low_one.astype(F32)
                GF[1, rows, cols] = low_two.astype(F32)
                out.append((rows8(one), rows8(two)))
            return tuple(a + b for a, b in zip(acc, [o[0] for o in out] + [o[1] for o in out]))

        zero = jnp.zeros((8, LANES), F32)
        if l < L - 1:
            grad_copy(l + 1).wait_send()
        bias = lax.fori_loop(0, TL // CHUNK, gate, (zero,) * CB)
        grad_copy(l).start()
        return bias

    def act_backward(l, bias):
        GA[...] = lax.dot_general(LG[...], W[l], (((1,), (1,)), ((), ())), preferred_element_type=F32)

        def act(i):
            rows = pl.ds(i * CHUNK, CHUNK)
            for g in range(CG):
                m = mixed_of(l, g, rows)
                th = gelu_parts(m)
                slope = 0.5 * (1.0 + th) + 0.5 * m * (1.0 - th * th) * GELU_K * (1.0 + 3 * 0.044715 * m * m)
                GS[l, g, rows, :] = GA[rows, g * LANES : (g + 1) * LANES] * slope

        for q in range(NQ - 1, -1, -1):
            for i in range(q * TB // CHUNK, (q + 1) * TB // CHUNK):
                act(i)
            for d in peers:
                j = me ^ d
                seq_copy(2, j, q, GS.at[l, j // NSP, rows_of(q)], GMR.at[l, me, rows_of(q)]).start()
        GMR[l, me] = GS[l, cg]
        extra = list(bias) + [ST[l, k] for k in range(4)]
        extra = jnp.concatenate([jnp.sum(v, axis=0, keepdims=True) for v in extra], axis=0)
        base = l * SB_LAYER + 2 * NL + 4
        SBW[base : base + len(bias) + 4, :] = extra

    def weight_grad(l):
        if l == L - 1:
            act_copy(l).wait_send()
        act_copy(l).wait_recv()
        grad_copy(l).wait_recv()

        def cast(i, _):
            rows = pl.ds(pl.multiple_of(i * CHUNK, CHUNK), CHUNK)
            also = pl.ds(pl.multiple_of(TL + i * CHUNK, CHUNK), CHUNK)
            LA2[rows, :] = LA[l, rows, :]
            LA2[also, :] = AR[l, rows, :].astype(BF16)
            LG2[rows, :] = GF[side, rows, :].astype(BF16)
            LG2[also, :] = GFR[l, rows, :].astype(BF16)
            return 0

        lax.fori_loop(0, TL // CHUNK, cast, 0)
        half = lax.dot_general(LA2[...], LG2[...], (((0,), (0,)), ((), ())), preferred_element_type=F32)
        for q in range(CB // 2):
            FB[l, pl.ds(q * D, D), :] = half[:, q * LANES : (q + 1) * LANES]

    def scan_backward(l, steps):
        gain = gain_ref[l : l + 1, clane]
        o2 = o2_ref[l : l + 1, clane]
        stp = step_ref[l : l + 1, clane]
        skip = skip_ref[l : l + 1, clane]
        row_id = lax.broadcasted_iota(jnp.int32, (TB, LANES), 0)
        zero8 = jnp.zeros((8, LANES), F32)
        zeros = jnp.zeros((NL, LANES), F32)
        for v in range(4):
            VEC[v] = zero8

        def block(bb, carry):
            nu, acc, gdc, after = carry
            b = S * NQ - 1 - bb
            k, q = b // NQ, lax.rem(b, NQ)
            here, t0 = span(k, q), b * TB

            @pl.when(k != me)
            def _():
                seq_wait(2, k, q, GMR.at[l, k, rows_of(q)])

            na, wt = NA[l], WT[l]

            def inner(ii, c):
                nu, acc, gdc = c
                i = TB // UN - 1 - ii
                for s in range(UN - 1, -1, -1):
                    t = i * UN + s
                    logs = na * R[l, pl.ds(t0 + t, 1), :]
                    gm = GMR[l, k, pl.ds(q * TB + t, 1), :]
                    mu = wt * gm + nu
                    if l == 0:
                        acc = acc + gm * SIG[l, t0 + t + 1]
                    at = pl.ds(pl.multiple_of(t * 8, 8), 8)
                    P1[at, :] = rows8(mu)
                    nu = jnp.exp2(logs) * mu
                    part = nu * SIG[l, t0 + t] * logs
                    gdc = gdc + part
                    P2[at, :] = rows8(part)
                return nu, acc, gdc

            nu, acc, gdc = lax.fori_loop(0, TB // UN, inner, (nu, acc, gdc))
            for j in range(TB // 8):
                one = P1[pl.ds(j * 64, 8, stride=8), :]
                two = P2[pl.ds(j * 64, 8, stride=8), :]
                for s in range(1, 8):
                    one = one + P1[pl.ds(j * 64 + s, 8, stride=8), :]
                    two = two + P2[pl.ds(j * 64 + s, 8, stride=8), :]
                GX[pl.ds(pl.multiple_of(t0 + j * 8, 8), 8), :] = one
                GA[j * 8 : j * 8 + 8, 0:LANES] = two
            xhat = XR[l, here, :]
            normed = xhat * gain
            before = XR[l, pl.ds(jnp.maximum(t0 - 1, 0), 1), :] * gain
            before = jnp.where(b == 0, 0.0, before)
            prev = jnp.where(row_id == 0, before, pltpu.roll(normed, 1, 0))
            gm = GMR[l, k, rows_of(q), :] * first_part
            gdrv = GX[here, :] + skip * gm
            both = gdrv * normed
            h = o2 * both
            later = jnp.where(row_id == TB - 1, after, pltpu.roll(h, TB - 1, 0))
            rate = R[l, here, :]
            some = rate > 1e-30
            ratio = jnp.where(some, sigmoid(stp * normed) / jnp.where(some, rate, 1.0), 1.0)
            slope = GA[0:TB, 0:LANES] * LN2 * ratio
            gnormed = gdrv * (1.0 + o2 * prev) + later + slope * stp
            GX[here, :] = gnormed * gain
            VEC[0] = VEC[0] + rows8(gm * (normed + o2 * normed * prev))
            VEC[1] = VEC[1] + rows8(both * prev)
            VEC[2] = VEC[2] + rows8(slope * normed)
            VEC[3] = VEC[3] + rows8(gnormed * xhat)

            @pl.when(k != me)
            def _():
                seq_copy(2, k, q, GS.at[l, 0, rows_of(q)], GMR.at[l, me, rows_of(q)]).wait_send()
                seq_copy(3, k, q, GX.at[here], GXR.at[l, me, rows_of(q)]).start()

            if steps:
                hit = functools.reduce(jnp.logical_or, [bb == place for place in sorted(steps)])

                @pl.when(hit)
                def _():
                    for place in sorted(steps):

                        @pl.when(bb == place)
                        def _(todo=steps[place]):
                            for step in todo:
                                step()

            return nu, acc, gdc, h[0:1, :]

        carry = (zeros, zeros, zeros, jnp.zeros((1, LANES), F32))
        _, acc, gdc, _ = lax.fori_loop(0, S * NQ, block, carry)
        GXR[l, me] = GX[tblock(me), :]
        for q in range(NQ):
            for d in peers:
                here = span(me ^ d, q)
                sends.append(seq_copy(3, me ^ d, q, GX.at[here], GXR.at[l, me, rows_of(q)]).wait_send)
        gdc = gdc / NA[l]
        base = l * SB_LAYER
        SBW[base + NL : base + 2 * NL, :] = gdc
        if l == 0:
            SBW[base : base + NL, :] = acc
        vec = [jnp.sum(VEC[v], axis=0, keepdims=True) for v in range(4)]
        SBW[base + 2 * NL : base + 2 * NL + 4, :] = jnp.concatenate(vec, axis=0)

    def late_sum(l):
        def step(i, acc):
            for s in range(8):
                t = i * 8 + s
                acc = acc + GMR[l, i // (TL // 8), pl.ds(lax.rem(i, TL // 8) * 8 + s, 1), :] * SIG[l, t + 1]
            return acc

        SBW[l * SB_LAYER : l * SB_LAYER + NL, :] = lax.fori_loop(0, S * TL // 8, step, jnp.zeros((NL, LANES), F32))

    class Small:
        def __init__(self, first):
            self.after = [(first, first.n + 1)]
            self.todo = [self.begin, self.join, self.across]
            self.todo += [functools.partial(self.along, i) for i in range(len(bits_of(S)))]

        def part(self, j):
            return pl.ds(pl.multiple_of(j * SP, 8), SP)

        def rs(self, j, slot):
            return pltpu.make_async_remote_copy(
                src_ref=SBW.at[self.part(j)],
                dst_ref=SBR.at[slot],
                send_sem=sb_ssem.at[j],
                recv_sem=sb_rsem.at[0, slot],
                device_id=(me, j),
                device_id_type=MESH,
            )

        def ag(self, j, slot):
            rows = self.part(slot)
            return pltpu.make_async_remote_copy(
                src_ref=SBG.at[me, rows],
                dst_ref=SBG.at[me, rows],
                send_sem=sb_ssem.at[j],
                recv_sem=sb_rsem.at[1, slot],
                device_id=(me, j),
                device_id_type=MESH,
            )

        def seq(self, i, slot):
            return pltpu.make_async_remote_copy(
                src_ref=SBG.at[slot],
                dst_ref=SBG.at[slot],
                send_sem=sg_ssem.at[slot],
                recv_sem=sg_rsem.at[slot],
                device_id=(me ^ (S >> (i + 1)), bi),
                device_id_type=MESH,
            )

        def begin(self):
            if SB_ROWS > L * SB_LAYER:
                SBW[L * SB_LAYER :, :] = jnp.zeros((SB_ROWS - L * SB_LAYER, LANES), F32)
            for d in range(B - 1, 0, -1):
                self.rs(bi ^ d, bi).start()
            SBR[bi] = SBW[self.part(bi), :]

        def join(self):
            for d in range(B - 1, 0, -1):
                self.rs(bi ^ d, bi ^ d).wait()
            total = SBR[0]
            for j in range(1, B):
                total = total + SBR[j]
            SBG[me, self.part(bi), :] = total
            for d in range(B - 1, 0, -1):
                self.ag(bi ^ d, bi).start()

        def across(self):
            for d in range(B - 1, 0, -1):
                self.ag(bi ^ d, bi ^ d).wait()
            self.seq(0, me).start()

        def slots(self, i):
            held = [me]
            for k in range(i):
                held = held + [slot ^ (S >> (k + 1)) for slot in held]
            return held

        def along(self, i):
            step = S >> (i + 1)
            for slot in self.slots(i):
                self.seq(i, slot).wait_send()
                self.seq(i, slot ^ step).wait_recv()
            if i + 1 < len(bits_of(S)):
                for slot in self.slots(i + 1):
                    self.seq(i + 1, slot).start()
            else:
                for l in range(L):
                    self.gathered(l)

        def gathered(self, l):
            base = l * SB_LAYER
            for g in range(CG):
                cols = slice(g * LANES, (g + 1) * LANES)
                vec = None
                for h in range(NSP):
                    slot = g * NSP + h
                    rows = slice(h * NL, (h + 1) * NL)
                    acc = SBG[slot, base : base + NL, :]
                    gin_out[l, rows, cols] = OUTM[l, rows, cols] * acc
                    gout_out[l, rows, cols] = INM[l, rows, cols] * acc
                    gdec_out[l, rows, cols] = -SBG[slot, base + NL : base + 2 * NL, :]
                    part = SBG[slot, base + 2 * NL : base + 2 * NL + 4, :]
                    vec = part if vec is None else vec + part
                gskip_out[l : l + 1, cols] = vec[0:1]
                go2_out[l : l + 1, cols] = vec[1:2]
                gstep_out[l : l + 1, cols] = vec[2:3]
                ggain_out[l : l + 1, cols] = vec[3:4]
            base += 2 * NL + 4
            extra = SBG[0, base : base + CB + 4, :]
            for k in range(1, S):
                extra = extra + SBG[k, base : base + CB + 4, :]
            for q in range(CB):
                gbias_out[l : l + 1, q * LANES : (q + 1) * LANES] = extra[q : q + 1]
            sq = jnp.sum(extra[CB:], axis=1, keepdims=True)
            count = sq[3:4] * (1.0 / LANES)
            root = jnp.sqrt(sq[0:3] / (count * D))
            col = lax.broadcasted_iota(jnp.int32, (1, 3), 1)
            stats_out[l : l + 1, :] = jnp.where(col == 0, root[0:1], jnp.where(col == 1, root[1:2], root[2:3]))

    def norm_backward(l, gsrc, gdst):
        for q in range(NQ):
            for d in peers:
                seq_wait(3, me ^ d, q, GXR.at[l, me ^ d, rows_of(q)])

        def step(i, _):
            rows = pl.ds(pl.multiple_of(i * CHUNK, CHUNK), CHUNK)
            inv = RSTD[l, rows, :]
            gx, xh = [], []
            s1 = s2 = None
            for g in range(CG):
                v = GXR[l, g * NSP, rows, :]
                for h in range(1, NSP):
                    v = v + GXR[l, g * NSP + h, rows, :]
                x = XS[l, g, rows, :]
                gx.append(v)
                xh.append(x)
                s1 = v if s1 is None else s1 + v
                s2 = v * x if s2 is None else s2 + v * x
            m1 = jnp.sum(s1, axis=-1, keepdims=True) * (1.0 / D)
            m2 = jnp.sum(s2, axis=-1, keepdims=True) * (1.0 / D)
            for g in range(CG):
                cols = slice(g * LANES, (g + 1) * LANES)
                gdst[rows, cols] = gsrc[rows, cols] + inv * (gx[g] - m1 - xh[g] * m2)
            return 0

        lax.fori_loop(0, TL // CHUNK, step, 0)

    loads[0].wait()
    norm_forward(0, x_ref)
    pl.semaphore_wait(barrier, len(partners))
    for q in range(NQ):
        send_normed(0, q)
    for c in loads[1:]:
        c.wait()
    nrows = pl.ds(pl.multiple_of(n0, 8), NL)
    for l in range(L):
        NA[l] = DEC[l, nrows, clane] * (-LOG2E)
        WT[l] = INM[l, nrows, clane] * OUTM[l, nrows, clane]
    streams = [x_ref] + [STR.at[l] for l in range(L - 1)] + [y_out]
    for l in range(L):
        if l:
            norm_forward(l, streams[l], functools.partial(send_normed, l))
        scan_forward(l)
        glu_forward(l, streams[l], streams[l + 1])
        sent()

    grads = [gx_out] + [GRD.at[l] for l in range(L - 1)] + [ct_ref]
    def take(things):
        steps = []
        for t in things:
            if t.todo and all(len(a.todo) <= left for a, left in t.after):
                steps.append(t.todo.pop(0))
        return steps

    def run(*things):
        for step in take(things):
            step()

    def places(plan):
        return {(i + 1) * S * NQ // 16 - 1: take(plan[i]) for i in sorted(plan)}

    bigs = []
    for l in range(L - 1, -1, -1):
        bias = gate_backward(l, grads[l + 1])
        act_backward(l, bias)
        weight_grad(l)
        above = list(bigs)
        bigs.insert(0, Reduce(l))
        run(bigs[0])
        if above:
            late_sum(l + 1)
            scan_backward(l, places({5: above, 12: above, 13: bigs[:1]}))
        else:
            scan_backward(l, places({11: bigs}))
        if l == 0:
            small = Small(bigs[-1])
            run(small)
        norm_backward(l, grads[l + 1], grads[l])
        sent()
        run(*bigs)
    grad_copy(0).wait_send()
    while any(t.todo for t in bigs + [small]):
        run(bigs[0], small, *bigs[1:])


def hand_on(*refs):
    n = (len(refs) - 2) // 2
    sem, block_sem = refs[-2], refs[-1]
    copies = []
    for i, (a, o) in enumerate(zip(refs[:n], refs[n : 2 * n])):
        if a.shape == o.shape:
            copies.append(pltpu.make_async_copy(a, o, sem.at[i]))
            continue
        layers, rows, columns = o.shape
        for l in range(layers):
            for c in range(columns // LANES):
                block = o.at[l, :, pl.ds(c * LANES, LANES)]
                side, at = divmod(c * rows, a.shape[2])
                copies.append(pltpu.make_async_copy(a.at[l, side, pl.ds(at, rows)], block, block_sem.at[l, c]))
    for c in copies:
        c.start()
    for c in copies:
        c.wait()


def per_device(
    stream_in, cotangent, lengths, norm_gain, decay_rate, in_map, out_map, skip_gain, order_two, step_gain, glu_weight, glu_bias
):
    S, B = lax.axis_size("seq"), lax.axis_size("batch")
    _, TL, D = stream_in.shape
    L, NS = decay_rate.shape[:2]
    UN = math.gcd(TL // PIECES, 32)
    CG, E2 = D // LANES, 2 * D
    NL = NS // (S // CG)
    TA = S * TL
    CB = E2 // LANES
    GROWS = D * CB
    SBR = small_rows(L, NL, B)
    NB, NST = len(bits_of(B)), len(bits_of(B)) + len(bits_of(S))
    shape = jax.ShapeDtypeStruct
    vmem = pl.BlockSpec(memory_space=pltpu.VMEM)
    hbm = pl.BlockSpec(memory_space=pl.ANY)
    buf = pltpu.VMEM
    dma = pltpu.SemaphoreType.DMA
    outs = pl.pallas_call(
        functools.partial(kernel, (S, B, TL, D, NS, L, UN)),
        out_shape=[
            buf((TL, D), F32), buf((TL, D), F32), buf((L, D), F32),
            buf((L, NS, D), F32), buf((L, NS, D), F32), buf((L, NS, D), F32),
            buf((L, D), F32), buf((L, D), F32), buf((L, D), F32),
            buf((L, 2, GROWS // 2, LANES), F32), buf((L, E2), F32), buf((L, 3), F32),
        ],
        in_specs=[hbm] * 12,
        out_specs=[vmem] * 12,
        scratch_shapes=[
            buf((TL, D), F32), buf((TL, D), F32), pltpu.SMEM((1,), jnp.int32), buf((L, D), F32),
            buf((L, NS, D), F32), buf((L, NS, D), F32), buf((L, NS, D), F32),
            buf((L, D), F32), buf((L, D), F32), buf((L, D), F32), buf((L, D, E2), BF16), buf((L, E2), F32),
            buf((L, NL, LANES), F32), buf((L, NL, LANES), F32),
            buf((L, CG, TL, LANES), F32), buf((L, TA, LANES), F32), buf((L, TL, LANES), F32),
            buf((L, TA, LANES), F32), buf((TA, LANES), F32),
            buf((L, S, TL, LANES), F32), buf((L, CG, TL, LANES), F32), buf((L, S, TL, LANES), F32),
            buf((L, S, TL, LANES), F32),
            buf((L, TA + 1, NL, LANES), F32), buf((TL * 8, LANES), F32), buf((max(TL * 8, TA), LANES), F32),
            buf((L, TL, D), BF16), buf((L, TL, E2), F32), buf((TL, E2), BF16), buf((TL, D), F32),
            buf((L - 1, TL, D), F32), buf((L - 1, TL, D), F32), buf((L, 4, 8, LANES), F32),
            buf((L, GROWS // 2, LANES), F32), buf((L, GROWS // 2, LANES), F32),
            buf((TL, D), F32), buf((L, TL, D), F32), buf((2, TL, D), F32), buf((L, TL, D), F32), buf((2 * TL, D), BF16), buf((2 * TL, D), BF16),
            buf((SBR, LANES), F32), buf((B, SBR // B, LANES), F32), buf((S, SBR, LANES), F32),
            buf((4, 8, LANES), F32),
            dma((12,)), dma((S, PIECES)), dma((2, S, PIECES)), dma((L, CHAINS)), dma((L, CHAINS, NST + 1)),
            dma((B,)), dma((2, B)), dma((S,)), dma((S,)), dma((2,)), dma((2, L)),
        ],
        compiler_params=pltpu.CompilerParams(
            collective_id=0, has_side_effects=True, vmem_limit_bytes=57 * 2**20
        ),
        name="liquid_layers",
    )(
        stream_in[0], cotangent[0], lengths, norm_gain, decay_rate, in_map, out_map,
        skip_gain, order_two, step_gain, glu_weight, glu_bias,
    )
    outs = pl.pallas_call(
        hand_on,
        out_shape=[shape((L, D, E2), F32) if o.ndim == 4 else shape(o.shape, F32) for o in outs],
        in_specs=[vmem] * len(outs),
        out_specs=[hbm] * len(outs),
        scratch_shapes=[dma((len(outs),)), dma((L, CB))],
        compiler_params=pltpu.CompilerParams(vmem_limit_bytes=2**20),
        name="results",
    )(*outs)
    return (outs[0][None], outs[1][None], *outs[2:])


def solution(mesh):
    split = P("batch", "seq", None)
    in_specs = (split, split, P("batch")) + (P(),) * 9
    out_specs = (split, split) + (P(),) * 10
    return jax.shard_map(per_device, mesh=mesh, in_specs=in_specs, out_specs=out_specs, check_vma=False)
```
